32 devices in a mesh: pipe: 2 (over x), dp: 16 (over z, y, core).
Axes of the slice: x: 2, y: 2, z: 4, core: 2. Of those that a mesh axis runs over, the one named last changes fastest.
Arguments:
- activations: bfloat16 [32, 512, 768], P('dp'), may hold values from -6 to 6
- out_cotangent: bfloat16 [32, 512, 768], P('dp'), may hold values from -6 to 6
- doc_lengths: int32 [32, 5], P('dp'), may hold values from 1 to 256, 512 in all within a row
- mix_gain: float32 [2, 768], P('pipe'), may hold values from 0.25 to 1.75
- mix_bias: float32 [2, 768], P('pipe'), may hold values from -3 to 3
- weight_in: bfloat16 [2, 768, 3072], P('pipe'), may hold values from -0.21875 to 0.21875
- bias_in: float32 [2, 3072], P('pipe'), may hold values from -3 to 3
- weight_out: bfloat16 [2, 3072, 768], P('pipe'), may hold values from -0.109375 to 0.109375
- bias_out: float32 [2, 768], P('pipe'), may hold values from -3 to 3
- final_gain: float32 [2, 768], P('pipe'), may hold values from 0.25 to 1.75
- final_bias: float32 [2, 768], P('pipe'), may hold values from -3 to 3
Outputs:
- layer_outputs: bfloat16 [2, 32, 512, 768], P('pipe', 'dp')
- input_grads: float32 [2, 32, 512, 768], P('pipe', 'dp')
- mix_gain_grad: float32 [2, 768], P('pipe')
- mix_bias_grad: float32 [2, 768], P('pipe')
- weight_in_grad: float32 [2, 768, 3072], P('pipe')
- bias_in_grad: float32 [2, 3072], P('pipe')
- weight_out_grad: float32 [2, 3072, 768], P('pipe')
- bias_out_grad: float32 [2, 768], P('pipe')
- final_gain_grad: float32 [2, 768], P('pipe')
- final_bias_grad: float32 [2, 768], P('pipe')
The draws below stay inside these ranges and needn't reach their ends.
Inputs may be any that keep to these rules, and one draw needn't show every extreme that they name: `doc_lengths`: in each row the 4 document lengths and, last, the padding's length add up to 512; every row's largest entry is 256.
All inputs are finite; a program needn't handle non-finite values.
Results may differ from the reference program's by a relative error of at most 0.013.
Values may be sent and summed in bfloat16 or wider, within the bound.
No kernel may reach another device: no remote copies, remote signals or barrier semaphores. Data moves between devices by JAX's collectives and lax.ppermute only.
A program may use at most 192 MiB of HBM per device.

```python
import math
import jax
import jax.numpy as jnp
import numpy as np
from jax import lax

D = 768
FF = 3072
SEQ = 512
DOCS = 4
MOSTLEN = 256
ROWS = 32
N_PIPE = 2


def levels(stream_key, extent, split, least, top_value):
    def one(dim, blocks):
        steps = jax.random.uniform(jax.random.fold_in(jax.random.fold_in(stream_key, 6), dim), (blocks,), jnp.float32, least / len(split), top_value / len(split))
        return jnp.repeat(jnp.exp(steps), extent[dim] // blocks).reshape((-1,) + (1,) * (len(extent) - dim - 1))

    factor_of = one(*split[0])
    for cut in split[1:]:
        factor_of = factor_of * one(*cut)
    return factor_of


def length_profile(count, total, reach, slope):
    portions = [(1 << 20) // math.isqrt(grade ** slope) + 1 for grade in range(2, count + 1)]
    surplus, holding = total - reach - (count - 1), [1] * (count - 1)
    while surplus > 0:
        movable = [i for i in range(count - 1) if holding[i] < reach]
        pool, left = sum([portions[i] for i in movable]), surplus
        for i in movable:
            extra = min(reach - holding[i], max(1, left * portions[i] // pool), surplus)
            holding[i] = holding[i] + extra
            surplus = surplus - extra
    return np.array([reach] + holding)


def uneven_parts(rng, amount, total, most, slope):
    if amount == 2:
        one = jax.random.randint(rng, (), max(1, total - most), min(most, total - 1) + 1)
        return jnp.stack([one, total - one])
    lengths = jnp.asarray(length_profile(amount, total, most, slope), jnp.int32)
    twos = (amount - 1) // 2
    source_of, taker = lengths[1:1 + 2 * twos:2], lengths[2:2 + 2 * twos:2]
    margin = jnp.minimum(source_of - 1, most - taker)
    passed = jax.random.randint(jax.random.fold_in(rng, 1), (twos,), 0, 1 << 20) % (margin + 1)
    lengths = lengths.at[1:1 + 2 * twos:2].set(source_of - passed).at[2:2 + 2 * twos:2].set(taker + passed)
    return lengths[jax.random.permutation(jax.random.fold_in(rng, 2), amount)]


def bell_draw(rng, extent, scale, reach, shards=(), kind=jnp.bfloat16):
    values = jax.random.normal(rng, extent, jnp.float32) * scale
    if len(shards) > 0:
        values = levels(rng, extent, shards, -0.22, 0.18) * values
    return jnp.clip(values, min=-reach, max=reach).astype(kind)


def setup_inputs(seed: int = 0) -> dict:
    streams_of = jax.random.split(jax.random.key(seed), 12)
    return {
        "activations": bell_draw(streams_of[0], (ROWS, SEQ, D), 1.0, 6.0, ((0, 16),)),
        "out_cotangent": bell_draw(streams_of[1], (ROWS, SEQ, D), 1.0, 6.0, ((0, 16),)),
        "doc_lengths": jax.vmap(lambda own: uneven_parts(own, DOCS + 1, SEQ, MOSTLEN, 1))(jax.random.split(streams_of[2], ROWS)).reshape((ROWS, DOCS + 1)).astype(jnp.int32),
        "mix_gain": jnp.clip(1.0 + 0.15 * jax.random.normal(streams_of[3], (N_PIPE, D), jnp.float32), 0.25, 1.75),
        "mix_bias": bell_draw(streams_of[4], (N_PIPE, D), 0.3, 3.0, ((0, 2),), jnp.float32),
        "weight_in": bell_draw(streams_of[5], (N_PIPE, D, FF), D ** -0.5, 0.21875, ((0, 2),)),
        "bias_in": bell_draw(streams_of[6], (N_PIPE, FF), 0.5, 3.0, ((0, 2),), jnp.float32),
        "weight_out": bell_draw(streams_of[7], (N_PIPE, FF, D), FF ** -0.5, 0.109375, ((0, 2),)),
        "bias_out": bell_draw(streams_of[8], (N_PIPE, D), 0.3, 3.0, ((0, 2),), jnp.float32),
        "final_gain": jnp.clip(1.0 + 0.15 * jax.random.normal(streams_of[9], (N_PIPE, D), jnp.float32), 0.25, 1.75),
        "final_bias": bell_draw(streams_of[10], (N_PIPE, D), 0.3, 3.0, ((0, 2),), jnp.float32),
    }


HIGH = lax.Precision.HIGHEST
eps_norm = 1e-06

@jax.custom_vjp
def low(v):
    return lax.optimization_barrier(v.astype(jnp.bfloat16)).astype(jnp.float32)

@jax.custom_vjp
def low_back(v):
    return v

def low_keep(v):
    return (low(v), None)

def low_pass(kept, grad):
    return (grad,)

def back_keep(v):
    return (v, None)

def back_low(kept, grad):
    return (low(grad),)
low.defvjp(low_keep, low_pass)
low_back.defvjp(back_keep, back_low)

def dft_tables(table_len):
    indices = jnp.arange(table_len, dtype=jnp.int32)
    product = indices[:, None] * indices[None, :] % table_len
    angles = product.astype(jnp.float32) * (2.0 * math.pi / table_len)
    scaled = 1.0 / math.sqrt(table_len)
    return (jnp.cos(angles) * scaled, jnp.sin(angles) * scaled)

def layer_norm(values, gain_vec, bias_vec):
    average = lax.optimization_barrier(jnp.mean(values, axis=-1, keepdims=True))
    centred = values - average
    spread = lax.optimization_barrier(jnp.mean(centred * centred, axis=-1, keepdims=True))
    return centred * lax.rsqrt(spread + eps_norm) * gain_vec + bias_vec

def one_layer(layer_in, params, mixers):
    hidden_mix, seq_mix = mixers
    mix_gain, mix_bias, weight_in, bias_in, weight_out, bias_out, final_gain, final_bias = params
    row_count, seq_len, model_width = layer_in.shape
    spectra = low_back(low(jnp.einsum('rld,kde->rkle', layer_in, hidden_mix, precision=HIGH)))
    stacked_spec = spectra.reshape(row_count, 2 * seq_len, model_width)
    mixed_seq = low_back(jnp.einsum('ml,rld->rmd', seq_mix, stacked_spec, precision=HIGH))
    hidden = layer_norm(layer_in + mixed_seq, mix_gain, mix_bias)
    inner_act = low_back(jnp.einsum('rld,df->rlf', low(hidden), weight_in, precision=HIGH) + bias_in)
    active = low(jax.nn.gelu(inner_act, approximate=True))
    branch = low_back(jnp.einsum('rlf,fd->rld', active, weight_out, precision=HIGH) + bias_out)
    return layer_norm(hidden + branch, final_gain, final_bias)

def reference(activations, out_cotangent, doc_lengths, mix_gain, mix_bias, weight_in, bias_in, weight_out, bias_out, final_gain, final_bias):
    padding = doc_lengths[:, -1]
    positions = jnp.arange(SEQ, dtype=jnp.int32)
    token_mask = (positions[None, :] < (SEQ - padding)[:, None]).astype(jnp.float32)
    cotangent = out_cotangent.astype(jnp.float32) * token_mask[:, :, None]
    stacks = [stacked.astype(jnp.float32) for stacked in (mix_gain, mix_bias, weight_in, bias_in, weight_out, bias_out, final_gain, final_bias)]
    first_params = tuple((stacked[0] for stacked in stacks))
    second_params = tuple((stacked[1] for stacked in stacks))
    cos_hid, sin_hid = dft_tables(D)
    cos_seq, sin_seq = dft_tables(SEQ)
    mixers = (low(jnp.stack([cos_hid, sin_hid])), low(jnp.concatenate([cos_seq, -sin_seq], axis=1)))

    def two_layers(layer_in, injected, params_one, params_two):
        first_out = one_layer(layer_in, params_one, mixers)
        second_in = low_back(low(first_out) + injected)
        second_out = one_layer(second_in, params_two, mixers)
        return (first_out, second_out)
    block_rows = 8
    block_count = ROWS // block_rows

    def one_block(totals, block_pair):
        block_in, block_cot = block_pair
        injected = jnp.zeros_like(block_in)
        outputs, pull_back = jax.vjp(two_layers, block_in, injected, first_params, second_params)
        grad_first_in, grad_second_in, grads_one, grads_two = pull_back((jnp.zeros_like(block_in), block_cot))
        totals = jax.tree.map(jnp.add, totals, (grads_one, grads_two))
        return (totals, (outputs[0].astype(jnp.bfloat16), outputs[1].astype(jnp.bfloat16), grad_first_in, grad_second_in))
    zero_totals = jax.tree.map(jnp.zeros_like, (first_params, second_params))
    block_inputs = activations.astype(jnp.float32).reshape(block_count, block_rows, SEQ, D)
    block_cots = cotangent.reshape(block_count, block_rows, SEQ, D)
    totals, stacked_out = lax.scan(one_block, zero_totals, (block_inputs, block_cots))
    first_out, second_out, first_grad, second_grad = stacked_out
    layer_outputs = jnp.stack([first_out.reshape(ROWS, SEQ, D), second_out.reshape(ROWS, SEQ, D)])
    input_grads = jnp.stack([first_grad.reshape(ROWS, SEQ, D), second_grad.reshape(ROWS, SEQ, D)])
    grad_pairs = [jnp.stack([first_term, second_term]) for first_term, second_term in zip(totals[0], totals[1])]
    return (layer_outputs, input_grads, grad_pairs[0], grad_pairs[1], grad_pairs[2], grad_pairs[3], grad_pairs[4], grad_pairs[5], grad_pairs[6], grad_pairs[7])
```

```python
import functools
import math

import jax
import jax.numpy as jnp
import numpy as np
from jax import lax
from jax.sharding import PartitionSpec as P


eps_norm = 1e-06


def from_behind(block, axis, distance):
    devices = range(lax.axis_size(axis))
    route = [(i - distance, i) for i in devices if i - distance in devices]
    return lax.ppermute(block, axis, route)


def dft_tables(table_len):
    indices = np.arange(table_len)
    angles = (indices[:, None] * indices[None, :] % table_len) * (2.0 * math.pi / table_len)
    scaled = 1.0 / math.sqrt(table_len)
    return (np.cos(angles) * scaled, np.sin(angles) * scaled)


def normalize(values):
    average = jnp.mean(values, axis=-1, keepdims=True)
    centred = values - average
    inverse = lax.rsqrt(jnp.mean(centred * centred, axis=-1, keepdims=True) + eps_norm)
    return (centred * inverse, inverse)


def norm_back(grad_norm, normed, inverse):
    first_term = jnp.mean(grad_norm, axis=-1, keepdims=True)
    second_term = jnp.mean(grad_norm * normed, axis=-1, keepdims=True)
    return inverse * (grad_norm - first_term - normed * second_term)


def gelu_tanh(values):
    return jax.nn.gelu(values, approximate=True)


def forward_parts(layer_in, params, mixers):
    hidden_mix, seq_mix = mixers
    mix_gain, mix_bias, weight_in, bias_in, weight_out, bias_out, final_gain, final_bias = params
    row_count, seq_len, model_width = layer_in.shape
    spectra = jnp.einsum(
        "rld,kde->rkle", layer_in, hidden_mix, preferred_element_type=jnp.float32
    ).astype(jnp.bfloat16)
    stacked_spec = spectra.reshape(row_count, 2 * seq_len, model_width)
    mixed_seq = jnp.einsum("ml,rld->rmd", seq_mix, stacked_spec, preferred_element_type=jnp.float32)
    normed_one, inverse_one = normalize(layer_in.astype(jnp.float32) + mixed_seq)
    hidden = normed_one * mix_gain + mix_bias
    hidden_low = hidden.astype(jnp.bfloat16)
    inner_act = (
        jnp.einsum("rld,df->rlf", hidden_low, weight_in, preferred_element_type=jnp.float32)
        + bias_in
    )
    active = gelu_tanh(inner_act).astype(jnp.bfloat16)
    branch = (
        jnp.einsum("rlf,fd->rld", active, weight_out, preferred_element_type=jnp.float32) + bias_out
    )
    normed_two, inverse_two = normalize(hidden + branch)
    result = normed_two * final_gain + final_bias
    return (
        result,
        (normed_one, inverse_one, hidden_low, inner_act, active, normed_two, inverse_two),
    )


def back_branch(grad_out, kept_parts, params):
    final_gain = params[6]
    normed_two, inverse_two = kept_parts[5:]
    final_gain_grad = jnp.sum(grad_out * normed_two, axis=0)
    final_bias_grad = jnp.sum(grad_out, axis=0)
    grad_sum_two = norm_back(grad_out * final_gain, normed_two, inverse_two)
    grad_branch = grad_sum_two.astype(jnp.bfloat16)
    bias_out_grad = jnp.sum(grad_branch.astype(jnp.float32), axis=0)
    return (grad_sum_two, grad_branch, (bias_out_grad, final_gain_grad, final_bias_grad))


def back_inner(grad_branch, kept_parts, params):
    weight_out, inner_act = (params[4], kept_parts[3])
    grad_active = jnp.einsum("ld,fd->lf", grad_branch, weight_out, preferred_element_type=jnp.float32)
    unused_value, gelu_pull = jax.vjp(gelu_tanh, inner_act)
    grad_inner = gelu_pull(grad_active)[0].astype(jnp.bfloat16)
    return (grad_inner, jnp.sum(grad_inner.astype(jnp.float32), axis=0))


def back_input(grad_sum_two, grad_inner, kept_parts, params, mixers):
    hidden_mix, seq_mix = mixers
    mix_gain, weight_in = (params[0], params[2])
    normed_one, inverse_one = kept_parts[:2]
    seq_len, model_width = normed_one.shape
    grad_hidden = grad_sum_two + jnp.einsum(
        "lf,df->ld", grad_inner, weight_in, preferred_element_type=jnp.float32
    )
    mix_gain_grad = jnp.sum(grad_hidden * normed_one, axis=0)
    mix_bias_grad = jnp.sum(grad_hidden, axis=0)
    grad_mixed = norm_back(grad_hidden * mix_gain, normed_one, inverse_one)
    grad_seq = grad_mixed.astype(jnp.bfloat16)
    grad_spectra = jnp.einsum(
        "ml,md->ld", seq_mix, grad_seq, preferred_element_type=jnp.float32
    ).astype(jnp.bfloat16)
    grad_spectra = grad_spectra.reshape(2, seq_len, model_width)
    grad_in = grad_mixed + jnp.einsum(
        "kle,kde->ld", grad_spectra, hidden_mix, preferred_element_type=jnp.float32
    )
    return (grad_in, (mix_gain_grad, mix_bias_grad))


def exchange(block, distance):
    devices = range(lax.axis_size("dp"))
    return lax.ppermute(block, "dp", [(i, i ^ distance) for i in devices])


def add_low(first, second):
    return (first.astype(jnp.float32) + second.astype(jnp.float32)).astype(jnp.bfloat16)


def own_and_other(block, position):
    half = block.shape[0] // 2
    return (
        lax.dynamic_slice_in_dim(block, position * half, half),
        lax.dynamic_slice_in_dim(block, (1 - position) * half, half),
    )


def both_halves(own, other, position):
    return jnp.where(position == 0, jnp.concatenate([own, other]), jnp.concatenate([other, own]))


def sum_over_line(block):
    line = lax.axis_size("dp") // 4
    place = lax.axis_index("dp") // 4

    def along(value, steps):
        return lax.ppermute(
            value, "dp", [(a * 4 + j, b * 4 + j) for a, b in steps for j in range(4)]
        )

    if line == 4:
        block = add_low(block, along(block, [(0, 1), (3, 2)]))
        block = add_low(block, along(block, [(1, 2), (2, 1)]))
        spread = along(block, [(1, 0), (2, 3)])
        return jnp.where((place == 1) | (place == 2), block, spread)
    distance = 4
    while distance < 4 * line:
        block = add_low(block, exchange(block, distance))
        distance *= 2
    return block


def sum_chunk(block):
    place = lax.axis_index("dp")
    core, pair = (place % 2, (place // 2) % 2)
    own, other = own_and_other(block, core)
    chip_sum = add_low(own, exchange(other, 1))
    own, other = own_and_other(chip_sum, pair)
    pair_sum = add_low(own, exchange(other, 2))
    whole = sum_over_line(pair_sum)
    whole = both_halves(whole, exchange(whole, 2), pair)
    whole = both_halves(whole, exchange(whole, 1), core)
    return whole.astype(jnp.float32)


def sum_small(vectors):
    packed = jnp.concatenate(vectors)
    distance = 1
    while distance < lax.axis_size("dp"):
        packed = packed + exchange(packed, distance)
        distance *= 2
    return jnp.split(packed, np.cumsum([v.shape[0] for v in vectors])[:-1])


CHUNKS = 2


def per_device(
    activations,
    out_cotangent,
    doc_lengths,
    mix_gain,
    mix_bias,
    weight_in,
    bias_in,
    weight_out,
    bias_out,
    final_gain,
    final_bias,
):
    is_first = lax.axis_index("pipe") == 0
    row_count, seq_len, model_width = activations.shape
    params = (
        mix_gain[0],
        mix_bias[0],
        weight_in[0],
        bias_in[0],
        weight_out[0],
        bias_out[0],
        final_gain[0],
        final_bias[0],
    )
    cos_hid, sin_hid = dft_tables(model_width)
    cos_seq, sin_seq = dft_tables(seq_len)
    mixers = (
        jnp.asarray(np.stack([cos_hid, sin_hid]), jnp.bfloat16),
        jnp.asarray(np.concatenate([cos_seq, -sin_seq], axis=1), jnp.bfloat16),
    )
    padding = doc_lengths[:, -1]
    positions = jnp.arange(seq_len, dtype=jnp.int32)
    token_mask = (positions[None, :] < (seq_len - padding)[:, None]).astype(jnp.float32)

    def forward(row_in):
        result, kept_parts = forward_parts(row_in[None], params, mixers)
        return (result[0].astype(jnp.bfloat16), tuple(part[0] for part in kept_parts))

    def back_row(grad_out, kept_parts):
        grad_sum_two, grad_branch, out_terms = back_branch(grad_out, kept_parts, params)
        grad_inner, bias_in_grad = back_inner(grad_branch, kept_parts, params)
        grad_in, in_terms = back_input(grad_sum_two, grad_inner, kept_parts, params, mixers)
        terms = (*in_terms, bias_in_grad, *out_terms)
        return (grad_in, terms, (kept_parts[2], kept_parts[4], grad_branch, grad_inner))

    def only_if(condition, work, *operands):
        shapes = jax.eval_shape(work, *operands)
        blank = jax.tree.map(lambda s: jnp.zeros(s.shape, s.dtype), shapes)
        return lax.cond(condition, work, lambda *unused: blank, *operands)

    def later_row(row_in, row):
        result, kept_parts = forward(row_in)
        cotangent = out_cotangent[row].astype(jnp.float32) * token_mask[row][:, None]
        grad_in, terms, kept = back_row(cotangent, kept_parts)
        return (result, grad_in.astype(jnp.bfloat16), terms, kept)

    first_done = [only_if(is_first, forward, activations[row]) for row in range(row_count)]
    handed = [from_behind(done[0], "pipe", 1) for done in first_done]
    later_done = [
        only_if(~is_first, functools.partial(later_row, row=row), handed[row])
        for row in range(row_count)
    ]
    returned = [from_behind(done[1], "pipe", -1) for done in later_done]
    rows_done = []
    for row in range(row_count):

        def first_back(grad_low, kept_parts, unused_done):
            return back_row(grad_low.astype(jnp.float32), kept_parts)

        def pass_on(unused_grad, unused_parts, done):
            return (done[1].astype(jnp.float32), done[2], done[3])

        rows_done.append(
            lax.cond(
                is_first, first_back, pass_on, returned[row], first_done[row][1], later_done[row]
            )
        )
    layer_rows = jnp.stack(
        [
            jnp.where(is_first, first_done[row][0], later_done[row][0])
            for row in range(row_count)
        ]
    )
    grad_rows = jnp.stack([done[0] for done in rows_done])
    small = [sum(parts) for parts in zip(*[done[1] for done in rows_done])]
    hidden_low, active, grad_branch, grad_inner = (
        jnp.concatenate(parts) for parts in zip(*[done[2] for done in rows_done])
    )

    def summed(left, right):
        pieces = jnp.split(left, CHUNKS, axis=1)
        partial = [
            jnp.einsum("tf,td->fd", piece, right, preferred_element_type=jnp.float32)
            for piece in pieces
        ]
        return jnp.concatenate([sum_chunk(part.astype(jnp.bfloat16)) for part in partial])

    weight_out_grad = summed(active, grad_branch)
    weight_in_grad = summed(hidden_low, grad_inner)
    small = sum_small(small)
    return (
        layer_rows[None],
        grad_rows[None],
        small[0][None],
        small[1][None],
        weight_in_grad[None],
        small[2][None],
        weight_out_grad[None],
        small[3][None],
        small[4][None],
        small[5][None],
    )


def solution(mesh):
    placed = (
        P("dp", None, None),
        P("dp", None, None),
        P("dp", None),
        P("pipe", None),
        P("pipe", None),
        P("pipe", None, None),
        P("pipe", None),
        P("pipe", None, None),
        P("pipe", None),
        P("pipe", None),
        P("pipe", None),
    )
    return jax.shard_map(
        per_device,
        mesh=mesh,
        in_specs=placed,
        out_specs=(
            P("pipe", "dp", None, None),
            P("pipe", "dp", None, None),
            P("pipe", None),
            P("pipe", None),
            P("pipe", None, None),
            P("pipe", None),
            P("pipe", None, None),
            P("pipe", None),
            P("pipe", None),
            P("pipe", None),
        ),
        check_vma=False,
    )
```

```python
import functools
import math

import jax
import jax.numpy as jnp
import numpy as np
from jax import lax
from jax.experimental import pallas as pl
from jax.experimental.pallas import tpu as pltpu
from jax.sharding import PartitionSpec as P

eps_norm = 1e-06
low, wide = jnp.bfloat16, jnp.float32
slope = math.sqrt(2.0 / math.pi)
cubic = 0.044715
VMEM_SPARE = 6 * 2**20
SHARE = 800000000
VMEM_SHARED = 44 * 2**20
VMEM_ALL = 62 * 2**20
BLOCK = 256
ANY = pl.BlockSpec(memory_space=pltpu.HBM)
SCALARS = pl.BlockSpec(memory_space=pltpu.SMEM)
WHOLE = pl.BlockSpec(memory_space=pltpu.VMEM)

MIX_GAIN, MIX_BIAS, BIAS_OUT, FINAL_GAIN, FINAL_BIAS, BIAS_IN = 0, 1, 2, 3, 4, 16


class Names:
    def __getattr__(self, name):
        return name


n = Names()


def from_behind(block, axis, distance):
    devices = range(lax.axis_size(axis))
    route = [(i - distance, i) for i in devices if i - distance in devices]
    return lax.ppermute(block, axis, route)


def dft_tables(table_len):
    indices = np.arange(table_len)
    angles = (indices[:, None] * indices[None, :] % table_len) * (2.0 * math.pi / table_len)
    scaled = 1.0 / math.sqrt(table_len)
    return (np.cos(angles) * scaled, np.sin(angles) * scaled)


def matmul(left, right, left_dim=1, right_dim=0):
    return lax.dot_general(
        left, right, (((left_dim,), (right_dim,)), ((), ())), preferred_element_type=wide
    )


def mean_last(values):
    return jnp.mean(values, axis=-1, keepdims=True)


def normalize(values):
    centred = values - mean_last(values)
    inverse = lax.rsqrt(mean_last(centred * centred) + eps_norm)
    return (centred * inverse, inverse)


def norm_back(grad_norm, normed, inverse):
    return inverse * (grad_norm - mean_last(grad_norm) - normed * mean_last(grad_norm * normed))


def gelu_parts(values):
    square = values * values
    part = 0.5 + 0.5 * jnp.tanh(values * (slope + slope * cubic * square))
    active = values * part
    step = 2.0 * slope + 6.0 * slope * cubic * square
    return (active, part + active * (1.0 - part) * step)


def each_block(seq_len, body):
    def step(index, carry):
        body(pl.ds(pl.multiple_of(index * BLOCK, BLOCK), BLOCK), index == 0)
        return carry

    lax.fori_loop(0, seq_len // BLOCK, step, 0)


def add_rows(values):
    return jnp.sum(values, axis=0, keepdims=True)


class Copies:
    def __init__(self, sems):
        self.sems, self.used = sems, 0

    def start(self, source, target):
        copy = pltpu.make_async_copy(source, target, self.sems.at[self.used])
        self.used += 1
        copy.start()
        return copy


def add_to(small, place, values):
    small[place : place + 1] += add_rows(values)


def spectra_forward(s, x, hidden_mix, wait_later):
    seq_len = x.shape[0]

    def step(k, carry):
        pl.when(k == 1)(wait_later)
        rows = pl.ds(pl.multiple_of(k * seq_len, seq_len), seq_len)
        s.spectra[rows] = matmul(x[...], hidden_mix[k]).astype(low)
        return carry

    lax.fori_loop(0, 2, step, 0)


def forward_block(r, rows, wait_out):
    width = r.row.shape[1]
    normed, inverse = normalize(r.row[rows].astype(wide) + matmul(r.seq_mix[rows], r.spectra[...]))
    r.normed_one[rows] = normed
    r.inverse_one[rows] = jnp.broadcast_to(inverse, (BLOCK, 128))
    r.hidden_low[rows] = (normed * r.mix_gain[...] + r.mix_bias[...]).astype(low)
    for part in parts_of(r.weight_in.shape[1], width):
        inner = matmul(r.hidden_low[rows], r.weight_in[:, part]) + r.bias_in[:, part]
        active, gelu_grad = gelu_parts(inner)
        active = active.astype(low)
        r.active[rows, part] = active
        r.gelu_grad[rows, part] = gelu_grad.astype(low)
        if part.start == 0:
            wait_out()
            r.sum[rows] = matmul(active, r.weight_out[part])
        else:
            r.sum[rows] += matmul(active, r.weight_out[part])
    hidden = r.normed_one[rows] * r.mix_gain[...] + r.mix_bias[...]
    normed, inverse = normalize(hidden + r.sum[rows] + r.bias_out[...])
    r.normed_two[rows] = normed
    r.inverse_two[rows] = jnp.broadcast_to(inverse, (BLOCK, 128))
    r.result[rows] = (normed * r.final_gain[...] + r.final_bias[...]).astype(low)


def branch_back(r, rows, grad_out):
    normed = r.normed_two[rows]
    grad_sum = norm_back(grad_out * r.final_gain[...], normed, r.inverse_two[rows][:, :1])
    r.grad_sum[rows] = grad_sum
    grad_branch = grad_sum.astype(low)
    r.grad_branch[rows] = grad_branch
    add_to(r.small, BIAS_OUT, grad_branch.astype(wide))
    add_to(r.small, FINAL_GAIN, grad_out * normed)
    add_to(r.small, FINAL_BIAS, grad_out)


def inner_back(r, rows, index):
    width = r.grad_branch.shape[1]
    part = slice(index * width, (index + 1) * width)
    grad_active = matmul(r.grad_branch[rows], r.weight_out[part], 1, 1)
    grad_inner = grad_active * r.gelu_grad[rows, part].astype(wide)
    r.grad_inner[rows, part] = grad_inner.astype(low)
    add_to(r.small, BIAS_IN + index, grad_inner)


def input_back(r, rows):
    grad_hidden = r.grad_sum[rows] + matmul(r.grad_inner[rows], r.weight_in[...], 1, 1)
    normed = r.normed_one[rows]
    r.sum[rows] = norm_back(grad_hidden * r.mix_gain[...], normed, r.inverse_one[rows][:, :1])
    add_to(r.small, MIX_GAIN, grad_hidden * normed)
    add_to(r.small, MIX_BIAS, grad_hidden)


def spectra_back(s, put, hidden_mix, seq_mix):
    seq_len, width = s.sum.shape
    s.grad_seq[...] = s.sum[...].astype(low)

    def step(k, carry):
        rows = pl.ds(pl.multiple_of(k * seq_len, seq_len), seq_len)
        s.spectra[rows] = matmul(seq_mix[:, rows], s.grad_seq[...]).astype(low)
        return carry

    lax.fori_loop(0, 2, step, 0)

    def block(rows, first):
        later = pl.ds(rows.start + seq_len, BLOCK)
        put(
            rows,
            s.sum[rows]
            + matmul(s.spectra[rows], hidden_mix[0])
            + matmul(s.spectra[later], hidden_mix[1]),
        )

    each_block(seq_len, block)


class Named:
    def __init__(self, refs):
        self.__dict__.update(refs)


class Order:
    last = None
    shares_vmem = False


order = Order()


def run_kernel(name, body, inputs, outputs, taken, scratch):
    if order.last is not None:
        inputs = {**inputs, n.after: (order.last, ANY)}
    outputs = {**outputs, n.turn: (jax.ShapeDtypeStruct((8, 128), wide), ANY)}
    n_in, n_out = len(inputs), len(outputs)
    names_in, names_out = list(inputs), list(outputs)

    held = sum(math.prod(shape) * np.dtype(dtype).itemsize for shape, dtype in scratch.values())
    for array, spec in (*inputs.values(), *outputs.values()):
        if spec is WHOLE:
            held += math.prod(array.shape) * np.dtype(array.dtype).itemsize

    def kernel(*refs):
        named = dict(zip(names_in, refs[:n_in]))
        for name, ref in zip(names_out, refs[n_in : n_in + n_out]):
            named[name] = ref
        named.update(zip(scratch, refs[n_in + n_out : -1]))
        body(Named(named), Copies(refs[-1]))

    results = pl.pallas_call(
        kernel,
        name=name,
        in_specs=[spec for _, spec in inputs.values()],
        out_shape=[jax.ShapeDtypeStruct(shape.shape, shape.dtype) for shape, _ in outputs.values()],
        out_specs=[spec for _, spec in outputs.values()],
        scratch_shapes=[
            *[pltpu.VMEM(*shape) for shape in scratch.values()],
            pltpu.SemaphoreType.DMA((24,)),
        ],
        input_output_aliases={names_in.index(name): names_out.index(name) for name in taken},
        compiler_params=pltpu.CompilerParams(
            vmem_limit_bytes=max(VMEM_SHARED, VMEM_SPARE + held) if order.shares_vmem else VMEM_ALL
        ),
        cost_estimate=pl.CostEstimate(flops=SHARE if order.shares_vmem else 1, bytes_accessed=1, transcendentals=0),
    )(*[array for array, _ in inputs.values()])
    results = dict(zip(names_out, results))
    order.last = results.pop(n.turn)
    return results


class Sections:
    def __init__(self, where, rows, sizes, tables, weights, vectors):
        self.where, self.rows, self.sizes = where, rows, sizes
        self.tables = dict(zip((n.mix_hbm, n.seq_hbm), tables))
        self.weights = dict(zip((n.in_hbm, n.out_hbm), weights))
        self.vectors = vectors
        self.kept = {}
        seq_len, width, inner = sizes
        self.shapes = {
            n.row: ((seq_len, width), low),
            n.cot: ((seq_len, width), low),
            n.hidden_mix: ((2, width, width), low),
            n.seq_mix: ((seq_len, 2 * seq_len), low),
            n.weight_in: ((width, inner), low),
            n.weight_out: ((inner, width), low),
            n.spectra: ((2 * seq_len, width), low),
            n.sum: ((seq_len, width), wide),
            n.normed_one: ((seq_len, width), wide),
            n.inverse_one: ((seq_len, 128), wide),
            n.normed_two: ((seq_len, width), wide),
            n.inverse_two: ((seq_len, 128), wide),
            n.hidden_low: ((seq_len, width), low),
            n.active: ((seq_len, inner), low),
            n.gelu_grad: ((seq_len, inner), low),
            n.result: ((seq_len, width), low),
            n.grad_sum: ((seq_len, width), wide),
            n.grad_branch: ((seq_len, width), low),
            n.grad_inner: ((seq_len, inner), low),
            n.grad_seq: ((seq_len, width), low),
            n.grad_mixed: ((seq_len, width), wide),
            n.grad_low: ((seq_len, width), low),
            n.grad_wide: ((seq_len, width), wide),
        }
        self.small = jnp.zeros((64, width), wide)
        self.columns, self.stores = {}, {}
        for store, names in (
            (n.store_low, (n.active, n.gelu_grad, n.grad_inner, n.hidden_low, n.grad_branch)),
            (n.store_wide, (n.normed_one, n.normed_two, n.grad_sum, n.grad_mixed, n.inverse_one, n.inverse_two)),
        ):
            first = 0
            for name in names:
                (length, size), dtype = self.shapes[name]
                self.columns[name] = (store, first, size)
                first += size
            self.stores[store] = jax.ShapeDtypeStruct((rows * length, first), dtype)
        for store, dtype in ((n.layer_rows, low), (n.grad_rows, wide)):
            self.columns[store] = (store, None, None)
            self.stores[store] = jax.ShapeDtypeStruct((rows, seq_len, width), dtype)

    def stage(self, title, body, owner, inputs, made, reads, writes, scratch, uses_small=False):
        inputs = {n.place: (self.where, SCALARS), **inputs}
        outputs = {name: (shape, ANY) for name, shape in made.items()}
        taken = []
        for store in dict.fromkeys(self.columns[name][0] for name in (*writes, *reads)):
            if store in self.kept:
                inputs[store] = (self.kept[store], ANY)
            if any(self.columns[name][0] == store for name in writes):
                if store in self.kept:
                    taken.append(store)
                outputs[store] = (self.stores[store], ANY)
        if uses_small:
            inputs[n.small_before] = (self.small, WHOLE)
            outputs[n.small] = (self.small, WHOLE)

        def kernel(refs, copies):
            for name in (*reads, *writes):
                store, first, size = self.columns[name]
                ref = getattr(refs, store)
                setattr(refs, name + n._kept, ref if size is None else ref.at[:, first : first + size])
            if uses_small:
                refs.small[...] = refs.small_before[...]
            pl.when(refs.place[0] == owner)(lambda: body(refs, copies))

        results = run_kernel(
            title, kernel, inputs, outputs, taken, {name: self.shapes[name] for name in scratch}
        )
        if uses_small:
            self.small = results.pop(n.small)
        for name in list(results):
            if name in self.stores:
                self.kept[name] = results.pop(name)
        return results

    def place(self, row):
        return pl.ds(row * self.sizes[0], self.sizes[0])

    def row_shape(self, dtype):
        return jax.ShapeDtypeStruct(self.sizes[:2], dtype)

    def any_inputs(self, arrays):
        return {name: (array, ANY) for name, array in arrays.items()}

    def vector_inputs(self):
        return {name: (array, WHOLE) for name, array in self.vectors.items()}

    def first_forward(self, row, activations, keeps, hands):
        keep = (n.gelu_grad, n.normed_one, n.inverse_one, n.normed_two, n.inverse_two, n.active, n.hidden_low)

        def body(r, copies):
            out_load = forward_loads(r, copies, r.x_hbm.at[row])

            def block(rows, first):
                forward_block(r, rows, lambda: pl.when(first)(out_load.wait))

            each_block(r.row.shape[0], block)
            stores = []
            if hands:
                stores.append(copies.start(r.result, r.handed))
            if keeps:
                stores.append(copies.start(r.result, r.layer_rows.at[row]))
                for name in keep:
                    target = getattr(r, name + n._kept).at[self.place(row)]
                    stores.append(copies.start(getattr(r, name), target))
            for done in stores:
                done.wait()

        inputs = {
            **self.any_inputs({n.x_hbm: activations, **self.tables, **self.weights}),
            **self.vector_inputs(),
        }
        return self.stage(
            n.first_forward,
            body,
            0,
            inputs,
            {n.handed: self.row_shape(low)} if hands else {},
            (),
            (*keep, n.layer_rows) if keeps else (),
            (n.row, n.hidden_mix, n.seq_mix, n.weight_in, n.weight_out, n.spectra, n.sum, n.result, *keep),
        ).get(n.handed)

    def later_both(self, row, handed, out_cotangent, lengths):
        keep = (n.active, n.hidden_low, n.grad_branch, n.grad_inner)

        def body(r, copies):
            stores = []

            def store(name):
                target = getattr(r, name + n._kept).at[self.place(row)]
                stores.append(copies.start(getattr(r, name), target))

            out_load = forward_loads(r, copies, r.x_hbm)
            cot_load = copies.start(r.cot_hbm.at[row], r.cot)
            filled = r.cot.shape[0] - r.lengths[row, r.lengths.shape[1] - 1]

            def block(rows, first):
                forward_block(r, rows, lambda: pl.when(first)(out_load.wait))
                pl.when(first)(cot_load.wait)
                token = rows.start + lax.broadcasted_iota(jnp.int32, (BLOCK, r.cot.shape[1]), 0)
                branch_back(r, rows, jnp.where(token < filled, r.cot[rows].astype(wide), 0.0))
                for index in range(r.weight_out.shape[0] // r.cot.shape[1]):
                    inner_back(r, rows, index)
                input_back(r, rows)

            each_block(r.row.shape[0], block)
            stores.append(copies.start(r.result, r.layer_rows.at[row]))
            for name in keep:
                store(name)

            def put(rows, values):
                r.grad_low[rows] = values.astype(low)
                r.grad_wide[rows] = r.grad_low[rows].astype(wide)

            spectra_back(r, put, r.hidden_mix, r.seq_mix)
            stores.append(copies.start(r.grad_low, r.returned))
            stores.append(copies.start(r.grad_wide, r.grad_rows.at[row]))
            for store_done in stores:
                store_done.wait()

        inputs = {
            n.lengths: (lengths, SCALARS),
            **self.any_inputs(
                {n.x_hbm: handed, n.cot_hbm: out_cotangent, **self.tables, **self.weights}
            ),
            **self.vector_inputs(),
        }
        return self.stage(
            n.later_both,
            body,
            1,
            inputs,
            {n.returned: self.row_shape(low)},
            (),
            (*keep, n.layer_rows, n.grad_rows),
            tuple(name for name in self.shapes if name != n.grad_mixed),
            True,
        )[n.returned]

    def first_back_branch(self, row, returned):
        keep = (n.grad_branch, n.grad_sum)
        need = (n.normed_two, n.inverse_two)

        def body(r, copies):
            loads = [copies.start(r.cot_hbm, r.cot)]
            for name in need:
                loads.append(copies.start(getattr(r, name + n._kept).at[self.place(row)], getattr(r, name)))
            for load in loads:
                load.wait()
            each_block(
                r.cot.shape[0], lambda rows, first: branch_back(r, rows, r.cot[rows].astype(wide))
            )
            stores = [
                copies.start(getattr(r, name), getattr(r, name + n._kept).at[self.place(row)])
                for name in keep
            ]
            for store in stores:
                store.wait()

        inputs = {
            **self.any_inputs({n.cot_hbm: returned}),
            n.final_gain: (self.vectors[n.final_gain], WHOLE),
        }
        self.stage(
            n.back_branch, body, 0, inputs, {}, need, keep, (n.cot, *need, *keep), True
        )

    def first_back_inner(self, row):
        need = (n.gelu_grad, n.grad_branch)

        def body(r, copies):
            rows = self.place(row)
            first = copies.start(r.grad_branch_kept.at[rows], r.grad_branch)
            loads, stores = [], []
            for part in parts_of(r.grad_inner.shape[1], r.grad_branch.shape[1]):
                loads.append(
                    (
                        copies.start(r.out_hbm.at[0, part], r.weight_out.at[part]),
                        copies.start(r.gelu_grad_kept.at[rows, part], r.gelu_grad.at[:, part]),
                    )
                )
            first.wait()
            for index, part in enumerate(parts_of(r.grad_inner.shape[1], r.grad_branch.shape[1])):
                for load in loads[index]:
                    load.wait()
                inner_back(r, slice(None), index)
                stores.append(
                    copies.start(r.grad_inner.at[:, part], r.grad_inner_kept.at[rows, part])
                )
            for store in stores:
                store.wait()

        inputs = self.any_inputs({n.out_hbm: self.weights[n.out_hbm]})
        self.stage(
            n.back_inner, body, 0, inputs, {}, need, (n.grad_inner,), (n.weight_out, n.grad_inner, *need), True
        )

    def first_back_input(self, row):
        need = (n.grad_inner, n.grad_sum, n.normed_one, n.inverse_one)

        def body(r, copies):
            loads = [copies.start(r.in_hbm.at[0], r.weight_in)]
            for name in need:
                loads.append(copies.start(getattr(r, name + n._kept).at[self.place(row)], getattr(r, name)))
            for load in loads:
                load.wait()
            each_block(r.sum.shape[0], lambda rows, first: input_back(r, rows))
            copies.start(r.sum, r.grad_mixed_kept.at[self.place(row)]).wait()

        inputs = {
            **self.any_inputs({n.in_hbm: self.weights[n.in_hbm]}),
            n.mix_gain: (self.vectors[n.mix_gain], WHOLE),
        }
        self.stage(
            n.back_input, body, 0, inputs, {}, need, (n.grad_mixed,), (n.weight_in, n.sum, *need), True
        )

    def first_back_spectra(self, row):
        def body(r, copies):
            loads = [
                copies.start(r.grad_mixed_kept.at[self.place(row)], r.sum),
                copies.start(r.seq_hbm, r.seq_mix),
                copies.start(r.mix_hbm, r.hidden_mix),
            ]
            for load in loads:
                load.wait()

            def put(rows, values):
                r.grad_wide[rows] = values

            spectra_back(r, put, r.hidden_mix, r.seq_mix)
            copies.start(r.grad_wide, r.grad_rows.at[row]).wait()

        self.stage(
            n.back_spectra,
            body,
            0,
            self.any_inputs(self.tables),
            {},
            (n.grad_mixed,),
            (n.grad_rows,),
            (n.hidden_mix, n.seq_mix, n.spectra, n.sum, n.grad_seq, n.grad_wide),
        )

    def weight_chunk(self, kind, first, size, small):
        seq_len, width, inner = self.sizes
        tokens = self.rows * seq_len
        left, right = ((n.active, n.grad_branch), (n.hidden_low, n.grad_inner))[kind]
        height, columns = ((size, width), (width, size))[kind]
        half, quarter = height // 2, height // 4
        extra = 0 if small is None else small.shape[0] // 4
        long = quarter + extra

        def body(r, copies):
            left_first = self.columns[left][1] + (first if kind == 0 else 0)
            right_first = self.columns[right][1] + (first if kind == 1 else 0)
            right_load = copies.start(r.store.at[:, pl.ds(right_first, columns)], r.right)
            left_loads = [
                copies.start(
                    r.store.at[:, pl.ds(pl.multiple_of(left_first + core * half, 128), half)], r.left.at[k]
                )
                for k, core in ((0, 1 - r.place[1]), (1, r.place[1]))
            ]
            right_load.wait()
            for k, core in ((0, 1 - r.place[1]), (1, r.place[1])):
                left_loads[k].wait()
                total = matmul(r.left[k], r.right[...], 0, 0).astype(low)
                for piece in range(2):
                    target = (r.others_first, r.others_second)[piece] if k == 0 else r.own
                    begin = 0 if k == 0 else piece * long
                    target[begin : begin + quarter, :] = total[piece * quarter : (piece + 1) * quarter]
                    if extra:
                        rows = pl.ds(pl.multiple_of((2 * core + piece) * extra, extra), extra)
                        target[begin + quarter : begin + long, :width] = r.small[rows, :].astype(low)

        shape = jax.ShapeDtypeStruct((long, columns), low)
        inputs = {n.place: (self.where, SCALARS), n.store: (self.kept[n.store_low], ANY)}
        if extra:
            inputs[n.small] = (small, WHOLE)
        results = run_kernel(
            n.product,
            body,
            inputs,
            {
                n.own: (jax.ShapeDtypeStruct((2 * long, columns), low), WHOLE),
                n.others_first: (shape, WHOLE),
                n.others_second: (shape, WHOLE),
            },
            (),
            {n.left: ((2, tokens, half), low), n.right: ((tokens, columns), low)},
        )
        return results[n.own], results[n.others_first], results[n.others_second]

    def others_back_spectra(self, row):
        for earlier in range(row):
            self.first_back_spectra(earlier)

    def chunk(self, kind, first, size, with_small):
        return self.weight_chunk(kind, first, size, self.small if with_small else None)


def parts_of(inner, width):
    return [slice(first, first + width) for first in range(0, inner, width)]


def forward_loads(r, copies, x_hbm):
    x_load = copies.start(x_hbm, r.row)
    mix_loads = [copies.start(r.mix_hbm.at[k], r.hidden_mix.at[k]) for k in range(2)]
    x_load.wait()
    mix_loads[0].wait()
    seq_load = copies.start(r.seq_hbm, r.seq_mix)
    in_load = copies.start(r.in_hbm.at[0], r.weight_in)
    out_load = copies.start(r.out_hbm.at[0], r.weight_out)
    spectra_forward(r, r.row, r.hidden_mix, mix_loads[1].wait)
    seq_load.wait()
    in_load.wait()
    return out_load


def exchange(block, distance):
    devices = range(lax.axis_size("dp"))
    return lax.ppermute(block, "dp", [(i, i ^ distance) for i in devices])


def along_line(block, steps):
    route = [(a * 4 + j, b * 4 + j) for a, b in steps for j in range(4)]
    return lax.ppermute(block, "dp", route)


def low_sum(first, second):
    return (first[...].astype(wide) + second[...].astype(wide)).astype(low)


class Sum:
    def __init__(self, place, make):
        self.place, self.make = place, make

    def kernel(self, title, body, shapes, **come):
        results = run_kernel(
            title,
            body,
            {
                n.place: (self.place, SCALARS),
                n.own: (self.own, WHOLE),
                **{name: (array, WHOLE) for name, array in come.items()},
            },
            {name: (jax.ShapeDtypeStruct(shape, low), WHOLE) for name, shape in shapes.items()},
            (),
            {},
        )
        return [results[name] for name in shapes]

    def add(self):
        def body(r, copies):
            r.total[...] = low_sum(r.own, r.come)

        (self.own,) = self.kernel(n.add, body, {n.total: self.own.shape}, come=self.come)

    def core(self):
        self.own, first, second = self.make()
        self.come = exchange(first, 1), exchange(second, 1)

    def pair(self):
        rows, columns = self.own.shape
        half = rows // 2

        def body(r, copies):
            @pl.when(r.place[2] == 0)
            def keep_first():
                r.kept[...] = low_sum(r.own.at[:half], r.first)
                r.other[...] = low_sum(r.own.at[half:], r.second)

            @pl.when(r.place[2] == 1)
            def keep_second():
                r.other[...] = low_sum(r.own.at[:half], r.first)
                r.kept[...] = low_sum(r.own.at[half:], r.second)

        shapes = {n.kept: (half, columns), n.other: (half, columns)}
        first, second = self.come
        self.own, other = self.kernel(n.pair, body, shapes, first=first, second=second)
        self.come = exchange(other, 2)

    def inward(self):
        self.add()
        line = lax.axis_size("dp") // 4
        if line == 4:
            self.come = along_line(self.own, [(0, 1), (3, 2)])
            return
        distance = 4
        while distance < 4 * line:
            self.come = exchange(self.own, distance)
            distance *= 2
            if distance < 4 * line:
                self.add()

    def middle(self):
        self.add()
        if lax.axis_size("dp") == 16:
            self.come = along_line(self.own, [(1, 2), (2, 1)])

    def outward(self):
        if lax.axis_size("dp") == 16:
            self.add()
            self.come = along_line(self.own, [(1, 0), (2, 3)])

    def pair_back(self):
        if lax.axis_size("dp") == 16:

            def body(r, copies):
                r.total[...] = jnp.where(r.place[3] == 1, r.own[...], r.come[...])

            (self.own,) = self.kernel(n.take, body, {n.total: self.own.shape}, come=self.come)
        self.come = exchange(self.own, 2)

    def core_back(self):
        def body(r, copies):
            r.pair_part[...] = r.come[...]

        (self.pair_part,) = self.kernel(n.join, body, {n.pair_part: self.own.shape}, come=self.come)
        self.come = exchange(self.own, 1), exchange(self.pair_part, 1)

    def finish(self, target, shape, kind, first, size, extra):
        rows, columns = self.own.shape
        length = rows - extra

        def body(r, copies):
            stores = []
            parts = (r.own, r.pair_part, r.core_own, r.core_pair)
            for index, part in enumerate(parts):
                core = r.place[1] if index < 2 else 1 - r.place[1]
                pair = r.place[2] if index % 2 == 0 else 1 - r.place[2]
                quarter = 2 * core + pair
                r.full[index] = part[:length].astype(wide)
                rows_at = pl.ds(pl.multiple_of(quarter * length + (first if kind == 0 else 0), 16), length)
                where = (0, rows_at) if kind == 0 else (0, rows_at, pl.ds(first, size))
                stores.append(copies.start(r.full.at[index], r.target.at[where]))
                if extra:
                    to = pl.ds(pl.multiple_of(quarter * extra, extra), extra)
                    r.small[to, :] = part[length:, :size].astype(wide)
            for store in stores:
                store.wait()

        inputs = {
            n.place: (self.place, SCALARS),
            n.own: (self.own, WHOLE),
            n.pair_part: (self.pair_part, WHOLE),
            n.core_own: (self.come[0], WHOLE),
            n.core_pair: (self.come[1], WHOLE),
        }
        if target is not None:
            inputs[n.target] = (target, ANY)
        outputs = {n.target: (jax.ShapeDtypeStruct(shape, wide), ANY)}
        if extra:
            outputs[n.small] = (jax.ShapeDtypeStruct((4 * extra, columns), wide), WHOLE)
        results = run_kernel(
            n.finish,
            body,
            inputs,
            outputs,
            (n.target,) if target is not None else (),
            {n.full: ((4, length, columns), wide)},
        )
        return results[n.target], results.get(n.small)


CHUNKS = ((0, 6), (0, 6), (1, 6), (1, 6))
STEPS = (
    (1, n.core),
    (0, n.core),
    (1, n.pair),
    (None, n.first_back_inner),
    (2, n.core),
    (0, n.pair),
    (1, n.inward),
    (None, n.first_back_input),
    (3, n.core),
    (2, n.pair),
    (0, n.inward),
    (1, n.middle),
    (3, n.pair),
    (2, n.inward),
    (0, n.middle),
    (1, n.outward),
    (3, n.inward),
    (2, n.middle),
    (0, n.outward),
    (1, n.pair_back),
    (None, n.first_back_spectra),
    (3, n.middle),
    (2, n.outward),
    (1, n.core_back),
    (0, n.pair_back),
    (3, n.outward),
    (2, n.pair_back),
    (1, n.finish),
    (None, n.others_back_spectra),
    (0, n.core_back),
    (3, n.pair_back),
    (2, n.core_back),
    (0, n.finish),
    (3, n.core_back),
    (2, n.finish),
    (3, n.finish),
)


def per_device(
    activations,
    out_cotangent,
    doc_lengths,
    mix_gain,
    mix_bias,
    weight_in,
    bias_in,
    weight_out,
    bias_out,
    final_gain,
    final_bias,
):
    rows, seq_len, width = activations.shape
    inner = weight_in.shape[2]
    index = lax.axis_index("dp").astype(jnp.int32)
    line = index // 4
    on_inside = ((line == 1) | (line == 2)).astype(jnp.int32)
    section = lax.axis_index("pipe").astype(jnp.int32)
    place = jnp.stack([section, index % 2, index // 2 % 2, on_inside])
    order.last, order.shares_vmem = None, False
    seq_cos, seq_sin = dft_tables(seq_len)
    tables = (
        jnp.asarray(np.stack(dft_tables(width)), low),
        jnp.asarray(np.concatenate([seq_cos, -seq_sin], axis=1), low),
    )
    vectors = {
        n.mix_gain: mix_gain,
        n.mix_bias: mix_bias,
        n.bias_in: bias_in,
        n.bias_out: bias_out,
        n.final_gain: final_gain,
        n.final_bias: final_bias,
    }
    work = Sections(place, rows, (seq_len, width, inner), tables, (weight_in, weight_out), vectors)
    handed = []
    for row in range(rows):
        result = work.first_forward(row, activations, row == rows - 1, True)
        handed.append(from_behind(result, "pipe", 1))
    for row in range(rows - 1):
        work.first_forward(row, activations, True, False)
    returned = []
    for row in range(rows):
        result = work.later_both(row, handed[row], out_cotangent, doc_lengths)
        returned.append(from_behind(result, "pipe", -1))
    for row in range(rows):
        work.first_back_branch(row, returned[row])
        if row < rows - 1:
            work.first_back_inner(row)
            work.first_back_input(row)
    order.shares_vmem = True
    sums, first = [], [0, 0]
    for kind, units in CHUNKS:
        size = units * inner // 12
        last = len(sums) == len(CHUNKS) - 1
        make = functools.partial(work.chunk, kind, first[kind], size, last)
        sums.append((Sum(place, make), kind, first[kind], size, 16 if last else 0))
        first[kind] += size
    shapes, targets = (weight_out.shape, weight_in.shape), [None, None]
    for index, step in STEPS:
        if index is None:
            getattr(work, step)(rows - 1)
        elif step == n.finish:
            chunk, kind, *rest = sums[index]
            targets[kind], small = chunk.finish(targets[kind], shapes[kind], kind, *rest)
        else:
            getattr(sums[index][0], step)()
    return (
        work.kept[n.layer_rows][None],
        work.kept[n.grad_rows][None],
        small[MIX_GAIN, :width][None],
        small[MIX_BIAS, :width][None],
        targets[1],
        small[BIAS_IN : BIAS_IN + inner // width, :width].reshape(1, inner),
        targets[0],
        small[BIAS_OUT, :width][None],
        small[FINAL_GAIN, :width][None],
        small[FINAL_BIAS, :width][None],
    )


def solution(mesh):
    placed = (
        P("dp", None, None),
        P("dp", None, None),
        P("dp", None),
        P("pipe", None),
        P("pipe", None),
        P("pipe", None, None),
        P("pipe", None),
        P("pipe", None, None),
        P("pipe", None),
        P("pipe", None),
        P("pipe", None),
    )
    return jax.shard_map(
        per_device,
        mesh=mesh,
        in_specs=placed,
        out_specs=(
            P("pipe", "dp", None, None),
            P("pipe", "dp", None, None),
            P("pipe", None),
            P("pipe", None),
            P("pipe", None, None),
            P("pipe", None),
            P("pipe", None, None),
            P("pipe", None),
            P("pipe", None),
            P("pipe", None),
        ),
        check_vma=False,
    )
```

```python
import functools
import math

import jax
import jax.numpy as jnp
import numpy as np
from jax import lax
from jax.experimental import pallas as pl
from jax.experimental.pallas import tpu as pltpu
from jax.sharding import PartitionSpec as P

eps_norm = 1e-06
low, wide = jnp.bfloat16, jnp.float32
slope = math.sqrt(2.0 / math.pi)
cubic = 0.044715
VMEM_SPARE = 6 * 2**20
SHARE = 800000000
VMEM_SHARED = 44 * 2**20
VMEM_ALL = 62 * 2**20
VMEM_LATER = 50 * 2**20
BLOCK = 256
ANY = pl.BlockSpec(memory_space=pltpu.HBM)
SCALARS = pl.BlockSpec(memory_space=pltpu.SMEM)
WHOLE = pl.BlockSpec(memory_space=pltpu.VMEM)

MIX_GAIN, MIX_BIAS, BIAS_OUT, FINAL_GAIN, FINAL_BIAS, BIAS_IN = 0, 1, 2, 3, 4, 16


class Names:
    def __getattr__(self, name):
        return name


n = Names()


def from_behind(block, axis, distance):
    devices = range(lax.axis_size(axis))
    route = [(i - distance, i) for i in devices if i - distance in devices]
    return lax.ppermute(block, axis, route)


def dft_tables(table_len):
    indices = np.arange(table_len)
    angles = (indices[:, None] * indices[None, :] % table_len) * (2.0 * math.pi / table_len)
    scaled = 1.0 / math.sqrt(table_len)
    return (np.cos(angles) * scaled, np.sin(angles) * scaled)


def make_tables(width, seq_len):
    half = width // 2
    hid_cos, hid_sin = dft_tables(width)
    seq_cos, seq_sin = dft_tables(seq_len)
    hidden_mix = np.concatenate([hid_cos[:, : half + 1], hid_sin[:, 1:half]], axis=1)
    seq_mix = np.concatenate([seq_cos, -seq_sin], axis=1)
    return jnp.asarray(hidden_mix, low), jnp.asarray(seq_mix, low)


def matmul(left, right, left_dim=1, right_dim=0):
    return lax.dot_general(
        left, right, (((left_dim,), (right_dim,)), ((), ())), preferred_element_type=wide
    )


def mean_last(values):
    return jnp.mean(values, axis=-1, keepdims=True)


def normalize(values):
    centred = values - mean_last(values)
    inverse = lax.rsqrt(mean_last(centred * centred) + eps_norm)
    return (centred * inverse, inverse)


def norm_back(grad_norm, normed, inverse):
    return inverse * (grad_norm - mean_last(grad_norm) - normed * mean_last(grad_norm * normed))


def gelu_parts(values):
    square = values * values
    part = 0.5 + 0.5 * jnp.tanh(values * (slope + slope * cubic * square))
    active = values * part
    step = 2.0 * slope + 6.0 * slope * cubic * square
    return (active, part + active * (1.0 - part) * step)


def nothing():
    pass


def place_of():
    index = lax.axis_index("dp")
    line = index // 4
    inside = jnp.where((line == 1) | (line == 2), 1, 0)
    return lax.axis_index("pipe"), index % 2, index // 2 % 2, inside


def each_block(seq_len, body):
    def step(index, carry):
        body(pl.ds(pl.multiple_of(index * BLOCK, BLOCK), BLOCK), index)
        return carry

    lax.fori_loop(0, seq_len // BLOCK, step, 0)


def at_block(index, plans, call):
    for place in range(len(plans[0])):
        calls = [getattr(blocks[place], call) for blocks in plans]
        pl.when(index == place)(functools.partial(do_all, calls))


def wait_all(plans):
    do_all(copy.wait for blocks in plans for copy in blocks)


def add_rows(values):
    return jnp.sum(values, axis=0, keepdims=True)


class Copy:
    def __init__(self, source, target, sem):
        self.parts = source, target, sem

    def start(self):
        pltpu.make_async_copy(*self.parts).start()

    def wait(self):
        pltpu.make_async_copy(*self.parts).wait()


class Copies:
    def __init__(self, sems):
        self.sems, self.used = sems, 0

    def plan(self, source, target):
        self.used += 1
        return Copy(source, target, self.sems.at[self.used - 1])

    def blocks(self, source, target):
        parts = [slice(first, first + BLOCK) for first in range(0, target.shape[0], BLOCK)]
        return [self.plan(source.at[part], target.at[part]) for part in parts]

    def start(self, source, target):
        copy = self.plan(source, target)
        copy.start()
        return copy


def do_all(calls):
    for call in calls:
        call()


def add_to(small, place, values):
    small[place : place + 1] += add_rows(values)


def first_lane(values):
    return lax.broadcasted_iota(jnp.int32, values.shape, 1) == 0


def mirror(values):
    groups = values.shape[1] // 128
    parts = [values[:, 128 * g : 128 * (g + 1)] for g in range(groups)]
    lane = lax.broadcasted_iota(jnp.int32, parts[0].shape, 1)
    turned = [jnp.take_along_axis(part, lax.rem(128 - lane, 128), axis=1) for part in parts]
    mirrored = [
        jnp.where(lane == 0, turned[-g % groups], turned[groups - 1 - g]) for g in range(groups)
    ]
    return jnp.concatenate(mirrored, axis=1)


def mixed_rows(r, rows):
    seq_len, width = r.spectra.shape
    half = width // 2
    even = matmul(r.seq_mix[rows, :seq_len], r.spectra[:, : half + 128])
    odd = matmul(r.seq_mix[rows, seq_len:], r.spectra[:, half:])
    middle = even[:, half : half + 1]
    even = even[:, :half]
    odd = jnp.where(first_lane(odd), 0.0, odd)
    later = mirror(even - odd)
    return even + odd, jnp.where(first_lane(later), middle, later)


def forward_block(r, rows, index, in_load, out_load):
    width = r.row.shape[1]
    half = width // 2
    begin, end = mixed_rows(r, rows)
    r.sum[rows, :half] = r.row[rows, :half].astype(wide) + begin
    r.sum[rows, half:] = r.row[rows, half:].astype(wide) + end
    normed, inverse = normalize(r.sum[rows])
    r.normed_one[rows] = normed
    r.inverse_one[rows] = jnp.broadcast_to(inverse, (BLOCK, 128))
    r.hidden_low[rows] = (normed * r.mix_gain[...] + r.mix_bias[...]).astype(low)
    pl.when(index == 0)(in_load.wait)
    for part in parts_of(r.weight_in.shape[1], width):
        inner = matmul(r.hidden_low[rows], r.weight_in[:, part]) + r.bias_in[:, part]
        active, gelu_grad = gelu_parts(inner)
        active = active.astype(low)
        r.active[rows, part] = active
        r.gelu_grad[rows, part] = gelu_grad.astype(low)
        if part.start == 0:
            pl.when(index == 0)(out_load.wait)
            r.sum[rows] = matmul(active, r.weight_out[part])
        else:
            r.sum[rows] += matmul(active, r.weight_out[part])
    hidden = r.normed_one[rows] * r.mix_gain[...] + r.mix_bias[...]
    normed, inverse = normalize(hidden + r.sum[rows] + r.bias_out[...])
    r.normed_two[rows] = normed
    r.inverse_two[rows] = jnp.broadcast_to(inverse, (BLOCK, 128))
    r.result[rows] = (normed * r.final_gain[...] + r.final_bias[...]).astype(low)


def branch_back(r, rows, grad_out):
    normed = r.normed_two[rows]
    grad_sum = norm_back(grad_out * r.final_gain[...], normed, r.inverse_two[rows][:, :1])
    r.grad_sum[rows] = grad_sum
    grad_branch = grad_sum.astype(low)
    r.grad_branch[rows] = grad_branch
    add_to(r.small, BIAS_OUT, grad_branch.astype(wide))
    add_to(r.small, FINAL_GAIN, grad_out * normed)
    add_to(r.small, FINAL_BIAS, grad_out)


def inner_back(r, rows, index):
    width = r.grad_branch.shape[1]
    part = slice(index * width, (index + 1) * width)
    grad_active = matmul(r.grad_branch[rows], r.weight_out[part], 1, 1)
    grad_inner = grad_active * r.gelu_grad[rows, part].astype(wide)
    r.grad_inner[rows, part] = grad_inner.astype(low)
    add_to(r.small, BIAS_IN + index, grad_inner)


def input_back(r, rows):
    grad_hidden = r.grad_sum[rows] + matmul(r.grad_inner[rows], r.weight_in[...], 1, 1)
    normed = r.normed_one[rows]
    r.sum[rows] = norm_back(grad_hidden * r.mix_gain[...], normed, r.inverse_one[rows][:, :1])
    add_to(r.small, MIX_GAIN, grad_hidden * normed)
    add_to(r.small, MIX_BIAS, grad_hidden)


def spectra_back(r, put):
    seq_len, width = r.sum.shape
    half = width // 2

    def fold(rows, index):
        begin, end = r.sum[rows, :half], mirror(r.sum[rows, half:])
        lane = first_lane(begin)
        r.grad_seq[rows, :half] = jnp.where(lane, begin, begin + end).astype(low)
        r.grad_seq[rows, half:] = jnp.where(lane, end, begin - end).astype(low)

    each_block(seq_len, fold)

    def transform(rows, index):
        even = matmul(r.seq_mix[rows, :seq_len], r.grad_seq[:, : half + 128])
        odd = matmul(r.seq_mix[rows, seq_len:], r.grad_seq[:, half:])
        odd = jnp.where(first_lane(odd), even[:, half : half + 1], odd)
        r.spectra[rows, :half] = even[:, :half].astype(low)
        r.spectra[rows, half:] = odd.astype(low)
        put(rows, index, r.sum[rows] + matmul(r.spectra[rows], r.hidden_mix[...], 1, 1))

    each_block(seq_len, transform)


class Named:
    def __init__(self, refs):
        self.__dict__.update(refs)


class Order:
    last = None
    shares_vmem = False


order = Order()


def run_kernel(name, body, inputs, outputs, taken, scratch):
    if order.last is not None:
        inputs = {**inputs, n.after: (order.last, ANY)}
    outputs = {**outputs, n.turn: (jax.ShapeDtypeStruct((8, 128), wide), ANY)}
    n_in, n_out = len(inputs), len(outputs)
    names_in, names_out = list(inputs), list(outputs)

    held = sum(math.prod(shape) * np.dtype(dtype).itemsize for shape, dtype in scratch.values())
    for array, spec in (*inputs.values(), *outputs.values()):
        if spec is WHOLE:
            held += math.prod(array.shape) * np.dtype(array.dtype).itemsize

    def kernel(*refs):
        named = dict(zip(names_in, refs[:n_in]))
        for name, ref in zip(names_out, refs[n_in : n_in + n_out]):
            named[name] = ref
        named.update(zip(scratch, refs[n_in + n_out : -1]), place=place_of())
        body(Named(named), Copies(refs[-1]))

    results = pl.pallas_call(
        kernel,
        name=name,
        in_specs=[spec for _, spec in inputs.values()],
        out_shape=[jax.ShapeDtypeStruct(shape.shape, shape.dtype) for shape, _ in outputs.values()],
        out_specs=[spec for _, spec in outputs.values()],
        scratch_shapes=[
            *[pltpu.VMEM(*shape) for shape in scratch.values()],
            pltpu.SemaphoreType.DMA((48,)),
        ],
        input_output_aliases={names_in.index(name): names_out.index(name) for name in taken},
        compiler_params=pltpu.CompilerParams(
            vmem_limit_bytes=max(VMEM_SHARED, VMEM_SPARE + held) if order.shares_vmem else (VMEM_ALL if name == n.first_forward else VMEM_LATER)
        ),
        cost_estimate=pl.CostEstimate(flops=SHARE if order.shares_vmem else 1, bytes_accessed=1, transcendentals=0),
    )(*[array for array, _ in inputs.values()])
    results = dict(zip(names_out, results))
    order.last = results.pop(n.turn)
    return results


class Sections:
    def __init__(self, rows, sizes, tables, weights, vectors):
        self.rows, self.sizes = rows, sizes
        self.tables = dict(zip((n.mix_hbm, n.seq_hbm), tables))
        self.weights = dict(zip((n.in_hbm, n.out_hbm), weights))
        self.vectors = vectors
        self.kept = {}
        seq_len, width, inner = sizes
        self.shapes = {
            n.row: ((seq_len, width), low),
            n.cot: ((seq_len, width), low),
            n.hidden_mix: ((width, width), low),
            n.seq_mix: ((seq_len, 2 * seq_len), low),
            n.weight_in: ((width, inner), low),
            n.weight_out: ((inner, width), low),
            n.spectra: ((seq_len, width), low),
            n.sum: ((seq_len, width), wide),
            n.normed_one: ((seq_len, width), wide),
            n.inverse_one: ((seq_len, 128), wide),
            n.normed_two: ((seq_len, width), wide),
            n.inverse_two: ((seq_len, 128), wide),
            n.hidden_low: ((seq_len, width), low),
            n.active: ((seq_len, inner), low),
            n.gelu_grad: ((seq_len, inner), low),
            n.result: ((seq_len, width), low),
            n.grad_sum: ((seq_len, width), wide),
            n.grad_branch: ((seq_len, width), low),
            n.grad_inner: ((seq_len, inner), low),
            n.grad_seq: ((seq_len, width), low),
            n.grad_mixed: ((seq_len, width), wide),
            n.grad_low: ((seq_len, width), low),
            n.grad_wide: ((seq_len, width), wide),
        }
        self.small = jnp.zeros((32, width), wide)
        self.columns, self.stores = {}, {}
        for store, names in (
            (n.store_low, (n.active, n.gelu_grad, n.grad_inner, n.hidden_low, n.grad_branch)),
            (n.store_wide, (n.normed_one, n.normed_two, n.grad_sum, n.grad_mixed, n.inverse_one, n.inverse_two)),
        ):
            first = 0
            for name in names:
                (length, size), dtype = self.shapes[name]
                self.columns[name] = (store, first, size)
                first += size
            self.stores[store] = jax.ShapeDtypeStruct((rows * length, first), dtype)
        for store, dtype in ((n.layer_rows, low), (n.grad_rows, wide)):
            self.columns[store] = (store, None, None)
            self.stores[store] = jax.ShapeDtypeStruct((rows, seq_len, width), dtype)

    def stage(self, title, body, owner, inputs, made, reads, writes, scratch, uses_small=False):
        outputs = {name: (shape, ANY) for name, shape in made.items()}
        taken = []
        for store in dict.fromkeys(self.columns[name][0] for name in (*writes, *reads)):
            if store in self.kept:
                inputs[store] = (self.kept[store], ANY)
            if any(self.columns[name][0] == store for name in writes):
                if store in self.kept:
                    taken.append(store)
                outputs[store] = (self.stores[store], ANY)
        if uses_small:
            inputs[n.small_before] = (self.small, WHOLE)
            outputs[n.small] = (self.small, WHOLE)

        def kernel(refs, copies):
            for name in (*reads, *writes):
                store, first, size = self.columns[name]
                ref = getattr(refs, store)
                setattr(refs, name + n._kept, ref if size is None else ref.at[:, first : first + size])
            if uses_small:
                refs.small[...] = refs.small_before[...]
            pl.when(refs.place[0] == owner)(lambda: body(refs, copies))

        results = run_kernel(
            title, kernel, inputs, outputs, taken, {name: self.shapes[name] for name in scratch}
        )
        if uses_small:
            self.small = results.pop(n.small)
        for name in list(results):
            if name in self.stores:
                self.kept[name] = results.pop(name)
        return results

    def place(self, row):
        return pl.ds(row * self.sizes[0], self.sizes[0])

    def row_shape(self, dtype):
        return jax.ShapeDtypeStruct(self.sizes[:2], dtype)

    def any_inputs(self, arrays):
        return {name: (array, ANY) for name, array in arrays.items()}

    def vector_inputs(self):
        return {name: (array, WHOLE) for name, array in self.vectors.items()}

    def first_forward(self, row, activations, keeps, hands):
        keep = (n.gelu_grad, n.normed_one, n.inverse_one, n.normed_two, n.inverse_two, n.active, n.hidden_low)

        def body(r, copies):
            loads = forward_loads(r, copies, r.x_hbm.at[row])
            stores = []
            if hands:
                stores.append(copies.blocks(r.result, r.handed))
            if keeps:
                stores.append(copies.blocks(r.result, r.layer_rows.at[row]))
                for name in keep:
                    target = getattr(r, name + n._kept).at[self.place(row)]
                    stores.append(copies.blocks(getattr(r, name), target))

            def block(rows, index):
                forward_block(r, rows, index, *loads)
                at_block(index, stores, n.start)

            each_block(r.row.shape[0], block)
            wait_all(stores)

        inputs = {
            **self.any_inputs({n.x_hbm: activations, **self.tables, **self.weights}),
            **self.vector_inputs(),
        }
        return self.stage(
            n.first_forward,
            body,
            0,
            inputs,
            {n.handed: self.row_shape(low)} if hands else {},
            (),
            (*keep, n.layer_rows) if keeps else (),
            (n.row, n.hidden_mix, n.seq_mix, n.weight_in, n.weight_out, n.spectra, n.sum, n.result, *keep),
        ).get(n.handed)

    def later_both(self, row, handed, out_cotangent, lengths):
        keep = (n.active, n.hidden_low, n.grad_branch, n.grad_inner)

        def body(r, copies):
            loads = forward_loads(r, copies, r.x_hbm)
            cot_load = copies.start(r.cot_hbm.at[row], r.cot)
            filled = r.cot.shape[0] - r.lengths[row, r.lengths.shape[1] - 1]
            stores = [copies.blocks(r.result, r.layer_rows.at[row])]
            for name in keep:
                target = getattr(r, name + n._kept).at[self.place(row)]
                stores.append(copies.blocks(getattr(r, name), target))

            def block(rows, index):
                forward_block(r, rows, index, *loads)
                pl.when(index == 0)(cot_load.wait)
                token = rows.start + lax.broadcasted_iota(jnp.int32, (BLOCK, r.cot.shape[1]), 0)
                branch_back(r, rows, jnp.where(token < filled, r.cot[rows].astype(wide), 0.0))
                for part in range(r.weight_out.shape[0] // r.cot.shape[1]):
                    inner_back(r, rows, part)
                input_back(r, rows)
                at_block(index, stores, n.start)

            each_block(r.row.shape[0], block)
            results = [
                copies.blocks(r.grad_low, r.returned),
                copies.blocks(r.grad_wide, r.grad_rows.at[row]),
            ]

            def put(rows, index, values):
                r.grad_low[rows] = values.astype(low)
                r.grad_wide[rows] = r.grad_low[rows].astype(wide)
                at_block(index, results, n.start)

            spectra_back(r, put)
            wait_all(stores)
            wait_all(results)

        inputs = {
            n.lengths: (lengths, SCALARS),
            **self.any_inputs(
                {n.x_hbm: handed, n.cot_hbm: out_cotangent, **self.tables, **self.weights}
            ),
            **self.vector_inputs(),
        }
        return self.stage(
            n.later_both,
            body,
            1,
            inputs,
            {n.returned: self.row_shape(low)},
            (),
            (*keep, n.layer_rows, n.grad_rows),
            tuple(name for name in self.shapes if name != n.grad_mixed),
            True,
        )[n.returned]

    def first_back_branch(self, row, returned):
        keep = (n.grad_branch, n.grad_sum)
        need = (n.normed_two, n.inverse_two)

        def body(r, copies):
            loads = [copies.blocks(r.cot_hbm, r.cot)]
            for name in need:
                source = getattr(r, name + n._kept).at[self.place(row)]
                loads.append(copies.blocks(source, getattr(r, name)))
            stores = [
                copies.blocks(getattr(r, name), getattr(r, name + n._kept).at[self.place(row)])
                for name in keep
            ]
            for index in range(len(loads[0])):
                do_all(blocks[index].start for blocks in loads)

            def block(rows, index):
                at_block(index, loads, n.wait)
                branch_back(r, rows, r.cot[rows].astype(wide))
                at_block(index, stores, n.start)

            each_block(r.cot.shape[0], block)
            wait_all(stores)

        inputs = {
            **self.any_inputs({n.cot_hbm: returned}),
            n.final_gain: (self.vectors[n.final_gain], WHOLE),
        }
        self.stage(
            n.back_branch, body, 0, inputs, {}, need, keep, (n.cot, *need, *keep), True
        )

    def first_back_inner(self, row):
        need = (n.gelu_grad, n.grad_branch)

        def body(r, copies):
            rows = self.place(row)
            first = copies.start(r.grad_branch_kept.at[rows], r.grad_branch)
            width = r.grad_branch.shape[1]
            loads, stores = [], []
            for part in parts_of(r.grad_inner.shape[1], width):
                loads.append(
                    (
                        copies.start(r.out_hbm.at[0, part], r.weight_out.at[part]),
                        copies.start(r.gelu_grad_kept.at[rows, part], r.gelu_grad.at[:, part]),
                    )
                )
                stores.append(
                    copies.plan(r.grad_inner.at[:, part], r.grad_inner_kept.at[rows, part])
                )
            first.wait()

            def step(index, carry):
                for place, group in enumerate(loads):
                    pl.when(index == place)(functools.partial(do_all, [load.wait for load in group]))
                part = pl.ds(pl.multiple_of(index * width, width), width)
                grad_active = matmul(r.grad_branch[...], r.weight_out[part], 1, 1)
                grad_inner = grad_active * r.gelu_grad[:, part].astype(wide)
                r.grad_inner[:, part] = grad_inner.astype(low)
                r.small[pl.ds(BIAS_IN + index, 1)] += add_rows(grad_inner)
                for place, store in enumerate(stores):
                    pl.when(index == place)(store.start)
                return carry

            lax.fori_loop(0, len(loads), step, 0)
            for store in stores:
                store.wait()

        inputs = self.any_inputs({n.out_hbm: self.weights[n.out_hbm]})
        self.stage(
            n.back_inner, body, 0, inputs, {}, need, (n.grad_inner,), (n.weight_out, n.grad_inner, *need), True
        )

    def first_back_input(self, row):
        need = (n.grad_inner, n.grad_sum, n.normed_one, n.inverse_one)

        def body(r, copies):
            weight_load = copies.start(r.in_hbm.at[0], r.weight_in)
            loads = [
                copies.blocks(getattr(r, name + n._kept).at[self.place(row)], getattr(r, name))
                for name in need
            ]
            stores = [copies.blocks(r.sum, r.grad_mixed_kept.at[self.place(row)])]
            for index in range(len(loads[0])):
                do_all(blocks[index].start for blocks in loads)
            weight_load.wait()

            def block(rows, index):
                at_block(index, loads, n.wait)
                input_back(r, rows)
                at_block(index, stores, n.start)

            each_block(r.sum.shape[0], block)
            wait_all(stores)

        inputs = {
            **self.any_inputs({n.in_hbm: self.weights[n.in_hbm]}),
            n.mix_gain: (self.vectors[n.mix_gain], WHOLE),
        }
        self.stage(
            n.back_input, body, 0, inputs, {}, need, (n.grad_mixed,), (n.weight_in, n.sum, *need), True
        )

    def first_back_spectra(self, row):
        def body(r, copies):
            loads = [
                copies.start(r.grad_mixed_kept.at[self.place(row)], r.sum),
                copies.start(r.seq_hbm, r.seq_mix),
                copies.start(r.mix_hbm, r.hidden_mix),
            ]
            for load in loads:
                load.wait()

            stores = [copies.blocks(r.grad_wide, r.grad_rows.at[row])]

            def put(rows, index, values):
                r.grad_wide[rows] = values
                at_block(index, stores, n.start)

            spectra_back(r, put)
            wait_all(stores)

        self.stage(
            n.back_spectra,
            body,
            0,
            self.any_inputs(self.tables),
            {},
            (n.grad_mixed,),
            (n.grad_rows,),
            (n.hidden_mix, n.seq_mix, n.spectra, n.sum, n.grad_seq, n.grad_wide),
        )

    def weight_chunk(self, kind, first, size):
        seq_len, width, inner = self.sizes
        tokens = self.rows * seq_len
        left, right = ((n.active, n.grad_branch), (n.hidden_low, n.grad_inner))[kind]
        height, columns = ((size, width), (width, size))[kind]
        half, quarter = height // 2, height // 4
        length = (quarter, half)[kind]
        wide_part = (columns, columns // 2)[kind]

        def body(r, copies):
            cores = (1 - r.place[1], r.place[1])
            left_first = self.columns[left][1] + (first if kind == 0 else 0)
            right_first = self.columns[right][1] + (first if kind == 1 else 0)
            rights, lefts = [], []
            for k in range(columns // wide_part):
                part = slice(k * wide_part, (k + 1) * wide_part)
                source = r.store.at[:, pl.ds(right_first + k * wide_part, wide_part)]
                rights.append(copies.plan(source, r.right.at[:, part]))
            for k in range(height // length):
                steps_of_core = half // length
                begin = left_first + cores[k // steps_of_core] * half + (k % steps_of_core) * length
                source = r.store.at[:, pl.ds(pl.multiple_of(begin, 128), length)]
                lefts.append(copies.plan(source, r.left.at[k]))
            targets = (
                r.others_first,
                r.others_second,
                r.own.at[:quarter],
                r.own.at[quarter:],
            )
            if kind == 0:
                loads = ((rights[0], lefts[0]), (lefts[1],), (lefts[2],), (lefts[3],))
                outs = [(copies.plan(r.total.at[k], targets[k]),) for k in range(4)]
            else:
                loads = ((rights[0], lefts[0]), (lefts[1],), (rights[1],), ())
                pairs = [
                    [
                        copies.plan(r.total.at[k, piece * quarter : (piece + 1) * quarter], targets[2 * k + piece])
                        for piece in range(2)
                    ]
                    for k in range(2)
                ]
                outs = ((), (), pairs[0], pairs[1])
            do_all(load.start for group in loads for load in group)

            def step(index, carry):
                for place, group in enumerate(loads):
                    pl.when(index == place)(functools.partial(do_all, [load.wait for load in group]))
                if kind == 0:
                    r.total[index] = matmul(r.left[index], r.right[...], 0, 0).astype(low)
                else:
                    k = index % 2
                    part = pl.ds(pl.multiple_of(index // 2 * wide_part, wide_part), wide_part)
                    r.total[k, :, part] = matmul(r.left[k], r.right[:, part], 0, 0).astype(low)
                for place, group in enumerate(outs):
                    pl.when(index == place)(functools.partial(do_all, [out.start for out in group]))
                return carry

            lax.fori_loop(0, 4, step, 0)
            do_all(out.wait for group in outs for out in group)

        shape = jax.ShapeDtypeStruct((quarter, columns), low)
        results = run_kernel(
            n.product,
            body,
            {n.store: (self.kept[n.store_low], ANY)},
            {
                n.own: (jax.ShapeDtypeStruct((half, columns), low), ANY),
                n.others_first: (shape, ANY),
                n.others_second: (shape, ANY),
            },
            (),
            {
                n.left: ((height // length, tokens, length), low),
                n.right: ((tokens, columns), low),
                n.total: ((height // length, length, columns), low),
            },
        )
        return results[n.own], results[n.others_first], results[n.others_second]

    def others_back_spectra(self, row):
        for earlier in range(row):
            self.first_back_spectra(earlier)


def parts_of(inner, width):
    return [slice(first, first + width) for first in range(0, inner, width)]


def forward_loads(r, copies, x_hbm):
    x_load = copies.start(x_hbm, r.row)
    mix_load = copies.start(r.mix_hbm, r.hidden_mix)
    x_load.wait()
    mix_load.wait()
    seq_load = copies.start(r.seq_hbm, r.seq_mix)
    in_load = copies.start(r.in_hbm.at[0], r.weight_in)
    out_load = copies.start(r.out_hbm.at[0], r.weight_out)

    def transform(rows, index):
        r.spectra[rows] = matmul(r.row[rows], r.hidden_mix[...]).astype(low)

    each_block(r.row.shape[0], transform)
    seq_load.wait()
    return in_load, out_load


def exchange(block, distance):
    devices = range(lax.axis_size("dp"))
    return lax.ppermute(block, "dp", [(i, i ^ distance) for i in devices])


def along_line(block, steps):
    route = [(a * 4 + j, b * 4 + j) for a, b in steps for j in range(4)]
    return lax.ppermute(block, "dp", route)


def low_sum(first, second):
    return (first[...].astype(wide) + second[...].astype(wide)).astype(low)


class Sum:
    def __init__(self, make, small):
        self.make, self.small = make, small

    def kernel(self, title, body, shapes, **come):
        results = run_kernel(
            title,
            body,
            {
                n.own: (self.own, WHOLE),
                **{name: (array, WHOLE) for name, array in come.items()},
            },
            {name: (jax.ShapeDtypeStruct(shape, low), WHOLE) for name, shape in shapes.items()},
            (),
            {},
        )
        return [results[name] for name in shapes]

    def add(self):
        def body(r, copies):
            r.total[...] = low_sum(r.own, r.come)

        (self.own,) = self.kernel(n.add, body, {n.total: self.own.shape}, come=self.come)

    def core(self):
        self.own, first, second = self.make()
        self.come = exchange(first, 1), exchange(second, 1)

    def pair(self):
        rows, columns = self.own.shape
        half = rows // 2
        first, second = self.come
        come = {n.first: first, n.second: second}
        small = self.small()
        extra = 0
        if small is not None:
            come[n.small] = small
            extra = small.shape[0] // 2

        def body(r, copies):
            @pl.when(r.place[2] == 0)
            def keep_first():
                r.kept[:half] = low_sum(r.own.at[:half], r.first)
                r.other[:half] = low_sum(r.own.at[half:], r.second)

            @pl.when(r.place[2] == 1)
            def keep_second():
                r.other[:half] = low_sum(r.own.at[:half], r.first)
                r.kept[:half] = low_sum(r.own.at[half:], r.second)

            if extra:
                for target, pair in ((r.kept, r.place[2]), (r.other, 1 - r.place[2])):
                    rows = pl.ds(pl.multiple_of(pair * extra, extra), extra)
                    target[half:, : r.small.shape[1]] = r.small[rows, :].astype(low)

        shapes = {n.kept: (half + extra, columns), n.other: (half + extra, columns)}
        self.own, other = self.kernel(n.pair, body, shapes, **come)
        self.come = exchange(other, 2)

    def inward(self):
        self.add()
        line = lax.axis_size("dp") // 4
        if line == 4:
            self.come = along_line(self.own, [(0, 1), (3, 2)])
            return
        distance = 4
        while distance < 4 * line:
            self.come = exchange(self.own, distance)
            distance *= 2
            if distance < 4 * line:
                self.add()

    def middle(self):
        self.add()
        if lax.axis_size("dp") == 16:
            self.come = along_line(self.own, [(1, 2), (2, 1)])

    def outward(self):
        if lax.axis_size("dp") == 16:
            self.add()
            self.come = along_line(self.own, [(1, 0), (2, 3)])

    def pair_back(self):
        if lax.axis_size("dp") == 16:

            def body(r, copies):
                r.total[...] = jnp.where(r.place[3] == 1, r.own[...], r.come[...])

            (self.own,) = self.kernel(n.take, body, {n.total: self.own.shape}, come=self.come)
        self.come = exchange(self.own, 2)

    def core_back(self):
        def body(r, copies):
            r.pair_part[...] = r.come[...]

        (self.pair_part,) = self.kernel(n.join, body, {n.pair_part: self.own.shape}, come=self.come)
        self.come = exchange(self.own, 1), exchange(self.pair_part, 1)

    def finish(self, target, shape, kind, first, size, extra):
        rows, columns = self.own.shape
        length = rows - extra

        def body(r, copies):
            stores = []
            parts = (r.own, r.pair_part, r.core_own, r.core_pair)
            for index, part in enumerate(parts):
                core = r.place[1] if index < 2 else 1 - r.place[1]
                pair = r.place[2] if index % 2 == 0 else 1 - r.place[2]
                quarter = 2 * core + pair
                r.full[index] = part[:length].astype(wide)
                rows_at = pl.ds(pl.multiple_of(quarter * length + (first if kind == 0 else 0), 16), length)
                where = (0, rows_at) if kind == 0 else (0, rows_at, pl.ds(first, size))
                stores.append(copies.start(r.full.at[index], r.target.at[where]))
            if extra:
                for index in range(2):
                    pair = r.place[2] if index == 0 else 1 - r.place[2]
                    to = pl.ds(pl.multiple_of(pair * extra, extra), extra)
                    total = parts[index][length:, :].astype(wide) + parts[index + 2][length:, :].astype(wide)
                    r.small[to, :] = total[:, : r.small.shape[1]]
            for store in stores:
                store.wait()

        inputs = {
            n.own: (self.own, WHOLE),
            n.pair_part: (self.pair_part, WHOLE),
            n.core_own: (self.come[0], WHOLE),
            n.core_pair: (self.come[1], WHOLE),
        }
        if target is not None:
            inputs[n.target] = (target, ANY)
        outputs = {n.target: (jax.ShapeDtypeStruct(shape, wide), ANY)}
        if extra:
            outputs[n.small] = (jax.ShapeDtypeStruct((2 * extra, shape[1 + (1 - kind)] if kind else columns), wide), WHOLE)
        results = run_kernel(
            n.finish,
            body,
            inputs,
            outputs,
            (n.target,) if target is not None else (),
            {n.full: ((4, length, columns), wide)},
        )
        return results[n.target], results.get(n.small)


CHUNKS = ((0, 6), (0, 6), (1, 6), (1, 6))
STEPS = (
    (1, n.core),
    (0, n.core),
    (1, n.pair),
    (None, n.first_back_inner),
    (2, n.core),
    (0, n.pair),
    (1, n.inward),
    (None, n.first_back_input),
    (3, n.core),
    (2, n.pair),
    (0, n.inward),
    (1, n.middle),
    (3, n.pair),
    (2, n.inward),
    (0, n.middle),
    (1, n.outward),
    (3, n.inward),
    (2, n.middle),
    (0, n.outward),
    (1, n.pair_back),
    (None, n.first_back_spectra),
    (3, n.middle),
    (2, n.outward),
    (1, n.core_back),
    (0, n.pair_back),
    (3, n.outward),
    (2, n.pair_back),
    (1, n.finish),
    (None, n.others_back_spectra),
    (0, n.core_back),
    (3, n.pair_back),
    (2, n.core_back),
    (0, n.finish),
    (3, n.core_back),
    (2, n.finish),
    (3, n.finish),
)


def per_device(
    activations,
    out_cotangent,
    doc_lengths,
    mix_gain,
    mix_bias,
    weight_in,
    bias_in,
    weight_out,
    bias_out,
    final_gain,
    final_bias,
):
    rows, seq_len, width = activations.shape
    inner = weight_in.shape[2]
    order.last, order.shares_vmem = None, False
    tables = make_tables(width, seq_len)
    vectors = {
        n.mix_gain: mix_gain,
        n.mix_bias: mix_bias,
        n.bias_in: bias_in,
        n.bias_out: bias_out,
        n.final_gain: final_gain,
        n.final_bias: final_bias,
    }
    work = Sections(rows, (seq_len, width, inner), tables, (weight_in, weight_out), vectors)
    handed = []
    for row in range(rows):
        result = work.first_forward(row, activations, row == rows - 1, True)
        handed.append(from_behind(result, "pipe", 1))
    for row in range(rows - 1):
        work.first_forward(row, activations, True, False)
    returned = []
    for row in range(rows):
        result = work.later_both(row, handed[row], out_cotangent, doc_lengths)
        returned.append(from_behind(result, "pipe", -1))
    for row in range(rows):
        work.first_back_branch(row, returned[row])
        if row < rows - 1:
            work.first_back_inner(row)
            work.first_back_input(row)
    order.shares_vmem = True
    sums, first = [], [0, 0]
    for kind, units in CHUNKS:
        size = units * inner // 12
        last = len(sums) == len(CHUNKS) - 1
        make = functools.partial(work.weight_chunk, kind, first[kind], size)
        small_of = functools.partial(getattr, work, n.small) if last else nothing
        sums.append((Sum(make, small_of), kind, first[kind], size, 16 if last else 0))
        first[kind] += size
    shapes, targets = (weight_out.shape, weight_in.shape), [None, None]
    for index, step in STEPS:
        if index is None:
            getattr(work, step)(rows - 1)
        elif step == n.finish:
            chunk, kind, *rest = sums[index]
            targets[kind], small = chunk.finish(targets[kind], shapes[kind], kind, *rest)
        else:
            getattr(sums[index][0], step)()
    return (
        work.kept[n.layer_rows][None],
        work.kept[n.grad_rows][None],
        small[MIX_GAIN, :width][None],
        small[MIX_BIAS, :width][None],
        targets[1],
        small[BIAS_IN : BIAS_IN + inner // width, :width].reshape(1, inner),
        targets[0],
        small[BIAS_OUT, :width][None],
        small[FINAL_GAIN, :width][None],
        small[FINAL_BIAS, :width][None],
    )


def solution(mesh):
    placed = (
        P("dp", None, None),
        P("dp", None, None),
        P("dp", None),
        P("pipe", None),
        P("pipe", None),
        P("pipe", None, None),
        P("pipe", None),
        P("pipe", None, None),
        P("pipe", None),
        P("pipe", None),
        P("pipe", None),
    )
    return jax.shard_map(
        per_device,
        mesh=mesh,
        in_specs=placed,
        out_specs=(
            P("pipe", "dp", None, None),
            P("pipe", "dp", None, None),
            P("pipe", None),
            P("pipe", None),
            P("pipe", None, None),
            P("pipe", None),
            P("pipe", None, None),
            P("pipe", None),
            P("pipe", None),
            P("pipe", None),
        ),
        check_vma=False,
    )
```

```python
import functools
import math

import jax
import jax.numpy as jnp
import numpy as np
from jax import lax
from jax.experimental import pallas as pl
from jax.experimental.pallas import tpu as pltpu
from jax.sharding import PartitionSpec as P

eps_norm = 1e-06
low, wide = jnp.bfloat16, jnp.float32
slope = math.sqrt(2.0 / math.pi)
cubic = 0.044715
VMEM_SPARE = 6 * 2**20
SHARE = 800000000
SHARE = 800000000
LONG = 6000000000
VMEM_SHARED = 44 * 2**20
VMEM_ALL = 62 * 2**20
VMEM_LATER = 50 * 2**20
BLOCK = 256
ANY = pl.BlockSpec(memory_space=pltpu.HBM)
SCALARS = pl.BlockSpec(memory_space=pltpu.SMEM)
WHOLE = pl.BlockSpec(memory_space=pltpu.VMEM)

MIX_GAIN, MIX_BIAS, BIAS_OUT, FINAL_GAIN, FINAL_BIAS, BIAS_IN = 0, 1, 2, 3, 4, 16


class Names:
    def __getattr__(self, name):
        return name


n = Names()


def from_behind(block, axis, distance):
    devices = range(lax.axis_size(axis))
    route = [(i - distance, i) for i in devices if i - distance in devices]
    return lax.ppermute(block, axis, route)


def dft_tables(table_len):
    indices = np.arange(table_len)
    angles = (indices[:, None] * indices[None, :] % table_len) * (2.0 * math.pi / table_len)
    scaled = 1.0 / math.sqrt(table_len)
    return (np.cos(angles) * scaled, np.sin(angles) * scaled)


def make_tables(width, seq_len):
    half = width // 2
    hid_cos, hid_sin = dft_tables(width)
    seq_cos, seq_sin = dft_tables(seq_len)
    hidden_mix = np.concatenate([hid_cos[:, : half + 1], hid_sin[:, 1:half]], axis=1)
    seq_mix = np.concatenate([seq_cos, -seq_sin], axis=1)
    return jnp.asarray(hidden_mix, low), jnp.asarray(seq_mix, low)


def matmul(left, right, left_dim=1, right_dim=0):
    return lax.dot_general(
        left, right, (((left_dim,), (right_dim,)), ((), ())), preferred_element_type=wide
    )


def mean_last(values):
    return jnp.mean(values, axis=-1, keepdims=True)


def normalize(values):
    centred = values - mean_last(values)
    inverse = lax.rsqrt(mean_last(centred * centred) + eps_norm)
    return (centred * inverse, inverse)


def norm_back(grad_norm, normed, inverse):
    return inverse * (grad_norm - mean_last(grad_norm) - normed * mean_last(grad_norm * normed))


def gelu_parts(values):
    square = values * values
    part = 0.5 + 0.5 * jnp.tanh(values * (slope + slope * cubic * square))
    active = values * part
    step = 2.0 * slope + 6.0 * slope * cubic * square
    return (active, part + active * (1.0 - part) * step)


def nothing():
    pass


def place_of():
    index = lax.axis_index("dp")
    line = index // 4
    inside = jnp.where((line == 1) | (line == 2), 1, 0)
    return lax.axis_index("pipe"), index % 2, index // 2 % 2, inside


def each_block(seq_len, body):
    def step(index, carry):
        body(pl.ds(pl.multiple_of(index * BLOCK, BLOCK), BLOCK), index)
        return carry

    lax.fori_loop(0, seq_len // BLOCK, step, 0)


def at_block(index, plans, call):
    for place in range(len(plans[0])):
        calls = [getattr(blocks[place], call) for blocks in plans]
        pl.when(index == place)(functools.partial(do_all, calls))


def wait_all(plans):
    do_all(copy.wait for blocks in plans for copy in blocks)


def add_rows(values):
    return jnp.sum(values, axis=0, keepdims=True)


class Copy:
    def __init__(self, source, target, sem):
        self.parts = source, target, sem

    def start(self):
        pltpu.make_async_copy(*self.parts).start()

    def wait(self):
        pltpu.make_async_copy(*self.parts).wait()


class Copies:
    def __init__(self, sems):
        self.sems, self.used = sems, 0

    def plan(self, source, target):
        self.used += 1
        return Copy(source, target, self.sems.at[self.used - 1])

    def blocks(self, source, target):
        parts = [slice(first, first + BLOCK) for first in range(0, target.shape[0], BLOCK)]
        return [self.plan(source.at[part], target.at[part]) for part in parts]

    def start(self, source, target):
        copy = self.plan(source, target)
        copy.start()
        return copy


def do_all(calls):
    for call in calls:
        call()


def add_to(small, place, values):
    small[place : place + 1] += add_rows(values)


def first_lane(values):
    return lax.broadcasted_iota(jnp.int32, values.shape, 1) == 0


def mirror(values):
    groups = values.shape[1] // 128
    parts = [values[:, 128 * g : 128 * (g + 1)] for g in range(groups)]
    lane = lax.broadcasted_iota(jnp.int32, parts[0].shape, 1)
    turned = [jnp.take_along_axis(part, lax.rem(128 - lane, 128), axis=1) for part in parts]
    mirrored = [
        jnp.where(lane == 0, turned[-g % groups], turned[groups - 1 - g]) for g in range(groups)
    ]
    return jnp.concatenate(mirrored, axis=1)


def mixed_rows(r, rows):
    seq_len, width = r.spectra.shape
    half = width // 2
    even = matmul(r.seq_mix[rows, :seq_len], r.spectra[:, : half + 128])
    odd = matmul(r.seq_mix[rows, seq_len:], r.spectra[:, half:])
    middle = even[:, half : half + 1]
    even = even[:, :half]
    odd = jnp.where(first_lane(odd), 0.0, odd)
    later = mirror(even - odd)
    return even + odd, jnp.where(first_lane(later), middle, later)


def forward_block(r, rows, index, in_load, out_load):
    width = r.row.shape[1]
    half = width // 2
    begin, end = mixed_rows(r, rows)
    r.sum[rows, :half] = r.row[rows, :half].astype(wide) + begin
    r.sum[rows, half:] = r.row[rows, half:].astype(wide) + end
    normed, inverse = normalize(r.sum[rows])
    r.normed_one[rows] = normed
    r.inverse_one[rows] = jnp.broadcast_to(inverse, (BLOCK, 128))
    r.hidden_low[rows] = (normed * r.mix_gain[...] + r.mix_bias[...]).astype(low)
    pl.when(index == 0)(in_load.wait)
    for part in parts_of(r.weight_in.shape[1], width):
        inner = matmul(r.hidden_low[rows], r.weight_in[:, part]) + r.bias_in[:, part]
        active, gelu_grad = gelu_parts(inner)
        active = active.astype(low)
        r.active[rows, part] = active
        r.gelu_grad[rows, part] = gelu_grad.astype(low)
        if part.start == 0:
            pl.when(index == 0)(out_load.wait)
            r.sum[rows] = matmul(active, r.weight_out[part])
        else:
            r.sum[rows] += matmul(active, r.weight_out[part])
    hidden = r.normed_one[rows] * r.mix_gain[...] + r.mix_bias[...]
    normed, inverse = normalize(hidden + r.sum[rows] + r.bias_out[...])
    r.normed_two[rows] = normed
    r.inverse_two[rows] = jnp.broadcast_to(inverse, (BLOCK, 128))
    r.result[rows] = (normed * r.final_gain[...] + r.final_bias[...]).astype(low)


def branch_back(r, rows, grad_out):
    normed = r.normed_two[rows]
    grad_sum = norm_back(grad_out * r.final_gain[...], normed, r.inverse_two[rows][:, :1])
    r.grad_sum[rows] = grad_sum
    grad_branch = grad_sum.astype(low)
    r.grad_branch[rows] = grad_branch
    add_to(r.small, BIAS_OUT, grad_branch.astype(wide))
    add_to(r.small, FINAL_GAIN, grad_out * normed)
    add_to(r.small, FINAL_BIAS, grad_out)


def inner_back(r, rows, index):
    width = r.grad_branch.shape[1]
    part = slice(index * width, (index + 1) * width)
    grad_active = matmul(r.grad_branch[rows], r.weight_out[part], 1, 1)
    grad_inner = grad_active * r.gelu_grad[rows, part].astype(wide)
    r.grad_inner[rows, part] = grad_inner.astype(low)
    add_to(r.small, BIAS_IN + index, grad_inner)


def input_back(r, rows):
    grad_hidden = r.grad_sum[rows] + matmul(r.grad_inner[rows], r.weight_in[...], 1, 1)
    normed = r.normed_one[rows]
    r.sum[rows] = norm_back(grad_hidden * r.mix_gain[...], normed, r.inverse_one[rows][:, :1])
    add_to(r.small, MIX_GAIN, grad_hidden * normed)
    add_to(r.small, MIX_BIAS, grad_hidden)


def spectra_back(r, put):
    seq_len, width = r.sum.shape
    half = width // 2

    def fold(rows, index):
        begin, end = r.sum[rows, :half], mirror(r.sum[rows, half:])
        lane = first_lane(begin)
        r.grad_seq[rows, :half] = jnp.where(lane, begin, begin + end).astype(low)
        r.grad_seq[rows, half:] = jnp.where(lane, end, begin - end).astype(low)

    each_block(seq_len, fold)

    def transform(rows, index):
        even = matmul(r.seq_mix[rows, :seq_len], r.grad_seq[:, : half + 128])
        odd = matmul(r.seq_mix[rows, seq_len:], r.grad_seq[:, half:])
        odd = jnp.where(first_lane(odd), even[:, half : half + 1], odd)
        r.spectra[rows, :half] = even[:, :half].astype(low)
        r.spectra[rows, half:] = odd.astype(low)
        put(rows, index, r.sum[rows] + matmul(r.spectra[rows], r.hidden_mix[...], 1, 1))

    each_block(seq_len, transform)


class Named:
    def __init__(self, refs):
        self.__dict__.update(refs)


class Order:
    last = None
    shares_vmem = False


order = Order()


def run_kernel(name, body, inputs, outputs, taken, scratch):
    if order.last is not None:
        inputs = {**inputs, n.after: (order.last, ANY)}
    outputs = {**outputs, n.turn: (jax.ShapeDtypeStruct((8, 128), wide), ANY)}
    n_in, n_out = len(inputs), len(outputs)
    names_in, names_out = list(inputs), list(outputs)

    held = sum(math.prod(shape) * np.dtype(dtype).itemsize for shape, dtype in scratch.values())
    for array, spec in (*inputs.values(), *outputs.values()):
        if spec is WHOLE:
            held += math.prod(array.shape) * np.dtype(array.dtype).itemsize

    def kernel(*refs):
        named = dict(zip(names_in, refs[:n_in]))
        for name, ref in zip(names_out, refs[n_in : n_in + n_out]):
            named[name] = ref
        named.update(zip(scratch, refs[n_in + n_out : -1]), place=place_of())
        body(Named(named), Copies(refs[-1]))

    results = pl.pallas_call(
        kernel,
        name=name,
        in_specs=[spec for _, spec in inputs.values()],
        out_shape=[jax.ShapeDtypeStruct(shape.shape, shape.dtype) for shape, _ in outputs.values()],
        out_specs=[spec for _, spec in outputs.values()],
        scratch_shapes=[
            *[pltpu.VMEM(*shape) for shape in scratch.values()],
            pltpu.SemaphoreType.DMA((48,)),
        ],
        input_output_aliases={names_in.index(name): names_out.index(name) for name in taken},
        compiler_params=pltpu.CompilerParams(
            vmem_limit_bytes=max(VMEM_SHARED, VMEM_SPARE + held) if order.shares_vmem else (VMEM_ALL if name == n.first_forward else VMEM_LATER)
        ),
        cost_estimate=pl.CostEstimate(flops=SHARE if order.shares_vmem else (LONG if name == n.later_first else 1), bytes_accessed=1, transcendentals=0),
    )(*[array for array, _ in inputs.values()])
    results = dict(zip(names_out, results))
    order.last = results.pop(n.turn)
    return results


class Sections:
    def __init__(self, rows, sizes, tables, weights, vectors):
        self.rows, self.sizes = rows, sizes
        self.tables = dict(zip((n.mix_hbm, n.seq_hbm), tables))
        self.weights = dict(zip((n.in_hbm, n.out_hbm), weights))
        self.vectors = vectors
        self.kept = {}
        seq_len, width, inner = sizes
        self.shapes = {
            n.row: ((seq_len, width), low),
            n.cot: ((seq_len, width), low),
            n.hidden_mix: ((width, width), low),
            n.seq_mix: ((seq_len, 2 * seq_len), low),
            n.weight_in: ((width, inner), low),
            n.weight_out: ((inner, width), low),
            n.spectra: ((seq_len, width), low),
            n.sum: ((seq_len, width), wide),
            n.normed_one: ((seq_len, width), wide),
            n.inverse_one: ((seq_len, 128), wide),
            n.normed_two: ((seq_len, width), wide),
            n.inverse_two: ((seq_len, 128), wide),
            n.hidden_low: ((seq_len, width), low),
            n.active: ((seq_len, inner), low),
            n.gelu_grad: ((seq_len, inner), low),
            n.result: ((seq_len, width), low),
            n.grad_sum: ((seq_len, width), wide),
            n.grad_branch: ((seq_len, width), low),
            n.grad_inner: ((seq_len, inner), low),
            n.grad_seq: ((seq_len, width), low),
            n.grad_mixed: ((seq_len, width), wide),
            n.grad_low: ((seq_len, width), low),
            n.grad_wide: ((seq_len, width), wide),
        }
        self.small = None
        self.columns, self.stores = {}, {}
        for store, names in (
            (n.store_low, (n.active, n.gelu_grad, n.grad_inner, n.hidden_low, n.grad_branch)),
            (n.store_wide, (n.normed_one, n.normed_two, n.grad_sum, n.grad_mixed, n.inverse_one, n.inverse_two)),
        ):
            first = 0
            for name in names:
                (length, size), dtype = self.shapes[name]
                self.columns[name] = (store, first, size)
                first += size
            self.stores[store] = jax.ShapeDtypeStruct((rows * length, first), dtype)
        for store, dtype in ((n.layer_rows, low), (n.grad_rows, wide)):
            self.columns[store] = (store, None, None)
            self.stores[store] = jax.ShapeDtypeStruct((rows, seq_len, width), dtype)

    def stage(self, title, body, owner, inputs, made, reads, writes, scratch, uses_small=False):
        outputs = {name: (shape, ANY) for name, shape in made.items()}
        taken = []
        for store in dict.fromkeys(self.columns[name][0] for name in (*writes, *reads)):
            if store in self.kept:
                inputs[store] = (self.kept[store], ANY)
            if any(self.columns[name][0] == store for name in writes):
                if store in self.kept:
                    taken.append(store)
                outputs[store] = (self.stores[store], ANY)
        if uses_small:
            if self.small is not None:
                inputs[n.small_before] = (self.small, WHOLE)
            outputs[n.small] = (jax.ShapeDtypeStruct((32, self.sizes[1]), wide), WHOLE)

        def kernel(refs, copies):
            for name in (*reads, *writes):
                store, first, size = self.columns[name]
                ref = getattr(refs, store)
                setattr(refs, name + n._kept, ref if size is None else ref.at[:, first : first + size])
            if uses_small:
                before = getattr(refs, n.small_before, None)
                refs.small[...] = jnp.zeros_like(refs.small) if before is None else before[...]
            pl.when(refs.place[0] == owner)(lambda: body(refs, copies))

        results = run_kernel(
            title, kernel, inputs, outputs, taken, {name: self.shapes[name] for name in scratch}
        )
        if uses_small:
            self.small = results.pop(n.small)
        for name in list(results):
            if name in self.stores:
                self.kept[name] = results.pop(name)
        return results

    def place(self, row):
        return pl.ds(row * self.sizes[0], self.sizes[0])

    def row_shape(self, dtype):
        return jax.ShapeDtypeStruct(self.sizes[:2], dtype)

    def any_inputs(self, arrays):
        return {name: (array, ANY) for name, array in arrays.items()}

    def vector_inputs(self):
        return {name: (array, WHOLE) for name, array in self.vectors.items()}

    def first_forward(self, row, activations, keeps, hands):
        keep = (n.gelu_grad, n.normed_one, n.inverse_one, n.normed_two, n.inverse_two, n.active, n.hidden_low)

        def body(r, copies):
            loads = forward_loads(r, copies, r.x_hbm.at[row])
            stores = []
            if hands:
                stores.append(copies.blocks(r.result, r.handed))
            if keeps:
                stores.append(copies.blocks(r.result, r.layer_rows.at[row]))
                for name in keep:
                    target = getattr(r, name + n._kept).at[self.place(row)]
                    stores.append(copies.blocks(getattr(r, name), target))

            def block(rows, index):
                forward_block(r, rows, index, *loads)
                at_block(index, stores, n.start)

            each_block(r.row.shape[0], block)
            wait_all(stores)

        inputs = {
            **self.any_inputs({n.x_hbm: activations, **self.tables, **self.weights}),
            **self.vector_inputs(),
        }
        return self.stage(
            n.first_forward if hands else n.again_forward,
            body,
            0,
            inputs,
            {n.handed: self.row_shape(low)} if hands else {},
            (),
            (*keep, n.layer_rows) if keeps else (),
            (n.row, n.hidden_mix, n.seq_mix, n.weight_in, n.weight_out, n.spectra, n.sum, n.result, *keep),
        ).get(n.handed)

    def first_part(self, row, activations, block, spectra):
        fresh = spectra is None
        names = (n.row, n.hidden_mix, n.seq_mix, n.weight_in, n.weight_out, n.spectra, n.sum, n.result, n.normed_one,
                 n.inverse_one, n.normed_two, n.inverse_two, n.hidden_low, n.active, n.gelu_grad)

        def body(r, copies):
            stores = []
            if fresh:
                loads = forward_loads(r, copies, r.x_hbm.at[row])
                stores.append(copies.start(r.spectra, r.spectra_out))
            else:
                firsts = [
                    copies.start(r.x_hbm.at[row], r.row),
                    copies.start(r.spectra_in, r.spectra),
                    copies.start(r.seq_hbm, r.seq_mix),
                ]
                loads = (
                    copies.start(r.in_hbm.at[0], r.weight_in),
                    copies.start(r.out_hbm.at[0], r.weight_out),
                )
                do_all(first.wait for first in firsts)
            rows = slice(block * BLOCK, (block + 1) * BLOCK)
            forward_block(r, rows, 0, *loads)
            stores.append(copies.start(r.result.at[rows], r.handed.at[:BLOCK]))
            do_all(store.wait for store in stores)

        inputs = {
            **self.any_inputs({n.x_hbm: activations, **self.tables, **self.weights}),
            **self.vector_inputs(),
        }
        if not fresh:
            inputs[n.spectra_in] = (spectra, ANY)
        width = self.sizes[1]
        made = {n.handed: jax.ShapeDtypeStruct((BLOCK + (16 if fresh else 0), width), low)}
        if fresh:
            made[n.spectra_out] = jax.ShapeDtypeStruct(self.sizes[:2], low)
        results = self.stage(n.first_forward, body, 0, inputs, made, (), (), names)
        return results[n.handed], results.get(n.spectra_out)

    def later_both(self, row, handed, out_cotangent, lengths):
        pieces = {n.x_hbm + str(place): piece for place, piece in enumerate(handed)}
        keep = (n.active, n.hidden_low, n.grad_branch, n.grad_inner)

        def body(r, copies):
            loads = forward_loads(r, copies, *[getattr(r, name) for name in pieces])
            cot_load = copies.start(r.cot_hbm.at[row], r.cot)
            filled = r.cot.shape[0] - r.lengths[row, r.lengths.shape[1] - 1]
            stores = [copies.blocks(r.result, r.layer_rows.at[row])]
            for name in keep:
                target = getattr(r, name + n._kept).at[self.place(row)]
                stores.append(copies.blocks(getattr(r, name), target))

            def block(rows, index):
                forward_block(r, rows, index, *loads)
                pl.when(index == 0)(cot_load.wait)
                token = rows.start + lax.broadcasted_iota(jnp.int32, (BLOCK, r.cot.shape[1]), 0)
                branch_back(r, rows, jnp.where(token < filled, r.cot[rows].astype(wide), 0.0))
                for part in range(r.weight_out.shape[0] // r.cot.shape[1]):
                    inner_back(r, rows, part)
                input_back(r, rows)
                at_block(index, stores, n.start)

            each_block(r.row.shape[0], block)
            results = [
                copies.blocks(r.grad_low, r.returned),
                copies.blocks(r.grad_wide, r.grad_rows.at[row]),
            ]

            def put(rows, index, values):
                r.grad_low[rows] = values.astype(low)
                r.grad_wide[rows] = r.grad_low[rows].astype(wide)
                at_block(index, results, n.start)

            spectra_back(r, put)
            wait_all(stores)
            wait_all(results)

        inputs = {
            n.lengths: (lengths, SCALARS),
            **self.any_inputs(pieces),
            **self.any_inputs({n.cot_hbm: out_cotangent, **self.tables, **self.weights}),
            **self.vector_inputs(),
        }
        return self.stage(
            n.later_first if row == 0 else n.later_both,
            body,
            1,
            inputs,
            {n.returned: self.row_shape(low)},
            (),
            (*keep, n.layer_rows, n.grad_rows),
            tuple(name for name in self.shapes if name != n.grad_mixed),
            True,
        )[n.returned]

    def first_back_branch(self, row, returned):
        keep = (n.grad_branch, n.grad_sum)
        need = (n.normed_two, n.inverse_two)

        def body(r, copies):
            loads = [copies.blocks(r.cot_hbm, r.cot)]
            for name in need:
                source = getattr(r, name + n._kept).at[self.place(row)]
                loads.append(copies.blocks(source, getattr(r, name)))
            stores = [
                copies.blocks(getattr(r, name), getattr(r, name + n._kept).at[self.place(row)])
                for name in keep
            ]
            for index in range(len(loads[0])):
                do_all(blocks[index].start for blocks in loads)

            def block(rows, index):
                at_block(index, loads, n.wait)
                branch_back(r, rows, r.cot[rows].astype(wide))
                at_block(index, stores, n.start)

            each_block(r.cot.shape[0], block)
            wait_all(stores)

        inputs = {
            **self.any_inputs({n.cot_hbm: returned}),
            n.final_gain: (self.vectors[n.final_gain], WHOLE),
        }
        self.stage(
            n.back_branch, body, 0, inputs, {}, need, keep, (n.cot, *need, *keep), True
        )

    def first_back_inner(self, row):
        need = (n.gelu_grad, n.grad_branch)

        def body(r, copies):
            rows = self.place(row)
            first = copies.start(r.grad_branch_kept.at[rows], r.grad_branch)
            width = r.grad_branch.shape[1]
            loads, stores = [], []
            for part in parts_of(r.grad_inner.shape[1], width):
                loads.append(
                    (
                        copies.start(r.out_hbm.at[0, part], r.weight_out.at[part]),
                        copies.start(r.gelu_grad_kept.at[rows, part], r.gelu_grad.at[:, part]),
                    )
                )
                stores.append(
                    copies.plan(r.grad_inner.at[:, part], r.grad_inner_kept.at[rows, part])
                )
            first.wait()

            def step(index, carry):
                for place, group in enumerate(loads):
                    pl.when(index == place)(functools.partial(do_all, [load.wait for load in group]))
                part = pl.ds(pl.multiple_of(index * width, width), width)
                grad_active = matmul(r.grad_branch[...], r.weight_out[part], 1, 1)
                grad_inner = grad_active * r.gelu_grad[:, part].astype(wide)
                r.grad_inner[:, part] = grad_inner.astype(low)
                r.small[pl.ds(BIAS_IN + index, 1)] += add_rows(grad_inner)
                for place, store in enumerate(stores):
                    pl.when(index == place)(store.start)
                return carry

            lax.fori_loop(0, len(loads), step, 0)
            for store in stores:
                store.wait()

        inputs = self.any_inputs({n.out_hbm: self.weights[n.out_hbm]})
        self.stage(
            n.back_inner, body, 0, inputs, {}, need, (n.grad_inner,), (n.weight_out, n.grad_inner, *need), True
        )

    def first_back_input(self, row):
        need = (n.grad_inner, n.grad_sum, n.normed_one, n.inverse_one)

        def body(r, copies):
            weight_load = copies.start(r.in_hbm.at[0], r.weight_in)
            loads = [
                copies.blocks(getattr(r, name + n._kept).at[self.place(row)], getattr(r, name))
                for name in need
            ]
            stores = [copies.blocks(r.sum, r.grad_mixed_kept.at[self.place(row)])]
            for index in range(len(loads[0])):
                do_all(blocks[index].start for blocks in loads)
            weight_load.wait()

            def block(rows, index):
                at_block(index, loads, n.wait)
                input_back(r, rows)
                at_block(index, stores, n.start)

            each_block(r.sum.shape[0], block)
            wait_all(stores)

        inputs = {
            **self.any_inputs({n.in_hbm: self.weights[n.in_hbm]}),
            n.mix_gain: (self.vectors[n.mix_gain], WHOLE),
        }
        self.stage(
            n.back_input, body, 0, inputs, {}, need, (n.grad_mixed,), (n.weight_in, n.sum, *need), True
        )

    def first_back_spectra(self, row):
        def body(r, copies):
            loads = [
                copies.start(r.grad_mixed_kept.at[self.place(row)], r.sum),
                copies.start(r.seq_hbm, r.seq_mix),
                copies.start(r.mix_hbm, r.hidden_mix),
            ]
            for load in loads:
                load.wait()

            stores = [copies.blocks(r.grad_wide, r.grad_rows.at[row])]

            def put(rows, index, values):
                r.grad_wide[rows] = values
                at_block(index, stores, n.start)

            spectra_back(r, put)
            wait_all(stores)

        self.stage(
            n.back_spectra,
            body,
            0,
            self.any_inputs(self.tables),
            {},
            (n.grad_mixed,),
            (n.grad_rows,),
            (n.hidden_mix, n.seq_mix, n.spectra, n.sum, n.grad_seq, n.grad_wide),
        )

    def weight_chunk(self, kind, first, size):
        seq_len, width, inner = self.sizes
        tokens = self.rows * seq_len
        left, right = ((n.active, n.grad_branch), (n.hidden_low, n.grad_inner))[kind]
        height, columns = ((size, width), (width, size))[kind]
        half, quarter = height // 2, height // 4
        length = (quarter, half)[kind]
        wide_part = (columns, columns // 2)[kind]

        def body(r, copies):
            cores = (1 - r.place[1], r.place[1])
            left_first = self.columns[left][1] + (first if kind == 0 else 0)
            right_first = self.columns[right][1] + (first if kind == 1 else 0)
            rights, lefts = [], []
            for k in range(columns // wide_part):
                part = slice(k * wide_part, (k + 1) * wide_part)
                source = r.store.at[:, pl.ds(right_first + k * wide_part, wide_part)]
                rights.append(copies.plan(source, r.right.at[:, part]))
            for k in range(height // length):
                steps_of_core = half // length
                begin = left_first + cores[k // steps_of_core] * half + (k % steps_of_core) * length
                source = r.store.at[:, pl.ds(pl.multiple_of(begin, 128), length)]
                lefts.append(copies.plan(source, r.left.at[k]))
            targets = (
                r.others_first,
                r.others_second,
                r.own.at[:quarter],
                r.own.at[quarter:],
            )
            if kind == 0:
                loads = ((rights[0], lefts[0]), (lefts[1],), (lefts[2],), (lefts[3],))
                outs = [(copies.plan(r.total.at[k], targets[k]),) for k in range(4)]
            else:
                loads = ((rights[0], lefts[0]), (lefts[1],), (rights[1],), ())
                pairs = [
                    [
                        copies.plan(r.total.at[k, piece * quarter : (piece + 1) * quarter], targets[2 * k + piece])
                        for piece in range(2)
                    ]
                    for k in range(2)
                ]
                outs = ((), (), pairs[0], pairs[1])
            do_all(load.start for group in loads for load in group)

            def step(index, carry):
                for place, group in enumerate(loads):
                    pl.when(index == place)(functools.partial(do_all, [load.wait for load in group]))
                if kind == 0:
                    r.total[index] = matmul(r.left[index], r.right[...], 0, 0).astype(low)
                else:
                    k = index % 2
                    part = pl.ds(pl.multiple_of(index // 2 * wide_part, wide_part), wide_part)
                    r.total[k, :, part] = matmul(r.left[k], r.right[:, part], 0, 0).astype(low)
                for place, group in enumerate(outs):
                    pl.when(index == place)(functools.partial(do_all, [out.start for out in group]))
                return carry

            lax.fori_loop(0, 4, step, 0)
            do_all(out.wait for group in outs for out in group)

        shape = jax.ShapeDtypeStruct((quarter, columns), low)
        results = run_kernel(
            n.product,
            body,
            {n.store: (self.kept[n.store_low], ANY)},
            {
                n.own: (jax.ShapeDtypeStruct((half, columns), low), ANY),
                n.others_first: (shape, ANY),
                n.others_second: (shape, ANY),
            },
            (),
            {
                n.left: ((height // length, tokens, length), low),
                n.right: ((tokens, columns), low),
                n.total: ((height // length, length, columns), low),
            },
        )
        return results[n.own], results[n.others_first], results[n.others_second]

    def others_back_spectra(self, row):
        for earlier in range(row):
            self.first_back_spectra(earlier)


def parts_of(inner, width):
    return [slice(first, first + width) for first in range(0, inner, width)]


def forward_loads(r, copies, *pieces):
    x_loads, first = [], 0
    for piece in pieces:
        length = r.row.shape[0] // len(pieces)
        x_loads.append(copies.start(piece.at[:length], r.row.at[first : first + length]))
        first += length
    mix_load = copies.start(r.mix_hbm, r.hidden_mix)
    do_all(load.wait for load in x_loads)
    mix_load.wait()
    seq_load = copies.start(r.seq_hbm, r.seq_mix)
    in_load = copies.start(r.in_hbm.at[0], r.weight_in)
    out_load = copies.start(r.out_hbm.at[0], r.weight_out)

    def transform(rows, index):
        r.spectra[rows] = matmul(r.row[rows], r.hidden_mix[...]).astype(low)

    each_block(r.row.shape[0], transform)
    seq_load.wait()
    return in_load, out_load


def exchange(block, distance):
    devices = range(lax.axis_size("dp"))
    return lax.ppermute(block, "dp", [(i, i ^ distance) for i in devices])


def along_line(block, steps):
    route = [(a * 4 + j, b * 4 + j) for a, b in steps for j in range(4)]
    return lax.ppermute(block, "dp", route)


def low_sum(first, second):
    return (first[...].astype(wide) + second[...].astype(wide)).astype(low)


class Sum:
    def __init__(self, make, small):
        self.make, self.small = make, small

    def kernel(self, title, body, shapes, **come):
        results = run_kernel(
            title,
            body,
            {
                n.own: (self.own, WHOLE),
                **{name: (array, WHOLE) for name, array in come.items()},
            },
            {name: (jax.ShapeDtypeStruct(shape, low), WHOLE) for name, shape in shapes.items()},
            (),
            {},
        )
        return [results[name] for name in shapes]

    def add(self):
        def body(r, copies):
            r.total[...] = low_sum(r.own, r.come)

        (self.own,) = self.kernel(n.add, body, {n.total: self.own.shape}, come=self.come)

    def core(self):
        self.own, first, second = self.make()
        self.come = exchange(first, 1), exchange(second, 1)

    def pair(self):
        rows, columns = self.own.shape
        half = rows // 2
        first, second = self.come
        come = {n.first: first, n.second: second}
        small = self.small()
        extra = 0
        if small is not None:
            come[n.small] = small
            extra = small.shape[0] // 2

        def body(r, copies):
            @pl.when(r.place[2] == 0)
            def keep_first():
                r.kept[:half] = low_sum(r.own.at[:half], r.first)
                r.other[:half] = low_sum(r.own.at[half:], r.second)

            @pl.when(r.place[2] == 1)
            def keep_second():
                r.other[:half] = low_sum(r.own.at[:half], r.first)
                r.kept[:half] = low_sum(r.own.at[half:], r.second)

            if extra:
                for target, pair in ((r.kept, r.place[2]), (r.other, 1 - r.place[2])):
                    rows = pl.ds(pl.multiple_of(pair * extra, extra), extra)
                    target[half:, : r.small.shape[1]] = r.small[rows, :].astype(low)

        shapes = {n.kept: (half + extra, columns), n.other: (half + extra, columns)}
        self.own, other = self.kernel(n.pair, body, shapes, **come)
        self.come = exchange(other, 2)

    def inward(self):
        self.add()
        line = lax.axis_size("dp") // 4
        if line == 4:
            self.come = along_line(self.own, [(0, 1), (3, 2)])
            return
        distance = 4
        while distance < 4 * line:
            self.come = exchange(self.own, distance)
            distance *= 2
            if distance < 4 * line:
                self.add()

    def middle(self):
        self.add()
        if lax.axis_size("dp") == 16:
            self.come = along_line(self.own, [(1, 2), (2, 1)])

    def outward(self):
        if lax.axis_size("dp") == 16:
            self.add()
            self.come = along_line(self.own, [(1, 0), (2, 3)])

    def pair_back(self):
        if lax.axis_size("dp") == 16:

            def body(r, copies):
                r.total[...] = jnp.where(r.place[3] == 1, r.own[...], r.come[...])

            (self.own,) = self.kernel(n.take, body, {n.total: self.own.shape}, come=self.come)
        self.come = exchange(self.own, 2)

    def core_back(self):
        def body(r, copies):
            r.pair_part[...] = r.come[...]

        (self.pair_part,) = self.kernel(n.join, body, {n.pair_part: self.own.shape}, come=self.come)
        self.come = exchange(self.own, 1), exchange(self.pair_part, 1)

    def finish(self, target, shape, kind, first, size, extra, whose):
        rows, columns = self.own.shape
        length = rows - extra
        with_small = extra > 0 and 1 in whose
        arrays = {n.own: self.own, n.pair_part: self.pair_part}
        if 1 in whose:
            arrays.update({n.core_own: self.come[0], n.core_pair: self.come[1]})

        def body(r, copies):
            stores = []
            for core_place in whose:
                parts = ((r.own, r.pair_part) if core_place == 0 else (r.core_own, r.core_pair))
                core = r.place[1] if core_place == 0 else 1 - r.place[1]
                for index, part in enumerate(parts):
                    pair = r.place[2] if index == 0 else 1 - r.place[2]
                    quarter = 2 * core + pair
                    to = r.full.at[2 * core_place + index]
                    to[...] = part[:length].astype(wide)
                    rows_at = pl.ds(
                        pl.multiple_of(quarter * length + (first if kind == 0 else 0), 16), length
                    )
                    where = (0, rows_at) if kind == 0 else (0, rows_at, pl.ds(first, size))
                    stores.append(copies.start(to, r.target.at[where]))
            if with_small:
                width = r.small.shape[1]
                for index, (mine, others) in enumerate(
                    ((r.own, r.core_own), (r.pair_part, r.core_pair))
                ):
                    pair = r.place[2] if index == 0 else 1 - r.place[2]
                    to = pl.ds(pl.multiple_of(pair * extra, extra), extra)
                    total = mine[length:, :].astype(wide) + others[length:, :].astype(wide)
                    r.small[to, :] = total[:, :width]
                for place, output in enumerate(
                    (r.mix_gain, r.mix_bias, r.bias_out, r.final_gain, r.final_bias)
                ):
                    output[...] = r.small[place : place + 1]
                for place, part in enumerate(parts_of(r.bias_in.shape[1], width)):
                    r.bias_in[:, part] = r.small[BIAS_IN + place : BIAS_IN + place + 1]
            for store in stores:
                store.wait()

        inputs = {name: (array, WHOLE) for name, array in arrays.items()}
        if target is not None:
            inputs[n.target] = (target, ANY)
        outputs = {n.target: (jax.ShapeDtypeStruct(shape, wide), ANY)}
        scratch = {n.full: ((4, length, columns), wide)}
        if with_small:
            width, inner = shape[1:]
            one = (jax.ShapeDtypeStruct((1, width), wide), WHOLE)
            outputs.update(
                mix_gain=one,
                mix_bias=one,
                bias_out=one,
                final_gain=one,
                final_bias=one,
                bias_in=(jax.ShapeDtypeStruct((1, inner), wide), WHOLE),
            )
            scratch[n.small] = ((2 * extra, width), wide)
        results = run_kernel(
            n.finish,
            body,
            inputs,
            outputs,
            (n.target,) if target is not None else (),
            scratch,
        )
        return results.pop(n.target), results


CHUNKS = ((0, 6), (0, 6), (1, 6), (1, 6))
STEPS = (
    (1, n.core),
    (0, n.core),
    (1, n.pair),
    (None, n.first_back_inner),
    (2, n.core),
    (0, n.pair),
    (1, n.inward),
    (3, n.core),
    (2, n.pair),
    (0, n.inward),
    (1, n.middle),
    (None, n.first_back_input),
    (3, n.pair),
    (2, n.inward),
    (0, n.middle),
    (1, n.outward),
    (3, n.inward),
    (2, n.middle),
    (0, n.outward),
    (1, n.pair_back),
    (None, n.first_back_spectra),
    (3, n.middle),
    (2, n.outward),
    (1, n.core_back),
    (0, n.pair_back),
    (3, n.outward),
    (2, n.pair_back),
    (1, n.finish),
    (None, n.others_back_spectra),
    (0, n.core_back),
    (3, n.pair_back),
    (2, n.core_back),
    (0, n.finish),
    (2, n.finish),
    (3, n.core_back),
    (3, n.finish_own),
    (3, n.finish),
)


def per_device(
    activations,
    out_cotangent,
    doc_lengths,
    mix_gain,
    mix_bias,
    weight_in,
    bias_in,
    weight_out,
    bias_out,
    final_gain,
    final_bias,
):
    rows, seq_len, width = activations.shape
    inner = weight_in.shape[2]
    order.last, order.shares_vmem = None, False
    tables = make_tables(width, seq_len)
    vectors = {
        n.mix_gain: mix_gain,
        n.mix_bias: mix_bias,
        n.bias_in: bias_in,
        n.bias_out: bias_out,
        n.final_gain: final_gain,
        n.final_bias: final_bias,
    }
    work = Sections(rows, (seq_len, width, inner), tables, (weight_in, weight_out), vectors)
    handed = []
    for row in range(rows):
        if row == 0:
            pieces, spectra = [], None
            for block in range(seq_len // BLOCK):
                piece, made = work.first_part(row, activations, block, spectra)
                spectra = made if block == 0 else spectra
                pieces.append(from_behind(piece, "pipe", 1))
        else:
            result = work.first_forward(row, activations, True, True)
            pieces = [from_behind(result, "pipe", 1)]
        handed.append(pieces)
    returned = []
    for row in range(rows):
        result = work.later_both(row, handed[row], out_cotangent, doc_lengths)
        returned.append(from_behind(result, "pipe", -1))
        if row == 0:
            work.first_forward(row, activations, True, False)
    for row in range(rows):
        work.first_back_branch(row, returned[row])
        if row < rows - 1:
            work.first_back_inner(row)
            work.first_back_input(row)
    order.shares_vmem = True
    sums, first = [], [0, 0]
    for kind, units in CHUNKS:
        size = units * inner // 12
        last = len(sums) == len(CHUNKS) - 1
        make = functools.partial(work.weight_chunk, kind, first[kind], size)
        small_of = functools.partial(getattr, work, n.small) if last else nothing
        sums.append((Sum(make, small_of), kind, first[kind], size, 16 if last else 0))
        first[kind] += size
    shapes, targets = (weight_out.shape, weight_in.shape), [None, None]
    for index, step in STEPS:
        if index is None:
            getattr(work, step)(rows - 1)
        elif step in (n.finish, n.finish_own):
            chunk, kind, *rest = sums[index]
            whose = (0,) if step == n.finish_own else (1,) if (index, n.finish_own) in STEPS else (0, 1)
            targets[kind], small = chunk.finish(targets[kind], shapes[kind], kind, *rest, whose)
        else:
            getattr(sums[index][0], step)()
    return (
        work.kept[n.layer_rows][None],
        work.kept[n.grad_rows][None],
        small[n.mix_gain],
        small[n.mix_bias],
        targets[1],
        small[n.bias_in],
        targets[0],
        small[n.bias_out],
        small[n.final_gain],
        small[n.final_bias],
    )


def solution(mesh):
    placed = (
        P("dp", None, None),
        P("dp", None, None),
        P("dp", None),
        P("pipe", None),
        P("pipe", None),
        P("pipe", None, None),
        P("pipe", None),
        P("pipe", None, None),
        P("pipe", None),
        P("pipe", None),
        P("pipe", None),
    )
    return jax.shard_map(
        per_device,
        mesh=mesh,
        in_specs=placed,
        out_specs=(
            P("pipe", "dp", None, None),
            P("pipe", "dp", None, None),
            P("pipe", None),
            P("pipe", None),
            P("pipe", None, None),
            P("pipe", None),
            P("pipe", None, None),
            P("pipe", None),
            P("pipe", None),
            P("pipe", None),
        ),
        check_vma=False,
    )
```

```python
import functools
import math

import jax
import jax.numpy as jnp
import numpy as np
from jax import lax
from jax.experimental import pallas as pl
from jax.experimental.pallas import tpu as pltpu
from jax.sharding import PartitionSpec as P

eps_norm = 1e-06
low, wide = jnp.bfloat16, jnp.float32
slope = math.sqrt(2.0 / math.pi)
cubic = 0.044715
VMEM_SPARE = 6 * 2**20
SHARE = 800000000
SHARE = 800000000
LONG = 6000000000
VMEM_SHARED = 44 * 2**20
VMEM_ALL = 62 * 2**20
VMEM_LATER = 50 * 2**20
BLOCK = 256
ANY = pl.BlockSpec(memory_space=pltpu.HBM)
SCALARS = pl.BlockSpec(memory_space=pltpu.SMEM)
WHOLE = pl.BlockSpec(memory_space=pltpu.VMEM)

MIX_GAIN, MIX_BIAS, BIAS_OUT, FINAL_GAIN, FINAL_BIAS, BIAS_IN = 0, 1, 2, 3, 4, 16


class Names:
    def __getattr__(self, name):
        return name


n = Names()


def from_behind(block, axis, distance):
    devices = range(lax.axis_size(axis))
    route = [(i - distance, i) for i in devices if i - distance in devices]
    return lax.ppermute(block, axis, route)


def dft_tables(table_len):
    indices = np.arange(table_len)
    angles = (indices[:, None] * indices[None, :] % table_len) * (2.0 * math.pi / table_len)
    scaled = 1.0 / math.sqrt(table_len)
    return (np.cos(angles) * scaled, np.sin(angles) * scaled)


def make_tables(width, seq_len):
    half = width // 2
    hid_cos, hid_sin = dft_tables(width)
    seq_cos, seq_sin = dft_tables(seq_len)
    hidden_mix = np.concatenate([hid_cos[:, : half + 1], hid_sin[:, 1:half]], axis=1)
    seq_mix = np.concatenate([seq_cos, -seq_sin], axis=1)
    return jnp.asarray(hidden_mix, low), jnp.asarray(seq_mix, low)


def matmul(left, right, left_dim=1, right_dim=0):
    return lax.dot_general(
        left, right, (((left_dim,), (right_dim,)), ((), ())), preferred_element_type=wide
    )


def mean_last(values):
    return jnp.mean(values, axis=-1, keepdims=True)


def normalize(values):
    centred = values - mean_last(values)
    inverse = lax.rsqrt(mean_last(centred * centred) + eps_norm)
    return (centred * inverse, inverse)


def norm_back(grad_norm, normed, inverse):
    return inverse * (grad_norm - mean_last(grad_norm) - normed * mean_last(grad_norm * normed))


def gelu_parts(values):
    square = values * values
    part = 0.5 + 0.5 * jnp.tanh(values * (slope + slope * cubic * square))
    active = values * part
    step = 2.0 * slope + 6.0 * slope * cubic * square
    return (active, part + active * (1.0 - part) * step)


def nothing():
    pass


def place_of():
    index = lax.axis_index("dp")
    line = index // 4
    inside = jnp.where((line == 1) | (line == 2), 1, 0)
    return lax.axis_index("pipe"), index % 2, index // 2 % 2, inside


def each_block(seq_len, body):
    def step(index, carry):
        body(pl.ds(pl.multiple_of(index * BLOCK, BLOCK), BLOCK), index)
        return carry

    lax.fori_loop(0, seq_len // BLOCK, step, 0)


def at_block(index, plans, call):
    for place in range(len(plans[0])):
        calls = [getattr(blocks[place], call) for blocks in plans]
        pl.when(index == place)(functools.partial(do_all, calls))


def wait_all(plans):
    do_all(copy.wait for blocks in plans for copy in blocks)


def add_rows(values):
    return jnp.sum(values, axis=0, keepdims=True)


class Copy:
    def __init__(self, source, target, sem):
        self.parts = source, target, sem

    def start(self):
        pltpu.make_async_copy(*self.parts).start()

    def wait(self):
        pltpu.make_async_copy(*self.parts).wait()


class Copies:
    def __init__(self, sems):
        self.sems, self.used = sems, 0

    def plan(self, source, target):
        self.used += 1
        return Copy(source, target, self.sems.at[self.used - 1])

    def blocks(self, source, target):
        parts = [slice(first, first + BLOCK) for first in range(0, target.shape[0], BLOCK)]
        return [self.plan(source.at[part], target.at[part]) for part in parts]

    def start(self, source, target):
        copy = self.plan(source, target)
        copy.start()
        return copy


def do_all(calls):
    for call in calls:
        call()


def add_to(small, place, values):
    small[place : place + 1] += add_rows(values)


def first_lane(values):
    return lax.broadcasted_iota(jnp.int32, values.shape, 1) == 0


def mirror(values):
    groups = values.shape[1] // 128
    parts = [values[:, 128 * g : 128 * (g + 1)] for g in range(groups)]
    lane = lax.broadcasted_iota(jnp.int32, parts[0].shape, 1)
    turned = [jnp.take_along_axis(part, lax.rem(128 - lane, 128), axis=1) for part in parts]
    mirrored = [
        jnp.where(lane == 0, turned[-g % groups], turned[groups - 1 - g]) for g in range(groups)
    ]
    return jnp.concatenate(mirrored, axis=1)


def mixed_rows(r, rows):
    seq_len, width = r.spectra.shape
    half = width // 2
    even = matmul(r.seq_mix[rows, :seq_len], r.spectra[:, : half + 128])
    odd = matmul(r.seq_mix[rows, seq_len:], r.spectra[:, half:])
    middle = even[:, half : half + 1]
    even = even[:, :half]
    odd = jnp.where(first_lane(odd), 0.0, odd)
    later = mirror(even - odd)
    return even + odd, jnp.where(first_lane(later), middle, later)


def forward_block(r, rows, index, in_load, out_load):
    width = r.row.shape[1]
    half = width // 2
    begin, end = mixed_rows(r, rows)
    r.sum[rows, :half] = r.row[rows, :half].astype(wide) + begin
    r.sum[rows, half:] = r.row[rows, half:].astype(wide) + end
    normed, inverse = normalize(r.sum[rows])
    r.normed_one[rows] = normed
    r.inverse_one[rows] = jnp.broadcast_to(inverse, (BLOCK, 128))
    r.hidden_low[rows] = (normed * r.mix_gain[...] + r.mix_bias[...]).astype(low)
    pl.when(index == 0)(in_load.wait)
    for part in parts_of(r.weight_in.shape[1], width):
        inner = matmul(r.hidden_low[rows], r.weight_in[:, part]) + r.bias_in[:, part]
        active, gelu_grad = gelu_parts(inner)
        active = active.astype(low)
        r.active[rows, part] = active
        r.gelu_grad[rows, part] = gelu_grad.astype(low)
        if part.start == 0:
            pl.when(index == 0)(out_load.wait)
            r.sum[rows] = matmul(active, r.weight_out[part])
        else:
            r.sum[rows] += matmul(active, r.weight_out[part])
    hidden = r.normed_one[rows] * r.mix_gain[...] + r.mix_bias[...]
    normed, inverse = normalize(hidden + r.sum[rows] + r.bias_out[...])
    r.normed_two[rows] = normed
    r.inverse_two[rows] = jnp.broadcast_to(inverse, (BLOCK, 128))
    r.result[rows] = (normed * r.final_gain[...] + r.final_bias[...]).astype(low)


def branch_back(r, rows, grad_out):
    normed = r.normed_two[rows]
    grad_sum = norm_back(grad_out * r.final_gain[...], normed, r.inverse_two[rows][:, :1])
    r.grad_sum[rows] = grad_sum
    grad_branch = grad_sum.astype(low)
    r.grad_branch[rows] = grad_branch
    add_to(r.small, BIAS_OUT, grad_branch.astype(wide))
    add_to(r.small, FINAL_GAIN, grad_out * normed)
    add_to(r.small, FINAL_BIAS, grad_out)


def inner_back(r, rows, index):
    width = r.grad_branch.shape[1]
    part = slice(index * width, (index + 1) * width)
    grad_active = matmul(r.grad_branch[rows], r.weight_out[part], 1, 1)
    grad_inner = grad_active * r.gelu_grad[rows, part].astype(wide)
    r.grad_inner[rows, part] = grad_inner.astype(low)
    add_to(r.small, BIAS_IN + index, grad_inner)


def input_back(r, rows):
    grad_hidden = r.grad_sum[rows] + matmul(r.grad_inner[rows], r.weight_in[...], 1, 1)
    normed = r.normed_one[rows]
    r.sum[rows] = norm_back(grad_hidden * r.mix_gain[...], normed, r.inverse_one[rows][:, :1])
    add_to(r.small, MIX_GAIN, grad_hidden * normed)
    add_to(r.small, MIX_BIAS, grad_hidden)


def spectra_back(r, put):
    seq_len, width = r.sum.shape
    half = width // 2

    def fold(rows, index):
        begin, end = r.sum[rows, :half], mirror(r.sum[rows, half:])
        lane = first_lane(begin)
        r.grad_seq[rows, :half] = jnp.where(lane, begin, begin + end).astype(low)
        r.grad_seq[rows, half:] = jnp.where(lane, end, begin - end).astype(low)

    each_block(seq_len, fold)

    def transform(rows, index):
        even = matmul(r.seq_mix[rows, :seq_len], r.grad_seq[:, : half + 128])
        odd = matmul(r.seq_mix[rows, seq_len:], r.grad_seq[:, half:])
        odd = jnp.where(first_lane(odd), even[:, half : half + 1], odd)
        r.spectra[rows, :half] = even[:, :half].astype(low)
        r.spectra[rows, half:] = odd.astype(low)
        put(rows, index, r.sum[rows] + matmul(r.spectra[rows], r.hidden_mix[...], 1, 1))

    each_block(seq_len, transform)


class Named:
    def __init__(self, refs):
        self.__dict__.update(refs)


class Order:
    last = None
    shares_vmem = False


order = Order()


def run_kernel(name, body, inputs, outputs, taken, scratch):
    if order.last is not None:
        inputs = {**inputs, n.after: (order.last, ANY)}
    outputs = {**outputs, n.turn: (jax.ShapeDtypeStruct((8, 128), wide), ANY)}
    n_in, n_out = len(inputs), len(outputs)
    names_in, names_out = list(inputs), list(outputs)

    held = sum(math.prod(shape) * np.dtype(dtype).itemsize for shape, dtype in scratch.values())
    for array, spec in (*inputs.values(), *outputs.values()):
        if spec is WHOLE:
            held += math.prod(array.shape) * np.dtype(array.dtype).itemsize

    def kernel(*refs):
        named = dict(zip(names_in, refs[:n_in]))
        for name, ref in zip(names_out, refs[n_in : n_in + n_out]):
            named[name] = ref
        named.update(zip(scratch, refs[n_in + n_out : -1]), place=place_of())
        body(Named(named), Copies(refs[-1]))

    results = pl.pallas_call(
        kernel,
        name=name,
        in_specs=[spec for _, spec in inputs.values()],
        out_shape=[jax.ShapeDtypeStruct(shape.shape, shape.dtype) for shape, _ in outputs.values()],
        out_specs=[spec for _, spec in outputs.values()],
        scratch_shapes=[
            *[pltpu.VMEM(*shape) for shape in scratch.values()],
            pltpu.SemaphoreType.DMA((48,)),
        ],
        input_output_aliases={names_in.index(name): names_out.index(name) for name in taken},
        compiler_params=pltpu.CompilerParams(
            vmem_limit_bytes=max(VMEM_SHARED, VMEM_SPARE + held) if order.shares_vmem else (VMEM_ALL if name == n.first_forward else VMEM_LATER)
        ),
        cost_estimate=pl.CostEstimate(flops=(SHARE if name != n.finish else 1) if order.shares_vmem else (LONG if name == n.later_first else 1), bytes_accessed=1, transcendentals=0),
    )(*[array for array, _ in inputs.values()])
    results = dict(zip(names_out, results))
    order.last = results.pop(n.turn)
    return results


class Sections:
    def __init__(self, rows, sizes, tables, weights, vectors):
        self.rows, self.sizes = rows, sizes
        self.tables = dict(zip((n.mix_hbm, n.seq_hbm), tables))
        self.weights = dict(zip((n.in_hbm, n.out_hbm), weights))
        self.vectors = vectors
        self.kept = {}
        seq_len, width, inner = sizes
        self.shapes = {
            n.row: ((seq_len, width), low),
            n.cot: ((seq_len, width), low),
            n.hidden_mix: ((width, width), low),
            n.seq_mix: ((seq_len, 2 * seq_len), low),
            n.weight_in: ((width, inner), low),
            n.weight_out: ((inner, width), low),
            n.spectra: ((seq_len, width), low),
            n.sum: ((seq_len, width), wide),
            n.normed_one: ((seq_len, width), wide),
            n.inverse_one: ((seq_len, 128), wide),
            n.normed_two: ((seq_len, width), wide),
            n.inverse_two: ((seq_len, 128), wide),
            n.hidden_low: ((seq_len, width), low),
            n.active: ((seq_len, inner), low),
            n.gelu_grad: ((seq_len, inner), low),
            n.result: ((seq_len, width), low),
            n.grad_sum: ((seq_len, width), wide),
            n.grad_branch: ((seq_len, width), low),
            n.grad_inner: ((seq_len, inner), low),
            n.grad_seq: ((seq_len, width), low),
            n.grad_mixed: ((seq_len, width), wide),
            n.grad_low: ((seq_len, width), low),
            n.grad_wide: ((seq_len, width), wide),
        }
        self.small = None
        self.columns, self.stores = {}, {}
        for store, names in (
            (n.store_low, (n.active, n.gelu_grad, n.grad_inner, n.hidden_low, n.grad_branch)),
            (n.store_wide, (n.normed_one, n.normed_two, n.grad_sum, n.grad_mixed, n.inverse_one, n.inverse_two)),
        ):
            first = 0
            for name in names:
                (length, size), dtype = self.shapes[name]
                self.columns[name] = (store, first, size)
                first += size
            self.stores[store] = jax.ShapeDtypeStruct((rows * length, first), dtype)
        for store, dtype in ((n.layer_rows, low), (n.grad_rows, wide)):
            self.columns[store] = (store, None, None)
            self.stores[store] = jax.ShapeDtypeStruct((rows, seq_len, width), dtype)

    def stage(self, title, body, owner, inputs, made, reads, writes, scratch, uses_small=False):
        outputs = {name: (shape, ANY) for name, shape in made.items()}
        taken = []
        for store in dict.fromkeys(self.columns[name][0] for name in (*writes, *reads)):
            if store in self.kept:
                inputs[store] = (self.kept[store], ANY)
            if any(self.columns[name][0] == store for name in writes):
                if store in self.kept:
                    taken.append(store)
                outputs[store] = (self.stores[store], ANY)
        if uses_small:
            if self.small is not None:
                inputs[n.small_before] = (self.small, WHOLE)
            outputs[n.small] = (jax.ShapeDtypeStruct((32, self.sizes[1]), wide), WHOLE)

        def kernel(refs, copies):
            for name in (*reads, *writes):
                store, first, size = self.columns[name]
                ref = getattr(refs, store)
                setattr(refs, name + n._kept, ref if size is None else ref.at[:, first : first + size])
            if uses_small:
                before = getattr(refs, n.small_before, None)
                refs.small[...] = jnp.zeros_like(refs.small) if before is None else before[...]
            pl.when(refs.place[0] == owner)(lambda: body(refs, copies))

        results = run_kernel(
            title, kernel, inputs, outputs, taken, {name: self.shapes[name] for name in scratch}
        )
        if uses_small:
            self.small = results.pop(n.small)
        for name in list(results):
            if name in self.stores:
                self.kept[name] = results.pop(name)
        return results

    def place(self, row):
        return pl.ds(row * self.sizes[0], self.sizes[0])

    def row_shape(self, dtype):
        return jax.ShapeDtypeStruct(self.sizes[:2], dtype)

    def any_inputs(self, arrays):
        return {name: (array, ANY) for name, array in arrays.items()}

    def vector_inputs(self):
        return {name: (array, WHOLE) for name, array in self.vectors.items()}

    def first_forward(self, row, activations, keeps, hands):
        keep = (n.gelu_grad, n.normed_one, n.inverse_one, n.normed_two, n.inverse_two, n.active, n.hidden_low)

        def body(r, copies):
            loads = forward_loads(r, copies, r.x_hbm.at[row])
            stores = []
            if hands:
                stores.append(copies.blocks(r.result, r.handed))
            if keeps:
                stores.append(copies.blocks(r.result, r.layer_rows.at[row]))
                for name in keep:
                    target = getattr(r, name + n._kept).at[self.place(row)]
                    stores.append(copies.blocks(getattr(r, name), target))

            def block(rows, index):
                forward_block(r, rows, index, *loads)
                at_block(index, stores, n.start)

            each_block(r.row.shape[0], block)
            wait_all(stores)

        inputs = {
            **self.any_inputs({n.x_hbm: activations, **self.tables, **self.weights}),
            **self.vector_inputs(),
        }
        return self.stage(
            n.first_forward if hands else n.again_forward,
            body,
            0,
            inputs,
            {n.handed: self.row_shape(low)} if hands else {},
            (),
            (*keep, n.layer_rows) if keeps else (),
            (n.row, n.hidden_mix, n.seq_mix, n.weight_in, n.weight_out, n.spectra, n.sum, n.result, *keep),
        ).get(n.handed)

    def first_part(self, row, activations, block, spectra):
        fresh = spectra is None
        names = (n.row, n.hidden_mix, n.seq_mix, n.weight_in, n.weight_out, n.spectra, n.sum, n.result, n.normed_one,
                 n.inverse_one, n.normed_two, n.inverse_two, n.hidden_low, n.active, n.gelu_grad)

        def body(r, copies):
            stores = []
            if fresh:
                loads = forward_loads(r, copies, r.x_hbm.at[row])
                stores.append(copies.start(r.spectra, r.spectra_out))
            else:
                firsts = [
                    copies.start(r.x_hbm.at[row], r.row),
                    copies.start(r.spectra_in, r.spectra),
                    copies.start(r.seq_hbm, r.seq_mix),
                ]
                loads = (
                    copies.start(r.in_hbm.at[0], r.weight_in),
                    copies.start(r.out_hbm.at[0], r.weight_out),
                )
                do_all(first.wait for first in firsts)
            rows = slice(block * BLOCK, (block + 1) * BLOCK)
            forward_block(r, rows, 0, *loads)
            stores.append(copies.start(r.result.at[rows], r.handed.at[:BLOCK]))
            do_all(store.wait for store in stores)

        inputs = {
            **self.any_inputs({n.x_hbm: activations, **self.tables, **self.weights}),
            **self.vector_inputs(),
        }
        if not fresh:
            inputs[n.spectra_in] = (spectra, ANY)
        width = self.sizes[1]
        made = {n.handed: jax.ShapeDtypeStruct((BLOCK + (16 if fresh else 0), width), low)}
        if fresh:
            made[n.spectra_out] = jax.ShapeDtypeStruct(self.sizes[:2], low)
        results = self.stage(n.first_forward, body, 0, inputs, made, (), (), names)
        return results[n.handed], results.get(n.spectra_out)

    def later_both(self, row, handed, out_cotangent, lengths):
        pieces = {n.x_hbm + str(place): piece for place, piece in enumerate(handed)}
        keep = (n.active, n.hidden_low, n.grad_branch, n.grad_inner)

        def body(r, copies):
            loads = forward_loads(r, copies, *[getattr(r, name) for name in pieces])
            cot_load = copies.start(r.cot_hbm.at[row], r.cot)
            filled = r.cot.shape[0] - r.lengths[row, r.lengths.shape[1] - 1]
            stores = [copies.blocks(r.result, r.layer_rows.at[row])]
            for name in keep:
                target = getattr(r, name + n._kept).at[self.place(row)]
                stores.append(copies.blocks(getattr(r, name), target))

            def block(rows, index):
                forward_block(r, rows, index, *loads)
                pl.when(index == 0)(cot_load.wait)
                token = rows.start + lax.broadcasted_iota(jnp.int32, (BLOCK, r.cot.shape[1]), 0)
                branch_back(r, rows, jnp.where(token < filled, r.cot[rows].astype(wide), 0.0))
                for part in range(r.weight_out.shape[0] // r.cot.shape[1]):
                    inner_back(r, rows, part)
                input_back(r, rows)
                at_block(index, stores, n.start)

            each_block(r.row.shape[0], block)
            results = [
                copies.blocks(r.grad_low, r.returned),
                copies.blocks(r.grad_wide, r.grad_rows.at[row]),
            ]

            def put(rows, index, values):
                r.grad_low[rows] = values.astype(low)
                r.grad_wide[rows] = r.grad_low[rows].astype(wide)
                at_block(index, results, n.start)

            spectra_back(r, put)
            wait_all(stores)
            wait_all(results)

        inputs = {
            n.lengths: (lengths, SCALARS),
            **self.any_inputs(pieces),
            **self.any_inputs({n.cot_hbm: out_cotangent, **self.tables, **self.weights}),
            **self.vector_inputs(),
        }
        return self.stage(
            n.later_first if row == 0 else n.later_both,
            body,
            1,
            inputs,
            {n.returned: self.row_shape(low)},
            (),
            (*keep, n.layer_rows, n.grad_rows),
            tuple(name for name in self.shapes if name != n.grad_mixed),
            True,
        )[n.returned]

    def first_back_branch(self, row, returned):
        keep = (n.grad_branch, n.grad_sum)
        need = (n.normed_two, n.inverse_two)

        def body(r, copies):
            loads = [copies.blocks(r.cot_hbm, r.cot)]
            for name in need:
                source = getattr(r, name + n._kept).at[self.place(row)]
                loads.append(copies.blocks(source, getattr(r, name)))
            stores = [
                copies.blocks(getattr(r, name), getattr(r, name + n._kept).at[self.place(row)])
                for name in keep
            ]
            for index in range(len(loads[0])):
                do_all(blocks[index].start for blocks in loads)

            def block(rows, index):
                at_block(index, loads, n.wait)
                branch_back(r, rows, r.cot[rows].astype(wide))
                at_block(index, stores, n.start)

            each_block(r.cot.shape[0], block)
            wait_all(stores)

        inputs = {
            **self.any_inputs({n.cot_hbm: returned}),
            n.final_gain: (self.vectors[n.final_gain], WHOLE),
        }
        self.stage(
            n.back_branch, body, 0, inputs, {}, need, keep, (n.cot, *need, *keep), True
        )

    def first_back_inner(self, row):
        need = (n.gelu_grad, n.grad_branch)

        def body(r, copies):
            rows = self.place(row)
            first = copies.start(r.grad_branch_kept.at[rows], r.grad_branch)
            width = r.grad_branch.shape[1]
            loads, stores = [], []
            for part in parts_of(r.grad_inner.shape[1], width):
                loads.append(
                    (
                        copies.start(r.out_hbm.at[0, part], r.weight_out.at[part]),
                        copies.start(r.gelu_grad_kept.at[rows, part], r.gelu_grad.at[:, part]),
                    )
                )
                stores.append(
                    copies.plan(r.grad_inner.at[:, part], r.grad_inner_kept.at[rows, part])
                )
            first.wait()

            def step(index, carry):
                for place, group in enumerate(loads):
                    pl.when(index == place)(functools.partial(do_all, [load.wait for load in group]))
                part = pl.ds(pl.multiple_of(index * width, width), width)
                grad_active = matmul(r.grad_branch[...], r.weight_out[part], 1, 1)
                grad_inner = grad_active * r.gelu_grad[:, part].astype(wide)
                r.grad_inner[:, part] = grad_inner.astype(low)
                r.small[pl.ds(BIAS_IN + index, 1)] += add_rows(grad_inner)
                for place, store in enumerate(stores):
                    pl.when(index == place)(store.start)
                return carry

            lax.fori_loop(0, len(loads), step, 0)
            for store in stores:
                store.wait()

        inputs = self.any_inputs({n.out_hbm: self.weights[n.out_hbm]})
        self.stage(
            n.back_inner, body, 0, inputs, {}, need, (n.grad_inner,), (n.weight_out, n.grad_inner, *need), True
        )

    def first_back_input(self, row):
        need = (n.grad_inner, n.grad_sum, n.normed_one, n.inverse_one)

        def body(r, copies):
            weight_load = copies.start(r.in_hbm.at[0], r.weight_in)
            loads = [
                copies.blocks(getattr(r, name + n._kept).at[self.place(row)], getattr(r, name))
                for name in need
            ]
            stores = [copies.blocks(r.sum, r.grad_mixed_kept.at[self.place(row)])]
            for index in range(len(loads[0])):
                do_all(blocks[index].start for blocks in loads)
            weight_load.wait()

            def block(rows, index):
                at_block(index, loads, n.wait)
                input_back(r, rows)
                at_block(index, stores, n.start)

            each_block(r.sum.shape[0], block)
            wait_all(stores)

        inputs = {
            **self.any_inputs({n.in_hbm: self.weights[n.in_hbm]}),
            n.mix_gain: (self.vectors[n.mix_gain], WHOLE),
        }
        self.stage(
            n.back_input, body, 0, inputs, {}, need, (n.grad_mixed,), (n.weight_in, n.sum, *need), True
        )

    def first_back_spectra(self, row):
        def body(r, copies):
            loads = [
                copies.start(r.grad_mixed_kept.at[self.place(row)], r.sum),
                copies.start(r.seq_hbm, r.seq_mix),
                copies.start(r.mix_hbm, r.hidden_mix),
            ]
            for load in loads:
                load.wait()

            stores = [copies.blocks(r.grad_wide, r.grad_rows.at[row])]

            def put(rows, index, values):
                r.grad_wide[rows] = values
                at_block(index, stores, n.start)

            spectra_back(r, put)
            wait_all(stores)

        self.stage(
            n.back_spectra,
            body,
            0,
            self.any_inputs(self.tables),
            {},
            (n.grad_mixed,),
            (n.grad_rows,),
            (n.hidden_mix, n.seq_mix, n.spectra, n.sum, n.grad_seq, n.grad_wide),
        )

    def weight_chunk(self, kind, first, size):
        seq_len, width, inner = self.sizes
        tokens = self.rows * seq_len
        left, right = ((n.active, n.grad_branch), (n.hidden_low, n.grad_inner))[kind]
        height, columns = ((size, width), (width, size))[kind]
        half, quarter = height // 2, height // 4
        length = (quarter, half)[kind]
        wide_part = (columns, columns // 2)[kind]

        def body(r, copies):
            cores = (1 - r.place[1], r.place[1])
            left_first = self.columns[left][1] + (first if kind == 0 else 0)
            right_first = self.columns[right][1] + (first if kind == 1 else 0)
            rights, lefts = [], []
            for k in range(columns // wide_part):
                part = slice(k * wide_part, (k + 1) * wide_part)
                source = r.store.at[:, pl.ds(right_first + k * wide_part, wide_part)]
                rights.append(copies.plan(source, r.right.at[:, part]))
            for k in range(height // length):
                steps_of_core = half // length
                begin = left_first + cores[k // steps_of_core] * half + (k % steps_of_core) * length
                source = r.store.at[:, pl.ds(pl.multiple_of(begin, 128), length)]
                lefts.append(copies.plan(source, r.left.at[k]))
            targets = (
                r.others_first,
                r.others_second,
                r.own.at[:quarter],
                r.own.at[quarter:],
            )
            if kind == 0:
                loads = ((rights[0], lefts[0]), (lefts[1],), (lefts[2],), (lefts[3],))
                outs = [(copies.plan(r.total.at[k], targets[k]),) for k in range(4)]
            else:
                loads = ((rights[0], lefts[0]), (lefts[1],), (rights[1],), ())
                pairs = [
                    [
                        copies.plan(r.total.at[k, piece * quarter : (piece + 1) * quarter], targets[2 * k + piece])
                        for piece in range(2)
                    ]
                    for k in range(2)
                ]
                outs = ((), (), pairs[0], pairs[1])
            do_all(load.start for group in loads for load in group)

            def step(index, carry):
                for place, group in enumerate(loads):
                    pl.when(index == place)(functools.partial(do_all, [load.wait for load in group]))
                if kind == 0:
                    r.total[index] = matmul(r.left[index], r.right[...], 0, 0).astype(low)
                else:
                    k = index % 2
                    part = pl.ds(pl.multiple_of(index // 2 * wide_part, wide_part), wide_part)
                    r.total[k, :, part] = matmul(r.left[k], r.right[:, part], 0, 0).astype(low)
                for place, group in enumerate(outs):
                    pl.when(index == place)(functools.partial(do_all, [out.start for out in group]))
                return carry

            lax.fori_loop(0, 4, step, 0)
            do_all(out.wait for group in outs for out in group)

        shape = jax.ShapeDtypeStruct((quarter, columns), low)
        results = run_kernel(
            n.product,
            body,
            {n.store: (self.kept[n.store_low], ANY)},
            {
                n.own: (jax.ShapeDtypeStruct((half, columns), low), ANY),
                n.others_first: (shape, ANY),
                n.others_second: (shape, ANY),
            },
            (),
            {
                n.left: ((height // length, tokens, length), low),
                n.right: ((tokens, columns), low),
                n.total: ((height // length, length, columns), low),
            },
        )
        return results[n.own], results[n.others_first], results[n.others_second]

    def others_back_spectra(self, row):
        for earlier in range(row):
            self.first_back_spectra(earlier)


def parts_of(inner, width):
    return [slice(first, first + width) for first in range(0, inner, width)]


def forward_loads(r, copies, *pieces):
    x_loads, first = [], 0
    for piece in pieces:
        length = r.row.shape[0] // len(pieces)
        x_loads.append(copies.start(piece.at[:length], r.row.at[first : first + length]))
        first += length
    mix_load = copies.start(r.mix_hbm, r.hidden_mix)
    do_all(load.wait for load in x_loads)
    mix_load.wait()
    seq_load = copies.start(r.seq_hbm, r.seq_mix)
    in_load = copies.start(r.in_hbm.at[0], r.weight_in)
    out_load = copies.start(r.out_hbm.at[0], r.weight_out)

    def transform(rows, index):
        r.spectra[rows] = matmul(r.row[rows], r.hidden_mix[...]).astype(low)

    each_block(r.row.shape[0], transform)
    seq_load.wait()
    return in_load, out_load


def exchange(block, distance):
    devices = range(lax.axis_size("dp"))
    return lax.ppermute(block, "dp", [(i, i ^ distance) for i in devices])


def along_line(block, steps):
    route = [(a * 4 + j, b * 4 + j) for a, b in steps for j in range(4)]
    return lax.ppermute(block, "dp", route)


def low_sum(first, second):
    return (first[...].astype(wide) + second[...].astype(wide)).astype(low)


class Sum:
    def __init__(self, make, small):
        self.make, self.small = make, small

    def kernel(self, title, body, shapes, **come):
        results = run_kernel(
            title,
            body,
            {
                n.own: (self.own, WHOLE),
                **{name: (array, WHOLE) for name, array in come.items()},
            },
            {name: (jax.ShapeDtypeStruct(shape, low), WHOLE) for name, shape in shapes.items()},
            (),
            {},
        )
        return [results[name] for name in shapes]

    def add(self):
        def body(r, copies):
            r.total[...] = low_sum(r.own, r.come)

        (self.own,) = self.kernel(n.add, body, {n.total: self.own.shape}, come=self.come)

    def core(self):
        self.own, first, second = self.make()
        self.come = exchange(first, 1), exchange(second, 1)

    def pair(self):
        rows, columns = self.own.shape
        half = rows // 2
        first, second = self.come
        come = {n.first: first, n.second: second}
        small = self.small()
        extra = 0
        if small is not None:
            come[n.small] = small
            extra = small.shape[0] // 2

        def body(r, copies):
            @pl.when(r.place[2] == 0)
            def keep_first():
                r.kept[:half] = low_sum(r.own.at[:half], r.first)
                r.other[:half] = low_sum(r.own.at[half:], r.second)

            @pl.when(r.place[2] == 1)
            def keep_second():
                r.other[:half] = low_sum(r.own.at[:half], r.first)
                r.kept[:half] = low_sum(r.own.at[half:], r.second)

            if extra:
                for target, pair in ((r.kept, r.place[2]), (r.other, 1 - r.place[2])):
                    rows = pl.ds(pl.multiple_of(pair * extra, extra), extra)
                    target[half:, : r.small.shape[1]] = r.small[rows, :].astype(low)

        shapes = {n.kept: (half + extra, columns), n.other: (half + extra, columns)}
        self.own, other = self.kernel(n.pair, body, shapes, **come)
        self.come = exchange(other, 2)

    def inward(self):
        self.add()
        line = lax.axis_size("dp") // 4
        if line == 4:
            self.come = along_line(self.own, [(0, 1), (3, 2)])
            return
        distance = 4
        while distance < 4 * line:
            self.come = exchange(self.own, distance)
            distance *= 2
            if distance < 4 * line:
                self.add()

    def middle(self):
        self.add()
        if lax.axis_size("dp") == 16:
            self.come = along_line(self.own, [(1, 2), (2, 1)])

    def outward(self):
        if lax.axis_size("dp") == 16:
            self.add()
            self.come = along_line(self.own, [(1, 0), (2, 3)])

    def pair_back(self):
        if lax.axis_size("dp") == 16:

            def body(r, copies):
                r.total[...] = jnp.where(r.place[3] == 1, r.own[...], r.come[...])

            (self.own,) = self.kernel(n.take, body, {n.total: self.own.shape}, come=self.come)
        self.come = exchange(self.own, 2)

    def core_back(self):
        def body(r, copies):
            r.pair_part[...] = r.come[...]

        (self.pair_part,) = self.kernel(n.join, body, {n.pair_part: self.own.shape}, come=self.come)
        self.come = exchange(self.own, 1), exchange(self.pair_part, 1)

    def finish(self, target, shape, kind, first, size, extra, whose):
        rows, columns = self.own.shape
        length = rows - extra
        with_small = extra > 0 and 1 in whose
        arrays = {n.own: self.own, n.pair_part: self.pair_part}
        if 1 in whose:
            arrays.update({n.core_own: self.come[0], n.core_pair: self.come[1]})

        def body(r, copies):
            stores = []
            for core_place in whose:
                parts = ((r.own, r.pair_part) if core_place == 0 else (r.core_own, r.core_pair))
                core = r.place[1] if core_place == 0 else 1 - r.place[1]
                for index, part in enumerate(parts):
                    pair = r.place[2] if index == 0 else 1 - r.place[2]
                    quarter = 2 * core + pair
                    to = r.full.at[2 * core_place + index]
                    to[...] = part[:length].astype(wide)
                    rows_at = pl.ds(
                        pl.multiple_of(quarter * length + (first if kind == 0 else 0), 16), length
                    )
                    where = (0, rows_at) if kind == 0 else (0, rows_at, pl.ds(first, size))
                    stores.append(copies.start(to, r.target.at[where]))
            if with_small:
                width = r.small.shape[1]
                for index, (mine, others) in enumerate(
                    ((r.own, r.core_own), (r.pair_part, r.core_pair))
                ):
                    pair = r.place[2] if index == 0 else 1 - r.place[2]
                    to = pl.ds(pl.multiple_of(pair * extra, extra), extra)
                    total = mine[length:, :].astype(wide) + others[length:, :].astype(wide)
                    r.small[to, :] = total[:, :width]
                for place, output in enumerate(
                    (r.mix_gain, r.mix_bias, r.bias_out, r.final_gain, r.final_bias)
                ):
                    output[...] = r.small[place : place + 1]
                for place, part in enumerate(parts_of(r.bias_in.shape[1], width)):
                    r.bias_in[:, part] = r.small[BIAS_IN + place : BIAS_IN + place + 1]
            for store in stores:
                store.wait()

        inputs = {name: (array, WHOLE) for name, array in arrays.items()}
        if target is not None:
            inputs[n.target] = (target, ANY)
        outputs = {n.target: (jax.ShapeDtypeStruct(shape, wide), ANY)}
        scratch = {n.full: ((4, length, columns), wide)}
        if with_small:
            width, inner = shape[1:]
            one = (jax.ShapeDtypeStruct((1, width), wide), WHOLE)
            outputs.update(
                mix_gain=one,
                mix_bias=one,
                bias_out=one,
                final_gain=one,
                final_bias=one,
                bias_in=(jax.ShapeDtypeStruct((1, inner), wide), WHOLE),
            )
            scratch[n.small] = ((2 * extra, width), wide)
        results = run_kernel(
            n.finish,
            body,
            inputs,
            outputs,
            (n.target,) if target is not None else (),
            scratch,
        )
        return results.pop(n.target), results


CHUNKS = ((0, 6), (0, 6), (1, 6), (1, 6))
STEPS = (
    (1, n.core),
    (0, n.core),
    (1, n.pair),
    (None, n.first_back_inner),
    (2, n.core),
    (0, n.pair),
    (1, n.inward),
    (3, n.core),
    (2, n.pair),
    (0, n.inward),
    (1, n.middle),
    (None, n.first_back_input),
    (3, n.pair),
    (2, n.inward),
    (0, n.middle),
    (1, n.outward),
    (3, n.inward),
    (2, n.middle),
    (0, n.outward),
    (1, n.pair_back),
    (None, n.first_back_spectra),
    (3, n.middle),
    (2, n.outward),
    (1, n.core_back),
    (0, n.pair_back),
    (3, n.outward),
    (2, n.pair_back),
    (1, n.finish),
    (None, n.others_back_spectra),
    (0, n.core_back),
    (3, n.pair_back),
    (2, n.core_back),
    (0, n.finish),
    (2, n.finish),
    (3, n.core_back),
    (3, n.finish_own),
    (3, n.finish),
)


def per_device(
    activations,
    out_cotangent,
    doc_lengths,
    mix_gain,
    mix_bias,
    weight_in,
    bias_in,
    weight_out,
    bias_out,
    final_gain,
    final_bias,
):
    rows, seq_len, width = activations.shape
    inner = weight_in.shape[2]
    order.last, order.shares_vmem = None, False
    tables = make_tables(width, seq_len)
    vectors = {
        n.mix_gain: mix_gain,
        n.mix_bias: mix_bias,
        n.bias_in: bias_in,
        n.bias_out: bias_out,
        n.final_gain: final_gain,
        n.final_bias: final_bias,
    }
    work = Sections(rows, (seq_len, width, inner), tables, (weight_in, weight_out), vectors)
    handed = []
    for row in range(rows):
        if row == 0:
            pieces, spectra = [], None
            for block in range(seq_len // BLOCK):
                piece, made = work.first_part(row, activations, block, spectra)
                spectra = made if block == 0 else spectra
                pieces.append(from_behind(piece, "pipe", 1))
        else:
            result = work.first_forward(row, activations, True, True)
            pieces = [from_behind(result, "pipe", 1)]
        handed.append(pieces)
    returned = []
    for row in range(rows):
        result = work.later_both(row, handed[row], out_cotangent, doc_lengths)
        returned.append(from_behind(result, "pipe", -1))
        if row == 0:
            work.first_forward(row, activations, True, False)
    for row in range(rows):
        work.first_back_branch(row, returned[row])
        if row < rows - 1:
            work.first_back_inner(row)
            work.first_back_input(row)
    order.shares_vmem = True
    sums, first = [], [0, 0]
    for kind, units in CHUNKS:
        size = units * inner // 12
        last = len(sums) == len(CHUNKS) - 1
        make = functools.partial(work.weight_chunk, kind, first[kind], size)
        small_of = functools.partial(getattr, work, n.small) if last else nothing
        sums.append((Sum(make, small_of), kind, first[kind], size, 16 if last else 0))
        first[kind] += size
    shapes, targets = (weight_out.shape, weight_in.shape), [None, None]
    for index, step in STEPS:
        if index is None:
            getattr(work, step)(rows - 1)
        elif step in (n.finish, n.finish_own):
            chunk, kind, *rest = sums[index]
            whose = (0,) if step == n.finish_own else (1,) if (index, n.finish_own) in STEPS else (0, 1)
            targets[kind], small = chunk.finish(targets[kind], shapes[kind], kind, *rest, whose)
        else:
            getattr(sums[index][0], step)()
    return (
        work.kept[n.layer_rows][None],
        work.kept[n.grad_rows][None],
        small[n.mix_gain],
        small[n.mix_bias],
        targets[1],
        small[n.bias_in],
        targets[0],
        small[n.bias_out],
        small[n.final_gain],
        small[n.final_bias],
    )


def solution(mesh):
    placed = (
        P("dp", None, None),
        P("dp", None, None),
        P("dp", None),
        P("pipe", None),
        P("pipe", None),
        P("pipe", None, None),
        P("pipe", None),
        P("pipe", None, None),
        P("pipe", None),
        P("pipe", None),
        P("pipe", None),
    )
    return jax.shard_map(
        per_device,
        mesh=mesh,
        in_specs=placed,
        out_specs=(
            P("pipe", "dp", None, None),
            P("pipe", "dp", None, None),
            P("pipe", None),
            P("pipe", None),
            P("pipe", None, None),
            P("pipe", None),
            P("pipe", None, None),
            P("pipe", None),
            P("pipe", None),
            P("pipe", None),
        ),
        check_vma=False,
    )
```

```python
import functools
import math

import jax
import jax.numpy as jnp
import numpy as np
from jax import lax
from jax.experimental import pallas as pl
from jax.experimental.pallas import tpu as pltpu
from jax.sharding import PartitionSpec as P

eps_norm = 1e-06
low, wide = jnp.bfloat16, jnp.float32
slope = math.sqrt(2.0 / math.pi)
cubic = 0.044715
VMEM_SPARE = 6 * 2**20
SHARE = 800000000
SHARE = 800000000
LONG = 6000000000
VMEM_SHARED = 44 * 2**20
VMEM_ALL = 62 * 2**20
VMEM_LATER = 50 * 2**20
BLOCK = 256
ANY = pl.BlockSpec(memory_space=pltpu.HBM)
SCALARS = pl.BlockSpec(memory_space=pltpu.SMEM)
WHOLE = pl.BlockSpec(memory_space=pltpu.VMEM)

MIX_GAIN, MIX_BIAS, BIAS_OUT, FINAL_GAIN, FINAL_BIAS, BIAS_IN = 0, 1, 2, 3, 4, 16


class Names:
    def __getattr__(self, name):
        return name


n = Names()


def from_behind(block, axis, distance):
    devices = range(lax.axis_size(axis))
    route = [(i - distance, i) for i in devices if i - distance in devices]
    return lax.ppermute(block, axis, route)


def dft_tables(table_len):
    indices = np.arange(table_len)
    angles = (indices[:, None] * indices[None, :] % table_len) * (2.0 * math.pi / table_len)
    scaled = 1.0 / math.sqrt(table_len)
    return (np.cos(angles) * scaled, np.sin(angles) * scaled)


def make_tables(width, seq_len):
    half = width // 2
    hid_cos, hid_sin = dft_tables(width)
    seq_cos, seq_sin = dft_tables(seq_len)
    hidden_mix = np.concatenate([hid_cos[:, : half + 1], hid_sin[:, 1:half]], axis=1)
    seq_mix = np.concatenate([seq_cos, -seq_sin], axis=1)
    return jnp.asarray(hidden_mix, low), jnp.asarray(seq_mix, low)


def matmul(left, right, left_dim=1, right_dim=0):
    return lax.dot_general(
        left, right, (((left_dim,), (right_dim,)), ((), ())), preferred_element_type=wide
    )


def mean_last(values):
    return jnp.mean(values, axis=-1, keepdims=True)


def normalize(values):
    centred = values - mean_last(values)
    inverse = lax.rsqrt(mean_last(centred * centred) + eps_norm)
    return (centred * inverse, inverse)


def norm_back(grad_norm, normed, inverse):
    return inverse * (grad_norm - mean_last(grad_norm) - normed * mean_last(grad_norm * normed))


def gelu_parts(values):
    square = values * values
    part = 0.5 + 0.5 * jnp.tanh(values * (slope + slope * cubic * square))
    active = values * part
    step = 2.0 * slope + 6.0 * slope * cubic * square
    return (active, part + active * (1.0 - part) * step)


def nothing():
    pass


def place_of():
    index = lax.axis_index("dp")
    line = index // 4
    inside = jnp.where((line == 1) | (line == 2), 1, 0)
    return lax.axis_index("pipe"), index % 2, index // 2 % 2, inside


def each_block(seq_len, body):
    def step(index, carry):
        body(pl.ds(pl.multiple_of(index * BLOCK, BLOCK), BLOCK), index)
        return carry

    lax.fori_loop(0, seq_len // BLOCK, step, 0)


def at_block(index, plans, call):
    for place in range(len(plans[0])):
        calls = [getattr(blocks[place], call) for blocks in plans]
        pl.when(index == place)(functools.partial(do_all, calls))


def wait_all(plans):
    do_all(copy.wait for blocks in plans for copy in blocks)


def add_rows(values):
    return jnp.sum(values, axis=0, keepdims=True)


class Copy:
    def __init__(self, source, target, sem):
        self.parts = source, target, sem

    def start(self):
        pltpu.make_async_copy(*self.parts).start()

    def wait(self):
        pltpu.make_async_copy(*self.parts).wait()


class Copies:
    def __init__(self, sems):
        self.sems, self.used = sems, 0

    def plan(self, source, target):
        self.used += 1
        return Copy(source, target, self.sems.at[self.used - 1])

    def blocks(self, source, target):
        parts = [slice(first, first + BLOCK) for first in range(0, target.shape[0], BLOCK)]
        return [self.plan(source.at[part], target.at[part]) for part in parts]

    def start(self, source, target):
        copy = self.plan(source, target)
        copy.start()
        return copy


def do_all(calls):
    for call in calls:
        call()


def add_to(small, place, values):
    small[place : place + 1] += add_rows(values)


def first_lane(values):
    return lax.broadcasted_iota(jnp.int32, values.shape, 1) == 0


def mirror(values):
    groups = values.shape[1] // 128
    parts = [values[:, 128 * g : 128 * (g + 1)] for g in range(groups)]
    lane = lax.broadcasted_iota(jnp.int32, parts[0].shape, 1)
    turned = [jnp.take_along_axis(part, lax.rem(128 - lane, 128), axis=1) for part in parts]
    mirrored = [
        jnp.where(lane == 0, turned[-g % groups], turned[groups - 1 - g]) for g in range(groups)
    ]
    return jnp.concatenate(mirrored, axis=1)


def mixed_rows(r, rows):
    seq_len, width = r.spectra.shape
    half = width // 2
    even = matmul(r.seq_mix[rows, :seq_len], r.spectra[:, : half + 128])
    odd = matmul(r.seq_mix[rows, seq_len:], r.spectra[:, half:])
    middle = even[:, half : half + 1]
    even = even[:, :half]
    odd = jnp.where(first_lane(odd), 0.0, odd)
    later = mirror(even - odd)
    return even + odd, jnp.where(first_lane(later), middle, later)


def forward_block(r, rows, index, in_load, out_load):
    width = r.row.shape[1]
    half = width // 2
    begin, end = mixed_rows(r, rows)
    r.sum[rows, :half] = r.row[rows, :half].astype(wide) + begin
    r.sum[rows, half:] = r.row[rows, half:].astype(wide) + end
    normed, inverse = normalize(r.sum[rows])
    r.normed_one[rows] = normed
    r.inverse_one[rows] = jnp.broadcast_to(inverse, (BLOCK, 128))
    r.hidden_low[rows] = (normed * r.mix_gain[...] + r.mix_bias[...]).astype(low)
    by_part = isinstance(in_load, list)
    if not by_part:
        pl.when(index == 0)(in_load.wait)
    for place, part in enumerate(parts_of(r.weight_in.shape[1], width)):
        if by_part:
            in_load[place].wait()
        inner = matmul(r.hidden_low[rows], r.weight_in[:, part]) + r.bias_in[:, part]
        active, gelu_grad = gelu_parts(inner)
        active = active.astype(low)
        r.active[rows, part] = active
        r.gelu_grad[rows, part] = gelu_grad.astype(low)
        if by_part:
            out_load[place].wait()
        if part.start == 0:
            if not by_part:
                pl.when(index == 0)(out_load.wait)
            r.sum[rows] = matmul(active, r.weight_out[part])
        else:
            r.sum[rows] += matmul(active, r.weight_out[part])
    hidden = r.normed_one[rows] * r.mix_gain[...] + r.mix_bias[...]
    normed, inverse = normalize(hidden + r.sum[rows] + r.bias_out[...])
    r.normed_two[rows] = normed
    r.inverse_two[rows] = jnp.broadcast_to(inverse, (BLOCK, 128))
    r.result[rows] = (normed * r.final_gain[...] + r.final_bias[...]).astype(low)


def branch_back(r, rows, grad_out):
    normed = r.normed_two[rows]
    grad_sum = norm_back(grad_out * r.final_gain[...], normed, r.inverse_two[rows][:, :1])
    r.grad_sum[rows] = grad_sum
    grad_branch = grad_sum.astype(low)
    r.grad_branch[rows] = grad_branch
    add_to(r.small, BIAS_OUT, grad_branch.astype(wide))
    add_to(r.small, FINAL_GAIN, grad_out * normed)
    add_to(r.small, FINAL_BIAS, grad_out)


def inner_back(r, rows, index):
    width = r.grad_branch.shape[1]
    part = slice(index * width, (index + 1) * width)
    grad_active = matmul(r.grad_branch[rows], r.weight_out[part], 1, 1)
    grad_inner = grad_active * r.gelu_grad[rows, part].astype(wide)
    r.grad_inner[rows, part] = grad_inner.astype(low)
    add_to(r.small, BIAS_IN + index, grad_inner)


def input_back(r, rows):
    grad_hidden = r.grad_sum[rows] + matmul(r.grad_inner[rows], r.weight_in[...], 1, 1)
    normed = r.normed_one[rows]
    r.sum[rows] = norm_back(grad_hidden * r.mix_gain[...], normed, r.inverse_one[rows][:, :1])
    add_to(r.small, MIX_GAIN, grad_hidden * normed)
    add_to(r.small, MIX_BIAS, grad_hidden)


def spectra_back(r, put):
    seq_len, width = r.sum.shape
    half = width // 2

    def fold(rows, index):
        begin, end = r.sum[rows, :half], mirror(r.sum[rows, half:])
        lane = first_lane(begin)
        r.grad_seq[rows, :half] = jnp.where(lane, begin, begin + end).astype(low)
        r.grad_seq[rows, half:] = jnp.where(lane, end, begin - end).astype(low)

    each_block(seq_len, fold)

    def transform(rows, index):
        even = matmul(r.seq_mix[rows, :seq_len], r.grad_seq[:, : half + 128])
        odd = matmul(r.seq_mix[rows, seq_len:], r.grad_seq[:, half:])
        odd = jnp.where(first_lane(odd), even[:, half : half + 1], odd)
        r.spectra[rows, :half] = even[:, :half].astype(low)
        r.spectra[rows, half:] = odd.astype(low)
        put(rows, index, r.sum[rows] + matmul(r.spectra[rows], r.hidden_mix[...], 1, 1))

    each_block(seq_len, transform)


class Named:
    def __init__(self, refs):
        self.__dict__.update(refs)


class Order:
    last = None
    shares_vmem = False


order = Order()


def run_kernel(name, body, inputs, outputs, taken, scratch):
    if order.last is not None:
        inputs = {**inputs, n.after: (order.last, ANY)}
    outputs = {**outputs, n.turn: (jax.ShapeDtypeStruct((8, 128), wide), ANY)}
    n_in, n_out = len(inputs), len(outputs)
    names_in, names_out = list(inputs), list(outputs)

    held = sum(math.prod(shape) * np.dtype(dtype).itemsize for shape, dtype in scratch.values())
    for array, spec in (*inputs.values(), *outputs.values()):
        if spec is WHOLE:
            held += math.prod(array.shape) * np.dtype(array.dtype).itemsize

    def kernel(*refs):
        named = dict(zip(names_in, refs[:n_in]))
        for name, ref in zip(names_out, refs[n_in : n_in + n_out]):
            named[name] = ref
        named.update(zip(scratch, refs[n_in + n_out : -1]), place=place_of())
        body(Named(named), Copies(refs[-1]))

    results = pl.pallas_call(
        kernel,
        name=name,
        in_specs=[spec for _, spec in inputs.values()],
        out_shape=[jax.ShapeDtypeStruct(shape.shape, shape.dtype) for shape, _ in outputs.values()],
        out_specs=[spec for _, spec in outputs.values()],
        scratch_shapes=[
            *[pltpu.VMEM(*shape) for shape in scratch.values()],
            pltpu.SemaphoreType.DMA((48,)),
        ],
        input_output_aliases={names_in.index(name): names_out.index(name) for name in taken},
        compiler_params=pltpu.CompilerParams(
            vmem_limit_bytes=max(VMEM_SHARED, VMEM_SPARE + held) if order.shares_vmem else (VMEM_ALL if name == n.first_forward else VMEM_LATER)
        ),
        cost_estimate=pl.CostEstimate(flops=(SHARE if name != n.finish else 1) if order.shares_vmem else (LONG if name == n.later_first else 1), bytes_accessed=1, transcendentals=0),
    )(*[array for array, _ in inputs.values()])
    results = dict(zip(names_out, results))
    order.last = results.pop(n.turn)
    return results


class Sections:
    def __init__(self, rows, sizes, tables, weights, vectors):
        self.rows, self.sizes = rows, sizes
        self.tables = dict(zip((n.mix_hbm, n.seq_hbm), tables))
        self.weights = dict(zip((n.in_hbm, n.out_hbm), weights))
        self.vectors = vectors
        self.kept = {}
        seq_len, width, inner = sizes
        self.shapes = {
            n.row: ((seq_len, width), low),
            n.cot: ((seq_len, width), low),
            n.hidden_mix: ((width, width), low),
            n.seq_mix: ((seq_len, 2 * seq_len), low),
            n.weight_in: ((width, inner), low),
            n.weight_out: ((inner, width), low),
            n.spectra: ((seq_len, width), low),
            n.sum: ((seq_len, width), wide),
            n.normed_one: ((seq_len, width), wide),
            n.inverse_one: ((seq_len, 128), wide),
            n.normed_two: ((seq_len, width), wide),
            n.inverse_two: ((seq_len, 128), wide),
            n.hidden_low: ((seq_len, width), low),
            n.active: ((seq_len, inner), low),
            n.gelu_grad: ((seq_len, inner), low),
            n.result: ((seq_len, width), low),
            n.grad_sum: ((seq_len, width), wide),
            n.grad_branch: ((seq_len, width), low),
            n.grad_inner: ((seq_len, inner), low),
            n.grad_seq: ((seq_len, width), low),
            n.grad_mixed: ((seq_len, width), wide),
            n.grad_low: ((seq_len, width), low),
            n.grad_wide: ((seq_len, width), wide),
        }
        self.small = None
        self.columns, self.stores = {}, {}
        for store, names in (
            (n.store_low, (n.active, n.gelu_grad, n.grad_inner, n.hidden_low, n.grad_branch)),
            (n.store_wide, (n.normed_one, n.normed_two, n.grad_sum, n.grad_mixed, n.inverse_one, n.inverse_two)),
        ):
            first = 0
            for name in names:
                (length, size), dtype = self.shapes[name]
                self.columns[name] = (store, first, size)
                first += size
            self.stores[store] = jax.ShapeDtypeStruct((rows * length, first), dtype)
        for store, dtype in ((n.layer_rows, low), (n.grad_rows, wide)):
            self.columns[store] = (store, None, None)
            self.stores[store] = jax.ShapeDtypeStruct((rows, seq_len, width), dtype)

    def stage(self, title, body, owner, inputs, made, reads, writes, scratch, uses_small=False):
        outputs = {name: (shape, ANY) for name, shape in made.items()}
        taken = []
        for store in dict.fromkeys(self.columns[name][0] for name in (*writes, *reads)):
            if store in self.kept:
                inputs[store] = (self.kept[store], ANY)
            if any(self.columns[name][0] == store for name in writes):
                if store in self.kept:
                    taken.append(store)
                outputs[store] = (self.stores[store], ANY)
        if uses_small:
            if self.small is not None:
                inputs[n.small_before] = (self.small, WHOLE)
            outputs[n.small] = (jax.ShapeDtypeStruct((32, self.sizes[1]), wide), WHOLE)

        def kernel(refs, copies):
            for name in (*reads, *writes):
                store, first, size = self.columns[name]
                ref = getattr(refs, store)
                setattr(refs, name + n._kept, ref if size is None else ref.at[:, first : first + size])
            if uses_small:
                before = getattr(refs, n.small_before, None)
                refs.small[...] = jnp.zeros_like(refs.small) if before is None else before[...]
            pl.when(refs.place[0] == owner)(lambda: body(refs, copies))

        results = run_kernel(
            title, kernel, inputs, outputs, taken, {name: self.shapes[name] for name in scratch}
        )
        if uses_small:
            self.small = results.pop(n.small)
        for name in list(results):
            if name in self.stores:
                self.kept[name] = results.pop(name)
        return results

    def place(self, row):
        return pl.ds(row * self.sizes[0], self.sizes[0])

    def row_shape(self, dtype):
        return jax.ShapeDtypeStruct(self.sizes[:2], dtype)

    def any_inputs(self, arrays):
        return {name: (array, ANY) for name, array in arrays.items()}

    def vector_inputs(self):
        return {name: (array, WHOLE) for name, array in self.vectors.items()}

    def first_forward(self, row, activations, keeps, hands):
        keep = (n.gelu_grad, n.normed_one, n.inverse_one, n.normed_two, n.inverse_two, n.active, n.hidden_low)

        def body(r, copies):
            loads = forward_loads(r, copies, r.x_hbm.at[row])
            stores = []
            if hands:
                stores.append(copies.blocks(r.result, r.handed))
            if keeps:
                stores.append(copies.blocks(r.result, r.layer_rows.at[row]))
                for name in keep:
                    target = getattr(r, name + n._kept).at[self.place(row)]
                    stores.append(copies.blocks(getattr(r, name), target))

            def block(rows, index):
                forward_block(r, rows, index, *loads)
                at_block(index, stores, n.start)

            each_block(r.row.shape[0], block)
            wait_all(stores)

        inputs = {
            **self.any_inputs({n.x_hbm: activations, **self.tables, **self.weights}),
            **self.vector_inputs(),
        }
        return self.stage(
            n.first_forward if hands else n.again_forward,
            body,
            0,
            inputs,
            {n.handed: self.row_shape(low)} if hands else {},
            (),
            (*keep, n.layer_rows) if keeps else (),
            (n.row, n.hidden_mix, n.seq_mix, n.weight_in, n.weight_out, n.spectra, n.sum, n.result, *keep),
        ).get(n.handed)

    def first_part(self, row, activations, block, spectra):
        fresh = spectra is None
        names = (n.row, n.hidden_mix, n.seq_mix, n.weight_in, n.weight_out, n.spectra, n.sum, n.result, n.normed_one,
                 n.inverse_one, n.normed_two, n.inverse_two, n.hidden_low, n.active, n.gelu_grad)

        def body(r, copies):
            stores = []
            if fresh:
                loads = forward_loads(r, copies, r.x_hbm.at[row], by_part=True)
                stores.append(copies.start(r.spectra, r.spectra_out))
            else:
                firsts = [
                    copies.start(r.x_hbm.at[row], r.row),
                    copies.start(r.spectra_in, r.spectra),
                    copies.start(r.seq_hbm, r.seq_mix),
                ]
                loads = weight_parts(r, copies)
                do_all(first.wait for first in firsts)
            rows = slice(block * BLOCK, (block + 1) * BLOCK)
            forward_block(r, rows, 0, *loads)
            stores.append(copies.start(r.result.at[rows], r.handed.at[:BLOCK]))
            do_all(store.wait for store in stores)

        inputs = {
            **self.any_inputs({n.x_hbm: activations, **self.tables, **self.weights}),
            **self.vector_inputs(),
        }
        if not fresh:
            inputs[n.spectra_in] = (spectra, ANY)
        width = self.sizes[1]
        made = {n.handed: jax.ShapeDtypeStruct((BLOCK + (16 if fresh else 0), width), low)}
        if fresh:
            made[n.spectra_out] = jax.ShapeDtypeStruct(self.sizes[:2], low)
        results = self.stage(n.first_forward, body, 0, inputs, made, (), (), names)
        return results[n.handed], results.get(n.spectra_out)

    def later_both(self, row, handed, out_cotangent, lengths):
        pieces = {n.x_hbm + str(place): piece for place, piece in enumerate(handed)}
        keep = (n.active, n.hidden_low, n.grad_branch, n.grad_inner)

        def body(r, copies):
            loads = forward_loads(r, copies, *[getattr(r, name) for name in pieces])
            cot_load = copies.start(r.cot_hbm.at[row], r.cot)
            filled = r.cot.shape[0] - r.lengths[row, r.lengths.shape[1] - 1]
            stores = [copies.blocks(r.result, r.layer_rows.at[row])]
            for name in keep:
                target = getattr(r, name + n._kept).at[self.place(row)]
                stores.append(copies.blocks(getattr(r, name), target))

            def block(rows, index):
                forward_block(r, rows, index, *loads)
                pl.when(index == 0)(cot_load.wait)
                token = rows.start + lax.broadcasted_iota(jnp.int32, (BLOCK, r.cot.shape[1]), 0)
                branch_back(r, rows, jnp.where(token < filled, r.cot[rows].astype(wide), 0.0))
                for part in range(r.weight_out.shape[0] // r.cot.shape[1]):
                    inner_back(r, rows, part)
                input_back(r, rows)
                at_block(index, stores, n.start)

            each_block(r.row.shape[0], block)
            results = [
                copies.blocks(r.grad_low, r.returned),
                copies.blocks(r.grad_wide, r.grad_rows.at[row]),
            ]

            def put(rows, index, values):
                r.grad_low[rows] = values.astype(low)
                r.grad_wide[rows] = r.grad_low[rows].astype(wide)
                at_block(index, results, n.start)

            spectra_back(r, put)
            wait_all(stores)
            wait_all(results)

        inputs = {
            n.lengths: (lengths, SCALARS),
            **self.any_inputs(pieces),
            **self.any_inputs({n.cot_hbm: out_cotangent, **self.tables, **self.weights}),
            **self.vector_inputs(),
        }
        return self.stage(
            n.later_first if row == 0 else n.later_both,
            body,
            1,
            inputs,
            {n.returned: self.row_shape(low)},
            (),
            (*keep, n.layer_rows, n.grad_rows),
            tuple(name for name in self.shapes if name != n.grad_mixed),
            True,
        )[n.returned]

    def first_back_branch(self, row, returned):
        keep = (n.grad_branch, n.grad_sum)
        need = (n.normed_two, n.inverse_two)

        def body(r, copies):
            loads = [copies.blocks(r.cot_hbm, r.cot)]
            for name in need:
                source = getattr(r, name + n._kept).at[self.place(row)]
                loads.append(copies.blocks(source, getattr(r, name)))
            stores = [
                copies.blocks(getattr(r, name), getattr(r, name + n._kept).at[self.place(row)])
                for name in keep
            ]
            for index in range(len(loads[0])):
                do_all(blocks[index].start for blocks in loads)

            def block(rows, index):
                at_block(index, loads, n.wait)
                branch_back(r, rows, r.cot[rows].astype(wide))
                at_block(index, stores, n.start)

            each_block(r.cot.shape[0], block)
            wait_all(stores)

        inputs = {
            **self.any_inputs({n.cot_hbm: returned}),
            n.final_gain: (self.vectors[n.final_gain], WHOLE),
        }
        self.stage(
            n.back_branch, body, 0, inputs, {}, need, keep, (n.cot, *need, *keep), True
        )

    def first_back_inner(self, row):
        need = (n.gelu_grad, n.grad_branch)

        def body(r, copies):
            rows = self.place(row)
            first = copies.start(r.grad_branch_kept.at[rows], r.grad_branch)
            width = r.grad_branch.shape[1]
            loads, stores = [], []
            for part in parts_of(r.grad_inner.shape[1], width):
                loads.append(
                    (
                        copies.start(r.out_hbm.at[0, part], r.weight_out.at[part]),
                        copies.start(r.gelu_grad_kept.at[rows, part], r.gelu_grad.at[:, part]),
                    )
                )
                stores.append(
                    copies.plan(r.grad_inner.at[:, part], r.grad_inner_kept.at[rows, part])
                )
            first.wait()

            def step(index, carry):
                for place, group in enumerate(loads):
                    pl.when(index == place)(functools.partial(do_all, [load.wait for load in group]))
                part = pl.ds(pl.multiple_of(index * width, width), width)
                grad_active = matmul(r.grad_branch[...], r.weight_out[part], 1, 1)
                grad_inner = grad_active * r.gelu_grad[:, part].astype(wide)
                r.grad_inner[:, part] = grad_inner.astype(low)
                r.small[pl.ds(BIAS_IN + index, 1)] += add_rows(grad_inner)
                for place, store in enumerate(stores):
                    pl.when(index == place)(store.start)
                return carry

            lax.fori_loop(0, len(loads), step, 0)
            for store in stores:
                store.wait()

        inputs = self.any_inputs({n.out_hbm: self.weights[n.out_hbm]})
        self.stage(
            n.back_inner, body, 0, inputs, {}, need, (n.grad_inner,), (n.weight_out, n.grad_inner, *need), True
        )

    def first_back_input(self, row):
        need = (n.grad_inner, n.grad_sum, n.normed_one, n.inverse_one)

        def body(r, copies):
            weight_load = copies.start(r.in_hbm.at[0], r.weight_in)
            loads = [
                copies.blocks(getattr(r, name + n._kept).at[self.place(row)], getattr(r, name))
                for name in need
            ]
            stores = [copies.blocks(r.sum, r.grad_mixed_kept.at[self.place(row)])]
            for index in range(len(loads[0])):
                do_all(blocks[index].start for blocks in loads)
            weight_load.wait()

            def block(rows, index):
                at_block(index, loads, n.wait)
                input_back(r, rows)
                at_block(index, stores, n.start)

            each_block(r.sum.shape[0], block)
            wait_all(stores)

        inputs = {
            **self.any_inputs({n.in_hbm: self.weights[n.in_hbm]}),
            n.mix_gain: (self.vectors[n.mix_gain], WHOLE),
        }
        self.stage(
            n.back_input, body, 0, inputs, {}, need, (n.grad_mixed,), (n.weight_in, n.sum, *need), True
        )

    def first_back_spectra(self, row):
        def body(r, copies):
            loads = [
                copies.start(r.grad_mixed_kept.at[self.place(row)], r.sum),
                copies.start(r.seq_hbm, r.seq_mix),
                copies.start(r.mix_hbm, r.hidden_mix),
            ]
            for load in loads:
                load.wait()

            stores = [copies.blocks(r.grad_wide, r.grad_rows.at[row])]

            def put(rows, index, values):
                r.grad_wide[rows] = values
                at_block(index, stores, n.start)

            spectra_back(r, put)
            wait_all(stores)

        self.stage(
            n.back_spectra,
            body,
            0,
            self.any_inputs(self.tables),
            {},
            (n.grad_mixed,),
            (n.grad_rows,),
            (n.hidden_mix, n.seq_mix, n.spectra, n.sum, n.grad_seq, n.grad_wide),
        )

    def weight_chunk(self, kind, first, size):
        seq_len, width, inner = self.sizes
        tokens = self.rows * seq_len
        left, right = ((n.active, n.grad_branch), (n.hidden_low, n.grad_inner))[kind]
        height, columns = ((size, width), (width, size))[kind]
        half, quarter = height // 2, height // 4
        length = (quarter, half)[kind]
        wide_part = (columns, columns // 2)[kind]

        def body(r, copies):
            cores = (1 - r.place[1], r.place[1])
            left_first = self.columns[left][1] + (first if kind == 0 else 0)
            right_first = self.columns[right][1] + (first if kind == 1 else 0)
            rights, lefts = [], []
            for k in range(columns // wide_part):
                part = slice(k * wide_part, (k + 1) * wide_part)
                source = r.store.at[:, pl.ds(right_first + k * wide_part, wide_part)]
                rights.append(copies.plan(source, r.right.at[:, part]))
            for k in range(height // length):
                steps_of_core = half // length
                begin = left_first + cores[k // steps_of_core] * half + (k % steps_of_core) * length
                source = r.store.at[:, pl.ds(pl.multiple_of(begin, 128), length)]
                lefts.append(copies.plan(source, r.left.at[k]))
            targets = (
                r.others_first,
                r.others_second,
                r.own.at[:quarter],
                r.own.at[quarter:],
            )
            if kind == 0:
                loads = ((rights[0], lefts[0]), (lefts[1],), (lefts[2],), (lefts[3],))
                outs = [(copies.plan(r.total.at[k], targets[k]),) for k in range(4)]
            else:
                loads = ((rights[0], lefts[0]), (lefts[1],), (rights[1],), ())
                pairs = [
                    [
                        copies.plan(r.total.at[k, piece * quarter : (piece + 1) * quarter], targets[2 * k + piece])
                        for piece in range(2)
                    ]
                    for k in range(2)
                ]
                outs = ((), (), pairs[0], pairs[1])
            do_all(load.start for group in loads for load in group)

            def step(index, carry):
                for place, group in enumerate(loads):
                    pl.when(index == place)(functools.partial(do_all, [load.wait for load in group]))
                if kind == 0:
                    r.total[index] = matmul(r.left[index], r.right[...], 0, 0).astype(low)
                else:
                    k = index % 2
                    part = pl.ds(pl.multiple_of(index // 2 * wide_part, wide_part), wide_part)
                    r.total[k, :, part] = matmul(r.left[k], r.right[:, part], 0, 0).astype(low)
                for place, group in enumerate(outs):
                    pl.when(index == place)(functools.partial(do_all, [out.start for out in group]))
                return carry

            lax.fori_loop(0, 4, step, 0)
            do_all(out.wait for group in outs for out in group)

        shape = jax.ShapeDtypeStruct((quarter, columns), low)
        results = run_kernel(
            n.product,
            body,
            {n.store: (self.kept[n.store_low], ANY)},
            {
                n.own: (jax.ShapeDtypeStruct((half, columns), low), ANY),
                n.others_first: (shape, ANY),
                n.others_second: (shape, ANY),
            },
            (),
            {
                n.left: ((height // length, tokens, length), low),
                n.right: ((tokens, columns), low),
                n.total: ((height // length, length, columns), low),
            },
        )
        return results[n.own], results[n.others_first], results[n.others_second]

    def others_back_spectra(self, row):
        for earlier in range(row):
            self.first_back_spectra(earlier)


def parts_of(inner, width):
    return [slice(first, first + width) for first in range(0, inner, width)]


def weight_parts(r, copies):
    in_loads, out_loads = [], []
    for part in parts_of(r.weight_in.shape[1], r.weight_in.shape[0]):
        in_loads.append(copies.start(r.in_hbm.at[0, :, part], r.weight_in.at[:, part]))
        out_loads.append(copies.start(r.out_hbm.at[0, part], r.weight_out.at[part]))
    return in_loads, out_loads


def forward_loads(r, copies, *pieces, by_part=False):
    x_loads, first = [], 0
    for piece in pieces:
        length = r.row.shape[0] // len(pieces)
        x_loads.append(copies.start(piece.at[:length], r.row.at[first : first + length]))
        first += length
    mix_load = copies.start(r.mix_hbm, r.hidden_mix)
    do_all(load.wait for load in x_loads)
    mix_load.wait()
    seq_load = copies.start(r.seq_hbm, r.seq_mix)
    if by_part:
        loads = weight_parts(r, copies)
    else:
        loads = (
            copies.start(r.in_hbm.at[0], r.weight_in),
            copies.start(r.out_hbm.at[0], r.weight_out),
        )

    def transform(rows, index):
        r.spectra[rows] = matmul(r.row[rows], r.hidden_mix[...]).astype(low)

    each_block(r.row.shape[0], transform)
    seq_load.wait()
    return loads


def exchange(block, distance):
    devices = range(lax.axis_size("dp"))
    return lax.ppermute(block, "dp", [(i, i ^ distance) for i in devices])


def along_line(block, steps):
    route = [(a * 4 + j, b * 4 + j) for a, b in steps for j in range(4)]
    return lax.ppermute(block, "dp", route)


def low_sum(first, second):
    return (first[...].astype(wide) + second[...].astype(wide)).astype(low)


class Sum:
    def __init__(self, make, small):
        self.make, self.small = make, small

    def kernel(self, title, body, shapes, **come):
        results = run_kernel(
            title,
            body,
            {
                n.own: (self.own, WHOLE),
                **{name: (array, WHOLE) for name, array in come.items()},
            },
            {name: (jax.ShapeDtypeStruct(shape, low), WHOLE) for name, shape in shapes.items()},
            (),
            {},
        )
        return [results[name] for name in shapes]

    def add(self):
        def body(r, copies):
            r.total[...] = low_sum(r.own, r.come)

        (self.own,) = self.kernel(n.add, body, {n.total: self.own.shape}, come=self.come)

    def core(self):
        self.own, first, second = self.make()
        self.come = exchange(first, 1), exchange(second, 1)

    def pair(self):
        rows, columns = self.own.shape
        half = rows // 2
        first, second = self.come
        come = {n.first: first, n.second: second}
        small = self.small()
        extra = 0
        if small is not None:
            come[n.small] = small
            extra = small.shape[0] // 2

        def body(r, copies):
            @pl.when(r.place[2] == 0)
            def keep_first():
                r.kept[:half] = low_sum(r.own.at[:half], r.first)
                r.other[:half] = low_sum(r.own.at[half:], r.second)

            @pl.when(r.place[2] == 1)
            def keep_second():
                r.other[:half] = low_sum(r.own.at[:half], r.first)
                r.kept[:half] = low_sum(r.own.at[half:], r.second)

            if extra:
                for target, pair in ((r.kept, r.place[2]), (r.other, 1 - r.place[2])):
                    rows = pl.ds(pl.multiple_of(pair * extra, extra), extra)
                    target[half:, : r.small.shape[1]] = r.small[rows, :].astype(low)

        shapes = {n.kept: (half + extra, columns), n.other: (half + extra, columns)}
        self.own, other = self.kernel(n.pair, body, shapes, **come)
        self.come = exchange(other, 2)

    def inward(self):
        self.add()
        line = lax.axis_size("dp") // 4
        if line == 4:
            self.come = along_line(self.own, [(0, 1), (3, 2)])
            return
        distance = 4
        while distance < 4 * line:
            self.come = exchange(self.own, distance)
            distance *= 2
            if distance < 4 * line:
                self.add()

    def middle(self):
        self.add()
        if lax.axis_size("dp") == 16:
            self.come = along_line(self.own, [(1, 2), (2, 1)])

    def outward(self):
        if lax.axis_size("dp") == 16:
            self.add()
            self.come = along_line(self.own, [(1, 0), (2, 3)])

    def pair_back(self):
        if lax.axis_size("dp") == 16:

            def body(r, copies):
                r.total[...] = jnp.where(r.place[3] == 1, r.own[...], r.come[...])

            (self.own,) = self.kernel(n.take, body, {n.total: self.own.shape}, come=self.come)
        self.come = exchange(self.own, 2)

    def core_back(self):
        def body(r, copies):
            r.pair_part[...] = r.come[...]

        (self.pair_part,) = self.kernel(n.join, body, {n.pair_part: self.own.shape}, come=self.come)
        self.come = exchange(self.own, 1), exchange(self.pair_part, 1)

    def finish(self, target, shape, kind, first, size, extra, whose):
        rows, columns = self.own.shape
        length = rows - extra
        with_small = extra > 0 and 1 in whose
        arrays = {n.own: self.own, n.pair_part: self.pair_part}
        if 1 in whose:
            arrays.update({n.core_own: self.come[0], n.core_pair: self.come[1]})

        def body(r, copies):
            stores = []
            for core_place in whose:
                parts = ((r.own, r.pair_part) if core_place == 0 else (r.core_own, r.core_pair))
                core = r.place[1] if core_place == 0 else 1 - r.place[1]
                for index, part in enumerate(parts):
                    pair = r.place[2] if index == 0 else 1 - r.place[2]
                    quarter = 2 * core + pair
                    to = r.full.at[2 * core_place + index]
                    to[...] = part[:length].astype(wide)
                    rows_at = pl.ds(
                        pl.multiple_of(quarter * length + (first if kind == 0 else 0), 16), length
                    )
                    where = (0, rows_at) if kind == 0 else (0, rows_at, pl.ds(first, size))
                    stores.append(copies.start(to, r.target.at[where]))
            if with_small:
                width = r.small.shape[1]
                for index, (mine, others) in enumerate(
                    ((r.own, r.core_own), (r.pair_part, r.core_pair))
                ):
                    pair = r.place[2] if index == 0 else 1 - r.place[2]
                    to = pl.ds(pl.multiple_of(pair * extra, extra), extra)
                    total = mine[length:, :].astype(wide) + others[length:, :].astype(wide)
                    r.small[to, :] = total[:, :width]
                for place, output in enumerate(
                    (r.mix_gain, r.mix_bias, r.bias_out, r.final_gain, r.final_bias)
                ):
                    output[...] = r.small[place : place + 1]
                for place, part in enumerate(parts_of(r.bias_in.shape[1], width)):
                    r.bias_in[:, part] = r.small[BIAS_IN + place : BIAS_IN + place + 1]
            for store in stores:
                store.wait()

        inputs = {name: (array, WHOLE) for name, array in arrays.items()}
        if target is not None:
            inputs[n.target] = (target, ANY)
        outputs = {n.target: (jax.ShapeDtypeStruct(shape, wide), ANY)}
        scratch = {n.full: ((4, length, columns), wide)}
        if with_small:
            width, inner = shape[1:]
            one = (jax.ShapeDtypeStruct((1, width), wide), WHOLE)
            outputs.update(
                mix_gain=one,
                mix_bias=one,
                bias_out=one,
                final_gain=one,
                final_bias=one,
                bias_in=(jax.ShapeDtypeStruct((1, inner), wide), WHOLE),
            )
            scratch[n.small] = ((2 * extra, width), wide)
        results = run_kernel(
            n.finish,
            body,
            inputs,
            outputs,
            (n.target,) if target is not None else (),
            scratch,
        )
        return results.pop(n.target), results


CHUNKS = ((0, 6), (0, 6), (1, 6), (1, 6))
STEPS = (
    (1, n.core),
    (0, n.core),
    (1, n.pair),
    (None, n.first_back_inner),
    (2, n.core),
    (0, n.pair),
    (1, n.inward),
    (3, n.core),
    (2, n.pair),
    (0, n.inward),
    (1, n.middle),
    (None, n.first_back_input),
    (3, n.pair),
    (2, n.inward),
    (0, n.middle),
    (1, n.outward),
    (3, n.inward),
    (2, n.middle),
    (0, n.outward),
    (1, n.pair_back),
    (None, n.first_back_spectra),
    (3, n.middle),
    (2, n.outward),
    (1, n.core_back),
    (0, n.pair_back),
    (3, n.outward),
    (2, n.pair_back),
    (1, n.finish),
    (None, n.others_back_spectra),
    (0, n.core_back),
    (3, n.pair_back),
    (2, n.core_back),
    (0, n.finish),
    (2, n.finish),
    (3, n.core_back),
    (3, n.finish_own),
    (3, n.finish),
)


def per_device(
    activations,
    out_cotangent,
    doc_lengths,
    mix_gain,
    mix_bias,
    weight_in,
    bias_in,
    weight_out,
    bias_out,
    final_gain,
    final_bias,
):
    rows, seq_len, width = activations.shape
    inner = weight_in.shape[2]
    order.last, order.shares_vmem = None, False
    tables = make_tables(width, seq_len)
    vectors = {
        n.mix_gain: mix_gain,
        n.mix_bias: mix_bias,
        n.bias_in: bias_in,
        n.bias_out: bias_out,
        n.final_gain: final_gain,
        n.final_bias: final_bias,
    }
    work = Sections(rows, (seq_len, width, inner), tables, (weight_in, weight_out), vectors)
    handed = []
    for row in range(rows):
        if row == 0:
            pieces, spectra = [], None
            for block in range(seq_len // BLOCK):
                piece, made = work.first_part(row, activations, block, spectra)
                spectra = made if block == 0 else spectra
                pieces.append(from_behind(piece, "pipe", 1))
        else:
            result = work.first_forward(row, activations, True, True)
            pieces = [from_behind(result, "pipe", 1)]
        handed.append(pieces)
    returned = []
    for row in range(rows):
        result = work.later_both(row, handed[row], out_cotangent, doc_lengths)
        returned.append(from_behind(result, "pipe", -1))
        if row == 0:
            work.first_forward(row, activations, True, False)
    for row in range(rows):
        work.first_back_branch(row, returned[row])
        if row < rows - 1:
            work.first_back_inner(row)
            work.first_back_input(row)
    order.shares_vmem = True
    sums, first = [], [0, 0]
    for kind, units in CHUNKS:
        size = units * inner // 12
        last = len(sums) == len(CHUNKS) - 1
        make = functools.partial(work.weight_chunk, kind, first[kind], size)
        small_of = functools.partial(getattr, work, n.small) if last else nothing
        sums.append((Sum(make, small_of), kind, first[kind], size, 16 if last else 0))
        first[kind] += size
    shapes, targets = (weight_out.shape, weight_in.shape), [None, None]
    for index, step in STEPS:
        if index is None:
            getattr(work, step)(rows - 1)
        elif step in (n.finish, n.finish_own):
            chunk, kind, *rest = sums[index]
            whose = (0,) if step == n.finish_own else (1,) if (index, n.finish_own) in STEPS else (0, 1)
            targets[kind], small = chunk.finish(targets[kind], shapes[kind], kind, *rest, whose)
        else:
            getattr(sums[index][0], step)()
    return (
        work.kept[n.layer_rows][None],
        work.kept[n.grad_rows][None],
        small[n.mix_gain],
        small[n.mix_bias],
        targets[1],
        small[n.bias_in],
        targets[0],
        small[n.bias_out],
        small[n.final_gain],
        small[n.final_bias],
    )


def solution(mesh):
    placed = (
        P("dp", None, None),
        P("dp", None, None),
        P("dp", None),
        P("pipe", None),
        P("pipe", None),
        P("pipe", None, None),
        P("pipe", None),
        P("pipe", None, None),
        P("pipe", None),
        P("pipe", None),
        P("pipe", None),
    )
    return jax.shard_map(
        per_device,
        mesh=mesh,
        in_specs=placed,
        out_specs=(
            P("pipe", "dp", None, None),
            P("pipe", "dp", None, None),
            P("pipe", None),
            P("pipe", None),
            P("pipe", None, None),
            P("pipe", None),
            P("pipe", None, None),
            P("pipe", None),
            P("pipe", None),
            P("pipe", None),
        ),
        check_vma=False,
    )
```
